128 devices in a mesh: rad: 8 (over x, core), chan: 16 (over z, y).
Axes of the slice: x: 4, y: 4, z: 4, core: 2. Of those that a mesh axis runs over, the one named last changes fastest.
Arguments:
- inner_state: float32 [2, 32768], P(None, ('rad', 'chan')), may hold values from -6 to 6
- outer_state: float32 [2, 49152, 512], P(None, ('rad', 'chan')), may hold values from -6 to 6
- inner_ham: float32 [8, 4096, 4096], P('rad', None, 'chan'), may hold values from -0.09375 to 0.09375
- inner_coupling: float32 [8, 2, 512, 4096], P('rad', None, None, 'chan'), may hold values from -0.125 to 0.125
- surface_amp: float32 [8, 2, 4096, 512], P('rad', None, 'chan'), may hold values from -0.09375 to 0.09375
- potential: float32 [49152, 512], P(('rad', 'chan')), may hold values from 0 to 1
- laser_mix: float32 [512, 512], replicated, may hold values from -0.0625 to 0.0625
- partners: int32 [8, 2], replicated, may hold values from 0 to 7
- band_offsets: int32 [8, 2], replicated, may hold values from -512 to 0
- channel_group: int32 [512], replicated, may hold values from 0 to 7
Outputs:
- last_inner: float32 [2, 32768], P(None, ('rad', 'chan'))
- last_outer: float32 [2, 49152, 512], P(None, ('rad', 'chan'))
- hessenberg: float32 [2, 3, 2], replicated
The draws below stay inside these ranges and needn't reach their ends.
All inputs are finite; a program needn't handle non-finite values.
Results may differ from the reference program's by a relative error of at most 0.00013.
Values sent between devices are 32-bit elements; how exact they have to be, the bound alone decides.
No kernel may reach another device: no remote copies, remote signals or barrier semaphores. Data moves between devices by JAX's collectives and lax.ppermute only.
A program may use at most 64 MiB of HBM per device.

```python
import jax
import jax.numpy as jnp
from jax import lax

ORDER = 4096
CH = 512
WIN = 512
STRIP = 256
NCOUP = 2
TERMS = 2
BLOCKS = 8
NINNER = 32768
NR = 49152


def with_ends(array, key, low, top_value):
    index_at = [jax.random.randint(jax.random.fold_in(key, axis), (), 0, length) for axis, length in enumerate(array.shape)]
    longest = array.shape.index(max(array.shape))
    next_to = index_at[:longest] + [(index_at[longest] + 1) % array.shape[longest]] + index_at[longest + 1:]
    return array.at[tuple(index_at)].set(low).at[tuple(next_to)].set(top_value)


def levels(stream_key, shape, cuts, least, largest):
    level = 1.0
    for position, parts in cuts:
        steps = jax.random.uniform(jax.random.fold_in(jax.random.fold_in(stream_key, 6), position), (parts,), jnp.float32, least / len(cuts), largest / len(cuts))
        level = level * jnp.repeat(jnp.exp(steps), shape[position] // parts).reshape((-1,) + (1,) * (len(shape) - 1 - position))
    return level


def bell_draw(stream_key, shape, width, bound, cuts=(), held_as=jnp.bfloat16):
    factor_of = levels(stream_key, shape, cuts, -0.22, 0.18) if cuts else 1.0
    result = jax.random.normal(stream_key, shape, jnp.float32) * width * factor_of
    return jnp.minimum(jnp.maximum(result, -bound), bound).astype(held_as)


def setup_inputs(seed: int = 0) -> dict:
    key_of = jax.random.split(jax.random.key(seed), 11)
    inner_state = bell_draw(key_of[0], (2, NINNER), 1.0, 6.0, ((1, 128),), jnp.float32)
    outer_state = bell_draw(key_of[1], (2, NR, CH), 1.0, 6.0, ((1, 128),), jnp.float32)
    inner_ham = bell_draw(key_of[2], (BLOCKS, ORDER, ORDER), ORDER ** -0.5, 0.09375, ((0, 8), (2, 16)), jnp.float32)
    inner_coupling = bell_draw(key_of[3], (BLOCKS, NCOUP, WIN, ORDER), (4 * WIN) ** -0.5, 0.125, ((0, 8), (3, 16)), jnp.float32)
    surface_amp = bell_draw(key_of[4], (BLOCKS, 2, ORDER, CH), ORDER ** -0.5, 0.09375, ((0, 8), (2, 16)), jnp.float32)
    potential = jnp.clip(1.0 * jax.random.uniform(key_of[5], (NR, CH), jnp.float32) ** levels(key_of[5], (NR, CH), ((0, 128),), -0.2, 0.2), 0.0, 1.0)
    laser_mix = bell_draw(key_of[6], (CH, CH), (16 * CH) ** -0.5, 0.0625, (), jnp.float32)
    partners = with_ends(jax.random.randint(key_of[7], (BLOCKS, NCOUP), 0, BLOCKS), jax.random.fold_in(key_of[7], 1), 0, BLOCKS - 1).astype(jnp.int32)
    band_offsets = with_ends(jax.random.randint(key_of[8], (BLOCKS, NCOUP), 0 - WIN, 1), jax.random.fold_in(key_of[8], 1), 0 - WIN, 0).astype(jnp.int32)
    channel_group = with_ends(jax.random.randint(key_of[9], (CH,), 0, BLOCKS), jax.random.fold_in(key_of[9], 1), 0, BLOCKS - 1).astype(jnp.int32)
    return dict(inner_state=inner_state, outer_state=outer_state, inner_ham=inner_ham, inner_coupling=inner_coupling, surface_amp=surface_amp, potential=potential, laser_mix=laser_mix, partners=partners, band_offsets=band_offsets, channel_group=channel_group)


highest = lax.Precision.HIGHEST
kinetic_coef = -0.5 * 0.05 / (12.0 * 0.25 * 0.25)
slope_coef = 1.0 / (12.0 * 0.25)
bloch_coef = 2.0

def local_parts(left, right):
    real_part = jnp.sum(left[0] * right[0]) + jnp.sum(left[1] * right[1])
    imag_part = jnp.sum(left[0][0] * right[0][1] - left[0][1] * right[0][0]) + jnp.sum(left[1][0] * right[1][1] - left[1][1] * right[1][0])
    return (real_part, imag_part)

def rotate(vector, real_coef, imag_coef):
    return jnp.stack([real_coef * vector[0] - imag_coef * vector[1], real_coef * vector[1] + imag_coef * vector[0]])

def operate(inner_vec, outer_vec, inner_ham, inner_coupling, surface_amp, potential, laser_mix, partners, band_offsets, channel_group):
    stacked = inner_vec.reshape(2, BLOCKS, ORDER)
    member = (channel_group[None, :] == jnp.arange(BLOCKS, dtype=jnp.int32)[:, None]).astype(jnp.float32)
    masked_amp = surface_amp * member[:, None, None, :]
    result_in = jnp.einsum('pbk,bkr->pbr', stacked, inner_ham, precision=highest)
    padded = jnp.pad(stacked, ((0, 0), (0, 0), (WIN, WIN)))
    strips = ORDER // STRIP
    strip_starts = jnp.arange(strips, dtype=jnp.int32) * STRIP + WIN
    coupled = []
    for block_index in range(BLOCKS):
        total_rows = jnp.zeros((2, ORDER), jnp.float32)
        for couple_index in range(NCOUP):
            source = lax.dynamic_index_in_dim(padded, partners[block_index, couple_index], 1, keepdims=False)
            starts = strip_starts + band_offsets[block_index, couple_index]
            windows = jax.vmap(lambda first_col: lax.dynamic_slice_in_dim(source, first_col, WIN, 1))(starts)
            tiles = inner_coupling[block_index, couple_index].reshape(WIN, strips, STRIP)
            total_rows = total_rows + jnp.einsum('spw,wsr->psr', windows, tiles, precision=highest).reshape(2, ORDER)
        coupled.append(total_rows)
    result_in = result_in + jnp.stack(coupled, axis=1)
    ghost_rows = jnp.einsum('pbk,bmki->pmi', stacked, masked_amp, precision=highest)
    first_row = outer_vec[:, 0, :]
    result_in = result_in + bloch_coef * jnp.einsum('pi,bki->pbk', first_row, masked_amp[:, 0], precision=highest)
    extended = jnp.concatenate([ghost_rows[:, 1:2], ghost_rows[:, 0:1], outer_vec, jnp.zeros((2, 2, CH), jnp.float32)], axis=1)
    points = outer_vec.shape[1]
    far_left = extended[:, 0:points]
    near_left = extended[:, 1:points + 1]
    centre_row = extended[:, 2:points + 2]
    near_right = extended[:, 3:points + 3]
    far_right = extended[:, 4:points + 4]
    laplace = -far_left + 16.0 * near_left - 30.0 * centre_row + 16.0 * near_right - far_right
    slope_rows = slope_coef * (far_left - 8.0 * near_left + 8.0 * near_right - far_right)
    mixed_slope = jnp.einsum('prc,cd->prd', slope_rows, laser_mix, precision=highest)
    result_out = kinetic_coef * laplace + potential * outer_vec + jnp.stack([mixed_slope[1], -mixed_slope[0]])
    return (result_in.reshape(2, BLOCKS * ORDER), result_out)

def reference(inner_state, outer_state, inner_ham, inner_coupling, surface_amp, potential, laser_mix, partners, band_offsets, channel_group):
    entries = float(BLOCKS * ORDER + NR * CH)
    start_sq = local_parts((inner_state, outer_state), (inner_state, outer_state))[0]
    start_norm = jnp.sqrt(start_sq / entries)
    krylov = [(inner_state / start_norm, outer_state / start_norm)]
    hessenberg = jnp.zeros((2, TERMS + 1, TERMS), jnp.float32)
    for term_index in range(TERMS):
        image_in, image_out = operate(krylov[term_index][0], krylov[term_index][1], inner_ham, inner_coupling, surface_amp, potential, laser_mix, partners, band_offsets, channel_group)
        for prior_index in range(term_index + 1):
            real_part, imag_part = local_parts(krylov[prior_index], (image_in, image_out))
            real_coef = real_part / entries
            imag_coef = imag_part / entries
            image_in = image_in - rotate(krylov[prior_index][0], real_coef, imag_coef)
            image_out = image_out - rotate(krylov[prior_index][1], real_coef, imag_coef)
            hessenberg = hessenberg.at[0, prior_index, term_index].set(real_coef)
            hessenberg = hessenberg.at[1, prior_index, term_index].set(imag_coef)
        new_length = jnp.sqrt(local_parts((image_in, image_out), (image_in, image_out))[0] / entries)
        hessenberg = hessenberg.at[0, term_index + 1, term_index].set(new_length)
        krylov.append((image_in / new_length, image_out / new_length))
    return (krylov[-1][0], krylov[-1][1], hessenberg)
```

```python
import jax
import jax.numpy as jnp
from jax import lax
from jax.sharding import PartitionSpec as P

STRIP = 256
TERMS = 2

highest = lax.Precision.HIGHEST
kinetic_coef = -0.5 * 0.05 / (12.0 * 0.25 * 0.25)
slope_coef = 1.0 / (12.0 * 0.25)
bloch_coef = 2.0
shift = 1.5
least_left = 0.02
both = ("rad", "chan")


def spread(block, axis, holder):
    block = jnp.where(lax.axis_index(axis) == holder, block, jnp.zeros_like(block))
    return lax.psum(block, axis)


def local_parts(left, right):
    real_part = jnp.sum(left[0] * right[0]) + jnp.sum(left[1] * right[1])
    imag_part = jnp.sum(left[0][0] * right[0][1] - left[0][1] * right[0][0]) + jnp.sum(
        left[1][0] * right[1][1] - left[1][1] * right[1][0]
    )
    return jnp.stack([real_part, imag_part])


def rotate(vector, real_coef, imag_coef):
    return jnp.stack(
        [
            real_coef * vector[0] - imag_coef * vector[1],
            real_coef * vector[1] + imag_coef * vector[0],
        ]
    )


def neighbours(block, width):
    count = lax.axis_size(both)
    forward = [(i, i + 1) for i in range(count - 1)]
    backward = [(target, source) for source, target in forward]
    low = lax.ppermute(block[:, block.shape[1] - width :], both, forward)
    high = lax.ppermute(block[:, :width], both, backward)
    return low, high


def outer_apply(extended, potential, laser_mix, moved):
    points = extended.shape[1] - 4
    far_left = extended[:, 0:points]
    near_left = extended[:, 1 : points + 1]
    centre_row = extended[:, 2 : points + 2]
    near_right = extended[:, 3 : points + 3]
    far_right = extended[:, 4 : points + 4]
    laplace = -far_left + 16.0 * near_left - 30.0 * centre_row + 16.0 * near_right - far_right
    slope_rows = slope_coef * (far_left - 8.0 * near_left + 8.0 * near_right - far_right)
    mixed_slope = jnp.einsum("prc,cd->prd", slope_rows, laser_mix, precision=highest)
    return (
        kinetic_coef * laplace
        + (potential - moved) * centre_row
        + jnp.stack([mixed_slope[1], -mixed_slope[0]])
    )


def inner_windows(shards, own_partners, own_offsets):
    windows = []
    for couple_index in range(own_partners.shape[0]):
        source = lax.dynamic_index_in_dim(shards, own_partners[couple_index], 0, keepdims=False)
        source = source.transpose(1, 0, 2).reshape(2, -1)
        band_width = source.shape[1] // 2
        windows.append(
            lax.dynamic_slice_in_dim(source, own_offsets[couple_index] + band_width, band_width, 1)
        )
    return windows


def exchange(inner_vec, ghost_part, row):
    rows = inner_vec.shape[1]
    blocks, strips = lax.axis_size("rad"), lax.axis_size("chan")
    chunk = jnp.concatenate(
        [
            inner_vec,
            ghost_part.reshape(-1, rows),
            row.reshape(-1, rows),
            jnp.zeros((2, rows), jnp.float32),
        ],
        axis=0,
    )
    got = lax.all_to_all(jnp.broadcast_to(chunk, (strips,) + chunk.shape), "chan", 0, 0)
    own = got[:, 0:2]
    ghost_sum = jnp.sum(got[:, 2:10], axis=0)
    padded = jnp.pad(own, ((2, 1), (0, 0), (0, 0)))
    near = lax.dynamic_slice_in_dim(padded, lax.axis_index("chan"), 4, 0)
    chunk = jnp.concatenate(
        [near.reshape(8, rows), ghost_sum, got[0, 10:14], jnp.zeros((4, rows), jnp.float32)],
        axis=0,
    )
    got_blocks = lax.all_to_all(jnp.broadcast_to(chunk, (blocks,) + chunk.shape), "rad", 0, 0)
    shards = got_blocks[:, 0:8].reshape(blocks, 4, 2, rows)
    ghost = jnp.sum(got_blocks[:, 8:16], axis=0).reshape(2, 2, -1)
    first_row = got_blocks[0, 16:20].reshape(2, -1)
    return own.transpose(1, 0, 2).reshape(2, -1), shards, ghost, first_row


def arnoldi_coefs(gram):
    ss, spr, spi, sqr, sqi, pp, pqr, pqi, qq = [gram[i] for i in range(9)]
    cr, ci = spr / ss, spi / ss
    left_1 = pp - (spr * cr + spi * ci)
    norm_1 = left_1 / ss
    h10 = jnp.sqrt(norm_1)
    sxr = sqr - (cr * spr - ci * spi)
    sxi = sqi - (cr * spi + ci * spr)
    h01r, h01i = sxr / (ss * h10), sxi / (ss * h10)
    pxr, pxi = pqr - cr * pp, pqi - ci * pp
    yxr = pxr - (cr * sxr + ci * sxi)
    yxi = pxi - (cr * sxi - ci * sxr)
    scale = 1.0 / left_1
    d11r, d11i = yxr * scale, yxi * scale
    xx = (qq - 2.0 * (cr * pqr + ci * pqi) + (cr * cr + ci * ci) * pp) * scale
    left_2 = xx - (h01r * h01r + h01i * h01i) - (d11r * d11r + d11i * d11i)
    h21 = jnp.sqrt(left_2)
    poor = jnp.logical_not((left_1 > least_left * pp) & (left_2 > least_left * xx))
    zero = jnp.zeros_like(ss)
    hessenberg = jnp.stack(
        [
            jnp.stack([jnp.stack([cr + shift, h01r]), jnp.stack([h10, d11r + shift]), jnp.stack([zero, h21])]),
            jnp.stack([jnp.stack([ci, h01i]), jnp.stack([zero, d11i]), jnp.stack([zero, zero])]),
        ]
    )
    a = jnp.sqrt(ss)
    down = 1.0 / (a * h10 * h21)
    coef_q = down
    coef_pr, coef_pi = -(cr + d11r) * down, -(ci + d11i) * down
    coef_sr = (d11r * cr - d11i * ci) * down - h01r / (a * h21)
    coef_si = (d11r * ci + d11i * cr) * down - h01i / (a * h21)
    return hessenberg, (coef_q, coef_pr, coef_pi, coef_sr, coef_si), poor


def combine(coefs, s, p, q):
    coef_q, coef_pr, coef_pi, coef_sr, coef_si = coefs
    return coef_q * q + rotate(p, coef_pr, coef_pi) + rotate(s, coef_sr, coef_si)


def gram_parts(s, p, q):
    def real_of(left, right):
        return jnp.sum(left * right)

    def imag_of(left, right):
        return jnp.sum(left[0] * right[1] - left[1] * right[0])

    return jnp.stack(
        [
            real_of(s, s),
            real_of(s, p),
            imag_of(s, p),
            real_of(s, q),
            imag_of(s, q),
            real_of(p, p),
            real_of(p, q),
            imag_of(p, q),
            real_of(q, q),
        ]
    )


def step_by_step(
    inner_state,
    outer_state,
    inner_ham,
    inner_coupling,
    surface_amp,
    potential,
    laser_mix,
    partners,
    band_offsets,
    channel_group,
):
    block_order = inner_ham.shape[1]
    points, channels = outer_state.shape[1:]
    entries = float(
        lax.axis_size("rad") * block_order + lax.axis_size(both) * points * channels
    )
    block_index = lax.axis_index("rad")
    is_first = lax.axis_index(both) == 0
    member = (channel_group == block_index).astype(jnp.float32)
    masked_amp = surface_amp[0] * member[None, None, :]
    own_partners = lax.dynamic_index_in_dim(partners, block_index, 0, keepdims=False)
    own_offsets = lax.dynamic_index_in_dim(band_offsets, block_index, 0, keepdims=False)

    def total(value):
        return lax.psum(value, both) / entries

    def squares(vector):
        return jnp.sum(vector[0] * vector[0]) + jnp.sum(vector[1] * vector[1])

    start_len = jnp.sqrt(total(squares((inner_state, outer_state))))
    krylov = [(inner_state / start_len, outer_state / start_len)]
    hessenberg = jnp.zeros((2, TERMS + 1, TERMS), jnp.float32)
    for term_index in range(TERMS):
        inner_vec, outer_vec = krylov[term_index]
        ghost_part = jnp.einsum("pk,mki->pmi", inner_vec, masked_amp, precision=highest)
        row = jnp.where(is_first, outer_vec[:, 0], 0.0)
        own_vec, shards, ghost, first_row = exchange(inner_vec, ghost_part, row)
        result_in = jnp.dot(own_vec, inner_ham[0], precision=highest)
        for couple_index, window in enumerate(inner_windows(shards, own_partners, own_offsets)):
            result_in = result_in + jnp.dot(window, inner_coupling[0, couple_index], precision=highest)
        result_in = result_in + bloch_coef * jnp.einsum(
            "pi,ki->pk", first_row, masked_amp[0], precision=highest
        )
        low, high = neighbours(outer_vec, 2)
        low = jnp.where(is_first, ghost[:, ::-1], low)
        extended = jnp.concatenate([low, outer_vec, high], axis=1)
        image = (result_in, outer_apply(extended, potential, laser_mix, 0.0))
        for prior_index in range(term_index + 1):
            prior = krylov[prior_index]
            coefs = total(local_parts(prior, image))
            image = tuple(
                part - rotate(prior_part, coefs[0], coefs[1])
                for part, prior_part in zip(image, prior)
            )
            hessenberg = hessenberg.at[:, prior_index, term_index].set(coefs)
        new_length = jnp.sqrt(total(squares(image)))
        hessenberg = hessenberg.at[0, term_index + 1, term_index].set(new_length)
        krylov.append((image[0] / new_length, image[1] / new_length))
    return (krylov[-1][0], krylov[-1][1], hessenberg)


def body(*inputs):
    (
        inner_state,
        outer_state,
        inner_ham,
        inner_coupling,
        surface_amp,
        potential,
        laser_mix,
        partners,
        band_offsets,
        channel_group,
    ) = inputs
    block_order = inner_ham.shape[1]
    points, channels = outer_state.shape[1:]
    count = lax.axis_size(both)
    entries = float(lax.axis_size("rad") * block_order + count * points * channels)
    block_index = lax.axis_index("rad")
    position = lax.axis_index(both)
    is_first, is_last = position == 0, position == count - 1
    member = (channel_group == block_index).astype(jnp.float32)
    amp = surface_amp[0]
    own_partners = lax.dynamic_index_in_dim(partners, block_index, 0, keepdims=False)
    own_offsets = lax.dynamic_index_in_dim(band_offsets, block_index, 0, keepdims=False)

    def inner_image(own_vec, shards, first_row, inner_vec):
        result = jnp.dot(own_vec, inner_ham[0], precision=highest) - shift * inner_vec
        for couple_index, window in enumerate(inner_windows(shards, own_partners, own_offsets)):
            result = result + jnp.dot(window, inner_coupling[0, couple_index], precision=highest)
        return result + bloch_coef * jnp.einsum(
            "pi,ki->pk", first_row * member, amp[0], precision=highest
        )

    def ghost_of(inner_vec):
        return jnp.einsum("pk,mki->pmi", inner_vec, amp, precision=highest) * member

    carried = jnp.concatenate([outer_state, potential[None]], axis=0)
    low, high = neighbours(carried, 4)
    wide = jnp.concatenate([low, carried, high], axis=1)
    p_wide = outer_apply(wide[:2], wide[2, 2:-2], laser_mix, shift)
    p_low = jnp.where(is_first, 0.0, p_wide[:, :2])
    p_high = jnp.where(is_last, 0.0, p_wide[:, -2:])
    p_outer = p_wide[:, 2:-2]
    q_outer = outer_apply(jnp.concatenate([p_low, p_outer, p_high], axis=1), potential, laser_mix, shift)

    s_inner = inner_state
    own_vec, shards, ghost, first_row = exchange(
        s_inner, ghost_of(s_inner), jnp.where(is_first, outer_state[:, 0], 0.0)
    )
    p_inner = inner_image(own_vec, shards, first_row, s_inner)
    side = jnp.concatenate([ghost[:, ::-1], jnp.zeros((2, 4, channels), jnp.float32)], axis=1)
    p_edge = p_outer[:, 0:6].at[:, 0:2].add(
        jnp.where(is_first, outer_apply(side, jnp.zeros((2, channels)), laser_mix, 0.0), 0.0)
    )
    own_vec, shards, ghost, first_row = exchange(
        p_inner, ghost_of(p_inner), jnp.where(is_first, p_edge[:, 0], 0.0)
    )
    q_inner = inner_image(own_vec, shards, first_row, p_inner)
    p_low = jnp.where(is_first, ghost[:, ::-1], p_low)
    q_edge = outer_apply(jnp.concatenate([p_low, p_edge], axis=1), potential[:4], laser_mix, shift)

    parts = (
        gram_parts(outer_state[:, 4:], p_outer[:, 4:], q_outer[:, 4:])
        + gram_parts(outer_state[:, :4], p_edge[:, :4], q_edge)
        + gram_parts(s_inner, p_inner, q_inner)
    )
    sent = jnp.broadcast_to(jnp.pad(parts, (0, 7)), (count, 16))
    gram = jnp.sum(lax.all_to_all(sent, both, 0, 0), axis=0) / entries
    hessenberg, coefs, poor = arnoldi_coefs(gram)
    last_inner = combine(coefs, s_inner, p_inner, q_inner)
    p_all = jnp.concatenate([p_edge[:, :4], p_outer[:, 4:]], axis=1)
    q_all = jnp.concatenate([q_edge, q_outer[:, 4:]], axis=1)
    last_outer = combine(coefs, outer_state, p_all, q_all)

    def again(state):
        return (jnp.zeros((), jnp.bool_),) + step_by_step(*inputs)

    return lax.while_loop(
        lambda state: state[0], again, (poor, last_inner, last_outer, hessenberg)
    )[1:]


def solution(mesh):
    return jax.shard_map(
        body,
        mesh=mesh,
        in_specs=(
            P(None, ("rad", "chan")),
            P(None, ("rad", "chan"), None),
            P("rad", None, "chan"),
            P("rad", None, None, "chan"),
            P("rad", None, "chan", None),
            P(("rad", "chan"), None),
            P(),
            P(),
            P(),
            P(),
        ),
        out_specs=(P(None, ("rad", "chan")), P(None, ("rad", "chan"), None), P()),
        check_vma=False,
    )
```

```python
import jax
import jax.numpy as jnp
from jax import lax
from jax.experimental import pallas as pl
from jax.experimental.pallas import tpu as pltpu
from jax.sharding import PartitionSpec as P

STRIP = 256
TERMS = 2

highest = lax.Precision.HIGHEST
kinetic_coef = -0.5 * 0.05 / (12.0 * 0.25 * 0.25)
slope_coef = 1.0 / (12.0 * 0.25)
bloch_coef = 2.0
shift = 1.5
least_left = 0.02
both = ("rad", "chan")


def spread(block, axis, holder):
    block = jnp.where(lax.axis_index(axis) == holder, block, jnp.zeros_like(block))
    return lax.psum(block, axis)


def local_parts(left, right):
    real_part = jnp.sum(left[0] * right[0]) + jnp.sum(left[1] * right[1])
    imag_part = jnp.sum(left[0][0] * right[0][1] - left[0][1] * right[0][0]) + jnp.sum(
        left[1][0] * right[1][1] - left[1][1] * right[1][0]
    )
    return jnp.stack([real_part, imag_part])


def rotate(vector, real_coef, imag_coef):
    return jnp.stack(
        [
            real_coef * vector[0] - imag_coef * vector[1],
            real_coef * vector[1] + imag_coef * vector[0],
        ]
    )


def neighbours(block, width):
    count = lax.axis_size(both)
    forward = [(i, i + 1) for i in range(count - 1)]
    backward = [(target, source) for source, target in forward]
    low = lax.ppermute(block[:, block.shape[1] - width :], both, forward)
    high = lax.ppermute(block[:, :width], both, backward)
    return low, high


def outer_apply(extended, potential, laser_mix, moved):
    points = extended.shape[1] - 4
    far_left = extended[:, 0:points]
    near_left = extended[:, 1 : points + 1]
    centre_row = extended[:, 2 : points + 2]
    near_right = extended[:, 3 : points + 3]
    far_right = extended[:, 4 : points + 4]
    laplace = -far_left + 16.0 * near_left - 30.0 * centre_row + 16.0 * near_right - far_right
    slope_rows = slope_coef * (far_left - 8.0 * near_left + 8.0 * near_right - far_right)
    mixed_slope = jnp.einsum("prc,cd->prd", slope_rows, laser_mix, precision=highest)
    return (
        kinetic_coef * laplace
        + (potential - moved) * centre_row
        + jnp.stack([mixed_slope[1], -mixed_slope[0]])
    )


def inner_windows(shards, own_partners, own_offsets):
    windows = []
    for couple_index in range(own_partners.shape[0]):
        source = lax.dynamic_index_in_dim(shards, own_partners[couple_index], 0, keepdims=False)
        source = source.transpose(1, 0, 2).reshape(2, -1)
        band_width = source.shape[1] // 2
        windows.append(
            lax.dynamic_slice_in_dim(source, own_offsets[couple_index] + band_width, band_width, 1)
        )
    return windows


def exchange(inner_vec, ghost_part, row):
    rows = inner_vec.shape[1]
    blocks, strips = lax.axis_size("rad"), lax.axis_size("chan")
    chunk = jnp.concatenate(
        [
            inner_vec,
            ghost_part.reshape(-1, rows),
            row.reshape(-1, rows),
            jnp.zeros((2, rows), jnp.float32),
        ],
        axis=0,
    )
    got = lax.all_to_all(jnp.broadcast_to(chunk, (strips,) + chunk.shape), "chan", 0, 0)
    own = got[:, 0:2]
    ghost_sum = jnp.sum(got[:, 2:10], axis=0)
    padded = jnp.pad(own, ((2, 1), (0, 0), (0, 0)))
    near = lax.dynamic_slice_in_dim(padded, lax.axis_index("chan"), 4, 0)
    chunk = jnp.concatenate(
        [near.reshape(8, rows), ghost_sum, got[0, 10:14], jnp.zeros((4, rows), jnp.float32)],
        axis=0,
    )
    got_blocks = lax.all_to_all(jnp.broadcast_to(chunk, (blocks,) + chunk.shape), "rad", 0, 0)
    shards = got_blocks[:, 0:8].reshape(blocks, 4, 2, rows)
    ghost = jnp.sum(got_blocks[:, 8:16], axis=0).reshape(2, 2, -1)
    first_row = got_blocks[0, 16:20].reshape(2, -1)
    return own.transpose(1, 0, 2).reshape(2, -1), shards, ghost, first_row


def step_by_step(
    inner_state,
    outer_state,
    inner_ham,
    inner_coupling,
    surface_amp,
    potential,
    laser_mix,
    partners,
    band_offsets,
    channel_group,
):
    block_order = inner_ham.shape[1]
    points, channels = outer_state.shape[1:]
    entries = float(
        lax.axis_size("rad") * block_order + lax.axis_size(both) * points * channels
    )
    block_index = lax.axis_index("rad")
    is_first = lax.axis_index(both) == 0
    member = (channel_group == block_index).astype(jnp.float32)
    masked_amp = surface_amp[0] * member[None, None, :]
    own_partners = lax.dynamic_index_in_dim(partners, block_index, 0, keepdims=False)
    own_offsets = lax.dynamic_index_in_dim(band_offsets, block_index, 0, keepdims=False)

    def total(value):
        return lax.psum(value, both) / entries

    def squares(vector):
        return jnp.sum(vector[0] * vector[0]) + jnp.sum(vector[1] * vector[1])

    start_len = jnp.sqrt(total(squares((inner_state, outer_state))))
    krylov = [(inner_state / start_len, outer_state / start_len)]
    hessenberg = jnp.zeros((2, TERMS + 1, TERMS), jnp.float32)
    for term_index in range(TERMS):
        inner_vec, outer_vec = krylov[term_index]
        ghost_part = jnp.einsum("pk,mki->pmi", inner_vec, masked_amp, precision=highest)
        row = jnp.where(is_first, outer_vec[:, 0], 0.0)
        own_vec, shards, ghost, first_row = exchange(inner_vec, ghost_part, row)
        result_in = jnp.dot(own_vec, inner_ham[0], precision=highest)
        for couple_index, window in enumerate(inner_windows(shards, own_partners, own_offsets)):
            result_in = result_in + jnp.dot(window, inner_coupling[0, couple_index], precision=highest)
        result_in = result_in + bloch_coef * jnp.einsum(
            "pi,ki->pk", first_row, masked_amp[0], precision=highest
        )
        low, high = neighbours(outer_vec, 2)
        low = jnp.where(is_first, ghost[:, ::-1], low)
        extended = jnp.concatenate([low, outer_vec, high], axis=1)
        image = (result_in, outer_apply(extended, potential, laser_mix, 0.0))
        for prior_index in range(term_index + 1):
            prior = krylov[prior_index]
            coefs = total(local_parts(prior, image))
            image = tuple(
                part - rotate(prior_part, coefs[0], coefs[1])
                for part, prior_part in zip(image, prior)
            )
            hessenberg = hessenberg.at[:, prior_index, term_index].set(coefs)
        new_length = jnp.sqrt(total(squares(image)))
        hessenberg = hessenberg.at[0, term_index + 1, term_index].set(new_length)
        krylov.append((image[0] / new_length, image[1] / new_length))
    return (krylov[-1][0], krylov[-1][1], hessenberg)


side_rows = 8
piece = 16
vmem_bytes = 24 * 2**20


def whole():
    return pl.BlockSpec(memory_space=pltpu.VMEM)


def scalars():
    return pl.BlockSpec(memory_space=pltpu.SMEM)


def run(kernel, outs, args, in_specs, scratch=()):
    return pl.pallas_call(
        kernel,
        out_shape=[jax.ShapeDtypeStruct(shape, jnp.float32) for shape in outs],
        in_specs=in_specs,
        out_specs=[whole()] * len(outs),
        scratch_shapes=list(scratch),
        compiler_params=pltpu.CompilerParams(vmem_limit_bytes=vmem_bytes),
    )(*args)


def two(x):
    high = x.astype(jnp.bfloat16)
    return high, (x - high.astype(jnp.float32)).astype(jnp.bfloat16)


def both_halves(x):
    high, low = two(x)
    rest = jnp.zeros((16 - 2 * x.shape[0], x.shape[1]), jnp.float32)
    return jnp.concatenate([high.astype(jnp.float32), low.astype(jnp.float32), rest], axis=0).astype(jnp.bfloat16)


def few_rows_dot(x, weights, flipped=False):
    rows = x.shape[0]
    lhs = both_halves(x)
    dims = (((1,), (1 if flipped else 0,)), ((), ()))
    total = sum(
        lax.dot_general(lhs, part, dims, preferred_element_type=jnp.float32) for part in two(weights)
    )
    return total[:rows] + total[rows : 2 * rows]


def write_chunk(out_ref, inner_vec, ghosts, row):
    half = inner_vec.shape[1]
    chunk = jnp.concatenate(
        [
            ghosts[:, :half],
            ghosts[:, half:],
            inner_vec,
            row[:, :half],
            row[:, half:],
            jnp.zeros((2, half), jnp.float32),
        ],
        axis=0,
    )
    for strip in range(out_ref.shape[0]):
        out_ref[strip] = chunk


def ghost_rows(inner_vec, amp_ref, member):
    return jnp.concatenate(
        [few_rows_dot(inner_vec, amp_ref[0, radius]) * member for radius in range(2)], axis=0
    )


def member_of(group_ref, place_ref):
    return jnp.where(group_ref[...] == place_ref[0], 1.0, 0.0)


def start_kernel(place_ref, inner_ref, head_ref, amp_ref, group_ref, out_ref):
    inner_vec = inner_ref[...]
    is_first = place_ref[2] == 1
    row = jnp.where(is_first, head_ref[:, 0, :], 0.0)
    write_chunk(out_ref, inner_vec, ghost_rows(inner_vec, amp_ref, member_of(group_ref, place_ref)), row)


def mix_in(out_ref, high_ref, low_ref, mix_ref, places, chunk):
    mix_high, mix_low = two(mix_ref[...])
    for part in range(2):
        for first in range(0, places, chunk):
            rows = pl.ds(first, chunk)
            high, low = high_ref[1 - part, rows], low_ref[1 - part, rows]
            mixed = (
                jnp.dot(high, mix_low, preferred_element_type=jnp.float32)
                + jnp.dot(low, mix_high, preferred_element_type=jnp.float32)
                + jnp.dot(high, mix_high, preferred_element_type=jnp.float32)
            )
            if part == 0:
                out_ref[part, rows] = out_ref[part, rows] + mixed
            else:
                out_ref[part, rows] = out_ref[part, rows] - mixed


def stencils(load):
    before_2, before_1, here, after_1, after_2 = [load(k) for k in range(-2, 3)]
    kinetic = kinetic_coef * (16.0 * (before_1 + after_1) - (before_2 + after_2) - 30.0 * here)
    slope = slope_coef * ((before_2 - after_2) + 8.0 * (after_1 - before_1))
    return kinetic, slope, here


def first_outer_kernel(
    place_ref, state_ref, low_ref, high_ref, pot_ref, mix_ref, out_ref, wide_ref, slope_h, slope_l
):
    points = state_ref.shape[1]
    places = points + 2 * side_rows
    for part in range(2):
        wide_ref[part, 0:16] = jnp.zeros((16, state_ref.shape[2]), jnp.float32)
        wide_ref[part, 12:16] = low_ref[part]
        wide_ref[part, 16 : 16 + points] = state_ref[part]
        wide_ref[part, 16 + points : 32 + points] = jnp.zeros((16, state_ref.shape[2]), jnp.float32)
        wide_ref[part, 16 + points : 20 + points] = high_ref[part]
    low_pot = jnp.concatenate([jnp.zeros((4, pot_ref.shape[1]), jnp.float32), low_ref[2]], axis=0)
    high_pot = jnp.concatenate([high_ref[2], jnp.zeros((4, pot_ref.shape[1]), jnp.float32)], axis=0)
    for part in range(2):
        for first in range(0, places, piece):
            kinetic, slope, here = stencils(
                lambda k, part=part, first=first: wide_ref[part, 8 + first + k : 8 + first + k + piece]
            )
            if first == 0:
                pot = jnp.concatenate([low_pot, pot_ref[0:8]], axis=0)
            elif first + piece == places:
                pot = jnp.concatenate([pot_ref[points - 8 : points], high_pot], axis=0)
            else:
                pot = pot_ref[first - 8 : first + 8]
            out_ref[part, first : first + piece] = kinetic + (pot - shift) * here
            slope_h[part, first : first + piece], slope_l[part, first : first + piece] = two(slope)
    mix_in(out_ref, slope_h, slope_l, mix_ref, places, places // 5)
    is_first, is_last = place_ref[2] == 1, place_ref[3] == 1
    for part in range(2):
        out_ref[part, 0:side_rows] = jnp.where(is_first, 0.0, out_ref[part, 0:side_rows])
        rows = pl.ds(points + side_rows, side_rows)
        out_ref[part, rows] = jnp.where(is_last, 0.0, out_ref[part, rows])


def products(s, p, q):
    return [
        s[0] * s[0] + s[1] * s[1],
        s[0] * p[0] + s[1] * p[1],
        s[0] * p[1] - s[1] * p[0],
        s[0] * q[0] + s[1] * q[1],
        s[0] * q[1] - s[1] * q[0],
        p[0] * p[0] + p[1] * p[1],
        p[0] * q[0] + p[1] * q[1],
        p[0] * q[1] - p[1] * q[0],
        q[0] * q[0] + q[1] * q[1],
    ]


def folded(x):
    columns = sum(x[:, k : k + 128] for k in range(0, x.shape[1], 128))
    return sum(columns[k : k + 8] for k in range(0, x.shape[0], 8))


def second_outer_kernel(wide_ref, state_ref, pot_ref, mix_ref, out_ref, gram_ref, slope_h, slope_l):
    points = state_ref.shape[1]
    for part in range(2):
        for first in range(0, points, piece):
            kinetic, slope, here = stencils(
                lambda k, part=part, first=first: wide_ref[part, 8 + first + k : 8 + first + k + piece]
            )
            rows = pl.ds(first, piece)
            out_ref[part, rows] = kinetic + (pot_ref[rows] - shift) * here
            slope_h[part, rows], slope_l[part, rows] = two(slope)
    mix_in(out_ref, slope_h, slope_l, mix_ref, points, points // 4)
    gram_ref[...] = jnp.zeros_like(gram_ref)
    for first in range(0, points, 8):
        entries = products(
            [state_ref[part, first : first + 8] for part in range(2)],
            [wide_ref[part, 8 + first : 16 + first] for part in range(2)],
            [out_ref[part, first : first + 8] for part in range(2)],
        )
        for k, entry in enumerate(entries):
            if first == 0:
                entry = jnp.where(lax.broadcasted_iota(jnp.int32, entry.shape, 0) < 4, 0.0, entry)
            gram_ref[k] = gram_ref[k] + folded(entry)


def block_kernel(got_ref, ham_ref, out_ref):
    rows = ham_ref.shape[2]
    total = jnp.zeros((16, rows), jnp.float32)
    for strip in range(got_ref.shape[0]):
        lhs = both_halves(got_ref[strip, 8:10])
        for part in two(ham_ref[0, strip * rows : (strip + 1) * rows]):
            total = total + jnp.dot(lhs, part, preferred_element_type=jnp.float32)
    out_ref[...] = total[0:2] + total[2:4]


def inner_result(block_ref, inner_ref, window_refs, coupling_ref, amp_ref, member, row):
    result = block_ref[...] - shift * inner_ref[...]
    for couple_index, window_ref in enumerate(window_refs):
        result = result + few_rows_dot(window_ref[...], coupling_ref[0, couple_index])
    return result + bloch_coef * few_rows_dot(row * member, amp_ref[0, 0], flipped=True)


def unpacked(sums_ref):
    ghosts = jnp.concatenate([sums_ref[0:4], sums_ref[4:8]], axis=1)
    row = jnp.concatenate([sums_ref[8:10], sums_ref[10:12]], axis=1)
    return ghosts, row


def between_kernel(
    place_ref, block_ref, inner_ref, window_a, window_b, sums_ref, coupling_ref, amp_ref, group_ref, wide_ref, mix_ref,
    image_ref, chunk_ref, head_ref,
):
    member = member_of(group_ref, place_ref)
    ghosts, row = unpacked(sums_ref)
    image = inner_result(block_ref, inner_ref, (window_a, window_b), coupling_ref, amp_ref, member, row)
    image_ref[...] = image
    near, far = ghosts[0:2], ghosts[2:4]
    kinetic = [kinetic_coef * (16.0 * near - far), -kinetic_coef * near]
    slope = jnp.concatenate([slope_coef * (far - 8.0 * near), slope_coef * near], axis=0)
    mixed = few_rows_dot(slope, mix_ref[...])
    is_first = place_ref[2] == 1
    rows = []
    for part in range(2):
        extra = [
            kinetic[k][part : part + 1]
            + (mixed[2 * k + 1 : 2 * k + 2] if part == 0 else -mixed[2 * k : 2 * k + 1])
            for k in range(2)
        ]
        extra = jnp.concatenate(extra + [jnp.zeros((6, near.shape[1]), jnp.float32)], axis=0)
        head = wide_ref[part, 8:16] + jnp.where(is_first, extra, 0.0)
        head_ref[part] = head
        rows.append(head[0:1])
    row = jnp.where(is_first, jnp.concatenate(rows, axis=0), 0.0)
    write_chunk(chunk_ref, image, ghost_rows(image, amp_ref, member), row)


def last_kernel(
    place_ref, block_ref, inner_ref, window_a, window_b, sums_ref, coupling_ref, amp_ref, group_ref, wide_ref, mix_ref,
    head_ref, state_ref, start_ref, second_ref, pot_ref, gram_in_ref,
    image_ref, out_ref, parts_ref, edge_ref,
):
    member = member_of(group_ref, place_ref)
    ghosts, row = unpacked(sums_ref)
    image = inner_result(block_ref, inner_ref, (window_a, window_b), coupling_ref, amp_ref, member, row)
    image_ref[...] = image
    is_first = place_ref[2] == 1
    kinetic, slopes = [], []
    for part in range(2):
        edge_ref[part, 0:8] = wide_ref[part, 0:8]
        ghost = jnp.concatenate([ghosts[2 + part : 3 + part], ghosts[part : part + 1]], axis=0)
        edge_ref[part, 6:8] = jnp.where(is_first, ghost, wide_ref[part, 6:8])
        edge_ref[part, 8:16] = head_ref[part]
        edge_ref[part, 16:24] = wide_ref[part, 16:24]
        inner, slope, here = stencils(lambda k, part=part: edge_ref[part, 8 + k : 16 + k])
        kinetic.append(inner + (pot_ref[0:8] - shift) * here)
        slopes.append(slope)
    mixed = few_rows_dot_wide(jnp.concatenate(slopes, axis=0), mix_ref[...])
    q = [kinetic[0] + mixed[8:16], kinetic[1] - mixed[0:8]]
    top = lax.broadcasted_iota(jnp.int32, q[0].shape, 0) < 4
    for part in range(2):
        q[part] = jnp.where(top, q[part], second_ref[part, 0:8])
        out_ref[part] = q[part]
    edge = products([state_ref[part, 0:8] for part in range(2)], [head_ref[part] for part in range(2)], q)
    start, inner = start_ref[...], inner_ref[...]
    inside = products(
        [start[0:1], start[1:2]], [inner[0:1], inner[1:2]], [image[0:1], image[1:2]]
    )
    lane = lax.broadcasted_iota(jnp.int32, (1, 128), 1)
    sums = jnp.zeros((1, 128), jnp.float32)
    for k in range(9):
        tile = gram_in_ref[k] + folded(jnp.where(top, edge[k], 0.0))
        line = jnp.sum(tile, axis=0, keepdims=True) + inside[k][:, :128] + inside[k][:, 128:]
        sums = jnp.where(lane == k, jnp.sum(line, axis=1, keepdims=True), sums)
    parts_ref[...] = jnp.broadcast_to(sums, parts_ref.shape)


def few_rows_dot_wide(x, weights):
    high, low = two(x)
    weight_high, weight_low = two(weights)
    return (
        jnp.dot(high, weight_low, preferred_element_type=jnp.float32)
        + jnp.dot(low, weight_high, preferred_element_type=jnp.float32)
        + jnp.dot(high, weight_high, preferred_element_type=jnp.float32)
    )


def arnoldi_coefs(gram):
    ss, spr, spi, sqr, sqi, pp, pqr, pqi, qq = gram
    cr, ci = spr / ss, spi / ss
    left_1 = pp - (spr * cr + spi * ci)
    h10 = jnp.sqrt(left_1 / ss)
    sxr = sqr - (cr * spr - ci * spi)
    sxi = sqi - (cr * spi + ci * spr)
    h01r, h01i = sxr / (ss * h10), sxi / (ss * h10)
    pxr, pxi = pqr - cr * pp, pqi - ci * pp
    yxr = pxr - (cr * sxr + ci * sxi)
    yxi = pxi - (cr * sxi - ci * sxr)
    scale = 1.0 / left_1
    h11r, h11i = yxr * scale, yxi * scale
    xx = (qq - 2.0 * (cr * pqr + ci * pqi) + (cr * cr + ci * ci) * pp) * scale
    left_2 = xx - (h01r * h01r + h01i * h01i) - (h11r * h11r + h11i * h11i)
    h21 = jnp.sqrt(left_2)
    fine = (left_1 > least_left * pp) & (left_2 > least_left * xx)
    poor = jnp.where(fine, 0.0, 1.0)
    zero = jnp.zeros_like(ss)
    entries = [cr + shift, h01r, h10, h11r + shift, zero, h21, ci, h01i, zero, h11i, zero, zero]
    a = jnp.sqrt(ss)
    coef_q = 1.0 / (a * h10 * h21)
    coef_p = (-(cr + h11r) * coef_q, -(ci + h11i) * coef_q)
    coef_s = (
        (h11r * cr - h11i * ci) * coef_q - h01r / (a * h21),
        (h11r * ci + h11i * cr) * coef_q - h01i / (a * h21),
    )
    return entries, (coef_q, coef_p, coef_s), poor


def combined(coefs, s, p, q):
    coef_q, coef_p, coef_s = coefs
    return (
        coef_q * q[0] + coef_p[0] * p[0] - coef_p[1] * p[1] + coef_s[0] * s[0] - coef_s[1] * s[1],
        coef_q * q[1] + coef_p[0] * p[1] + coef_p[1] * p[0] + coef_s[0] * s[1] + coef_s[1] * s[0],
    )


def finish_kernel(
    entries, parts_ref, start_ref, inner_ref, image_ref, state_ref, wide_ref, second_ref, head_ref, edge_ref,
    inner_out, outer_out, hess_out, poor_out,
):
    step = pl.program_id(0)
    count = outer_out.shape[1]
    sums = jnp.sum(parts_ref[...], axis=0, keepdims=True) * (1.0 / entries)
    lane = lax.broadcasted_iota(jnp.int32, sums.shape, 1)
    gram = [jnp.sum(jnp.where(lane == k, sums, 0.0), axis=1, keepdims=True) for k in range(9)]
    values, coefs, poor = arnoldi_coefs(gram)
    rows = pl.ds(pl.multiple_of(step * count, 8), count)
    wide_rows = pl.ds(pl.multiple_of(step * count + side_rows, 8), count)
    outer_out[0], outer_out[1] = combined(
        coefs,
        [state_ref[part, rows] for part in range(2)],
        [wide_ref[part, wide_rows] for part in range(2)],
        [second_ref[part, rows] for part in range(2)],
    )

    @pl.when(step == 0)
    def _():
        outer_out[0, 0:8], outer_out[1, 0:8] = combined(
            coefs,
            [state_ref[part, 0:8] for part in range(2)],
            [head_ref[part] for part in range(2)],
            [edge_ref[part] for part in range(2)],
        )
        inner_out[0:1], inner_out[1:2] = combined(
            coefs, *[[ref[0:1], ref[1:2]] for ref in (start_ref, inner_ref, image_ref)]
        )
        line = jnp.zeros((1, 128), jnp.float32)
        for k, value in enumerate(values):
            line = jnp.where(lane == k, value, line)
        hess_out[...] = line
        poor_out[...] = jnp.broadcast_to(poor, poor_out.shape)


def across_blocks(sums, near):
    blocks, strips = lax.axis_size("rad"), lax.axis_size("chan")
    chips = blocks // 2
    core = lax.rem(lax.axis_index("rad"), 2)
    mine = jnp.concatenate([sums, near], axis=0)
    other = lax.ppermute(mine, "rad", [(i, i ^ 1) for i in range(blocks)])
    sums = sums + other[:12]
    first = jnp.where(core == 0, near, other[12:])
    second = jnp.where(core == 0, other[12:], near)
    mine = jnp.concatenate([sums, first, second], axis=0)
    got = [mine] + [
        lax.ppermute(mine, "rad", [(i, (i + 2 * step) % blocks) for i in range(blocks)]) for step in range(1, chips)
    ]
    sums = sum(part[:12] for part in got)
    return sums, jnp.stack([part[12 + 8 * k : 20 + 8 * k] for part in got for k in range(2)])


def body(*inputs):
    (
        inner_state,
        outer_state,
        inner_ham,
        inner_coupling,
        surface_amp,
        potential,
        laser_mix,
        partners,
        band_offsets,
        channel_group,
    ) = inputs
    block_order, rows = inner_ham.shape[1:]
    points, channels = outer_state.shape[1:]
    count = lax.axis_size(both)
    blocks, strips = lax.axis_size("rad"), lax.axis_size("chan")
    entries = float(blocks * block_order + count * points * channels)
    block_index, chan_index = lax.axis_index("rad"), lax.axis_index("chan")
    position = lax.axis_index(both)
    place = jnp.stack(
        [block_index, chan_index, (position == 0).astype(jnp.int32), (position == count - 1).astype(jnp.int32)]
    )
    group = channel_group.reshape(1, channels)
    own_partners = lax.dynamic_index_in_dim(partners, block_index, 0, keepdims=False)
    own_offsets = lax.dynamic_index_in_dim(band_offsets, block_index, 0, keepdims=False)
    slots = lax.rem(block_index // 2 - own_partners // 2 + blocks // 2, blocks // 2) * 2 + lax.rem(own_partners, 2)
    head = outer_state[:, 0:8]
    places = points + 2 * side_rows

    def exchanged(chunk):
        got = lax.all_to_all(chunk, "chan", 0, 0)
        sums = jnp.concatenate([jnp.sum(got[:, 0:8], axis=0), got[0, 10:14]], axis=0)
        padded = jnp.pad(got[:, 8:10], ((2, 1), (0, 0), (0, 0)))
        near = lax.dynamic_slice_in_dim(padded, chan_index, 4, 0).reshape(8, rows)
        sums, shards = across_blocks(sums, near)
        windows = inner_windows(shards.reshape(blocks, 4, 2, rows), slots, own_offsets)
        (block_part,) = run(block_kernel, [(2, rows)], (got, inner_ham), [whole()] * 2)
        return block_part, windows, sums

    (chunk,) = run(
        start_kernel,
        [(strips, 16, rows)],
        (place, inner_state, head, surface_amp, group),
        [scalars()] + [whole()] * 4,
    )
    carried = jnp.concatenate([outer_state, potential[None]], axis=0)
    low, high = neighbours(carried, 4)
    (wide,) = run(
        first_outer_kernel,
        [(2, places, channels)],
        (place, outer_state, low, high, potential, laser_mix),
        [scalars()] + [whole()] * 5,
        [
            pltpu.VMEM((2, points + 32, channels), jnp.float32),
            pltpu.VMEM((2, places, channels), jnp.bfloat16),
            pltpu.VMEM((2, places, channels), jnp.bfloat16),
        ],
    )
    block_part, windows, sums = exchanged(chunk)
    p_inner, chunk, p_head = run(
        between_kernel,
        [(2, rows), (strips, 16, rows), (2, 8, channels)],
        (place, block_part, inner_state, *windows, sums, inner_coupling, surface_amp, group, wide, laser_mix),
        [scalars()] + [whole()] * 10,
    )
    second, gram = run(
        second_outer_kernel,
        [(2, points, channels), (9, 8, 128)],
        (wide, outer_state, potential, laser_mix),
        [whole()] * 4,
        [pltpu.VMEM((2, points, channels), jnp.bfloat16)] * 2,
    )
    block_part, windows, sums = exchanged(chunk)
    q_inner, q_head, parts = run(
        last_kernel,
        [(2, rows), (2, 8, channels), (count, 128)],
        (
            place, block_part, p_inner, *windows, sums, inner_coupling, surface_amp, group, wide, laser_mix,
            p_head, head, inner_state, second, potential, gram,
        ),
        [scalars()] + [whole()] * 16,
        [pltpu.VMEM((2, 24, channels), jnp.float32)],
    )
    parts = lax.all_to_all(parts.reshape(count, 1, 128), both, 0, 0).reshape(count, 128)
    steps = 4
    last_inner, last_outer, line, poor = pl.pallas_call(
        lambda *refs: finish_kernel(entries, *refs),
        grid=(steps,),
        out_shape=[
            jax.ShapeDtypeStruct(shape, jnp.float32)
            for shape in ((2, rows), (2, points, channels), (1, 128), (1, 128))
        ],
        in_specs=[whole()] * 9,
        out_specs=[
            pl.BlockSpec((2, rows), lambda step: (0, 0)),
            pl.BlockSpec((2, points // steps, channels), lambda step: (0, step, 0)),
            pl.BlockSpec((1, 128), lambda step: (0, 0)),
            pl.BlockSpec((1, 128), lambda step: (0, 0)),
        ],
        compiler_params=pltpu.CompilerParams(vmem_limit_bytes=vmem_bytes),
    )(parts, inner_state, p_inner, q_inner, outer_state, wide, second, p_head, q_head)
    hessenberg = line[0, :12].reshape(2, 3, 2)

    def again(state):
        return (jnp.zeros((), jnp.float32),) + step_by_step(*inputs)

    return lax.while_loop(
        lambda state: state[0] > 0.0, again, (poor[0, 0], last_inner, last_outer, hessenberg)
    )[1:]


def solution(mesh):
    return jax.shard_map(
        body,
        mesh=mesh,
        in_specs=(
            P(None, ("rad", "chan")),
            P(None, ("rad", "chan"), None),
            P("rad", None, "chan"),
            P("rad", None, None, "chan"),
            P("rad", None, "chan", None),
            P(("rad", "chan"), None),
            P(),
            P(),
            P(),
            P(),
        ),
        out_specs=(P(None, ("rad", "chan")), P(None, ("rad", "chan"), None), P()),
        check_vma=False,
    )
```

```python
import jax
import jax.numpy as jnp
from jax import lax
from jax.experimental import pallas as pl
from jax.experimental.pallas import tpu as pltpu
from jax.sharding import PartitionSpec as P

STRIP = 256
TERMS = 2

highest = lax.Precision.HIGHEST
kinetic_coef = -0.5 * 0.05 / (12.0 * 0.25 * 0.25)
slope_coef = 1.0 / (12.0 * 0.25)
bloch_coef = 2.0
shift = 1.5
least_left = 0.02
both = ("rad", "chan")


def spread(block, axis, holder):
    block = jnp.where(lax.axis_index(axis) == holder, block, jnp.zeros_like(block))
    return lax.psum(block, axis)


def local_parts(left, right):
    real_part = jnp.sum(left[0] * right[0]) + jnp.sum(left[1] * right[1])
    imag_part = jnp.sum(left[0][0] * right[0][1] - left[0][1] * right[0][0]) + jnp.sum(
        left[1][0] * right[1][1] - left[1][1] * right[1][0]
    )
    return jnp.stack([real_part, imag_part])


def rotate(vector, real_coef, imag_coef):
    return jnp.stack(
        [
            real_coef * vector[0] - imag_coef * vector[1],
            real_coef * vector[1] + imag_coef * vector[0],
        ]
    )


def neighbours(last_rows, first_rows):
    count = lax.axis_size(both)
    forward = [(i, i + 1) for i in range(count - 1)]
    backward = [(target, source) for source, target in forward]
    return lax.ppermute(last_rows, both, forward), lax.ppermute(first_rows, both, backward)


def outer_apply(extended, potential, laser_mix, moved):
    points = extended.shape[1] - 4
    far_left = extended[:, 0:points]
    near_left = extended[:, 1 : points + 1]
    centre_row = extended[:, 2 : points + 2]
    near_right = extended[:, 3 : points + 3]
    far_right = extended[:, 4 : points + 4]
    laplace = -far_left + 16.0 * near_left - 30.0 * centre_row + 16.0 * near_right - far_right
    slope_rows = slope_coef * (far_left - 8.0 * near_left + 8.0 * near_right - far_right)
    mixed_slope = jnp.einsum("prc,cd->prd", slope_rows, laser_mix, precision=highest)
    return (
        kinetic_coef * laplace
        + (potential - moved) * centre_row
        + jnp.stack([mixed_slope[1], -mixed_slope[0]])
    )


def inner_windows(shards, own_partners, own_offsets):
    windows = []
    for couple_index in range(own_partners.shape[0]):
        source = lax.dynamic_index_in_dim(shards, own_partners[couple_index], 0, keepdims=False)
        source = source.transpose(1, 0, 2).reshape(2, -1)
        band_width = source.shape[1] // 2
        windows.append(
            lax.dynamic_slice_in_dim(source, own_offsets[couple_index] + band_width, band_width, 1)
        )
    return windows


def exchange(inner_vec, ghost_part, row):
    rows = inner_vec.shape[1]
    blocks, strips = lax.axis_size("rad"), lax.axis_size("chan")
    chunk = jnp.concatenate(
        [
            inner_vec,
            ghost_part.reshape(-1, rows),
            row.reshape(-1, rows),
            jnp.zeros((2, rows), jnp.float32),
        ],
        axis=0,
    )
    got = lax.all_to_all(jnp.broadcast_to(chunk, (strips,) + chunk.shape), "chan", 0, 0)
    own = got[:, 0:2]
    ghost_sum = jnp.sum(got[:, 2:10], axis=0)
    padded = jnp.pad(own, ((2, 1), (0, 0), (0, 0)))
    near = lax.dynamic_slice_in_dim(padded, lax.axis_index("chan"), 4, 0)
    chunk = jnp.concatenate(
        [near.reshape(8, rows), ghost_sum, got[0, 10:14], jnp.zeros((4, rows), jnp.float32)],
        axis=0,
    )
    got_blocks = lax.all_to_all(jnp.broadcast_to(chunk, (blocks,) + chunk.shape), "rad", 0, 0)
    shards = got_blocks[:, 0:8].reshape(blocks, 4, 2, rows)
    ghost = jnp.sum(got_blocks[:, 8:16], axis=0).reshape(2, 2, -1)
    first_row = got_blocks[0, 16:20].reshape(2, -1)
    return own.transpose(1, 0, 2).reshape(2, -1), shards, ghost, first_row


def step_by_step(
    inner_state,
    outer_state,
    inner_ham,
    inner_coupling,
    surface_amp,
    potential,
    laser_mix,
    partners,
    band_offsets,
    channel_group,
):
    block_order = inner_ham.shape[1]
    points, channels = outer_state.shape[1:]
    entries = float(
        lax.axis_size("rad") * block_order + lax.axis_size(both) * points * channels
    )
    block_index = lax.axis_index("rad")
    is_first = lax.axis_index(both) == 0
    member = (channel_group == block_index).astype(jnp.float32)
    masked_amp = surface_amp[0] * member[None, None, :]
    own_partners = lax.dynamic_index_in_dim(partners, block_index, 0, keepdims=False)
    own_offsets = lax.dynamic_index_in_dim(band_offsets, block_index, 0, keepdims=False)

    def total(value):
        return lax.psum(value, both) / entries

    def squares(vector):
        return jnp.sum(vector[0] * vector[0]) + jnp.sum(vector[1] * vector[1])

    start_len = jnp.sqrt(total(squares((inner_state, outer_state))))
    krylov = [(inner_state / start_len, outer_state / start_len)]
    hessenberg = jnp.zeros((2, TERMS + 1, TERMS), jnp.float32)
    for term_index in range(TERMS):
        inner_vec, outer_vec = krylov[term_index]
        ghost_part = jnp.einsum("pk,mki->pmi", inner_vec, masked_amp, precision=highest)
        row = jnp.where(is_first, outer_vec[:, 0], 0.0)
        own_vec, shards, ghost, first_row = exchange(inner_vec, ghost_part, row)
        result_in = jnp.dot(own_vec, inner_ham[0], precision=highest)
        for couple_index, window in enumerate(inner_windows(shards, own_partners, own_offsets)):
            result_in = result_in + jnp.dot(window, inner_coupling[0, couple_index], precision=highest)
        result_in = result_in + bloch_coef * jnp.einsum(
            "pi,ki->pk", first_row, masked_amp[0], precision=highest
        )
        low, high = neighbours(outer_vec[:, points - 2 :], outer_vec[:, :2])
        low = jnp.where(is_first, ghost[:, ::-1], low)
        extended = jnp.concatenate([low, outer_vec, high], axis=1)
        image = (result_in, outer_apply(extended, potential, laser_mix, 0.0))
        for prior_index in range(term_index + 1):
            prior = krylov[prior_index]
            coefs = total(local_parts(prior, image))
            image = tuple(
                part - rotate(prior_part, coefs[0], coefs[1])
                for part, prior_part in zip(image, prior)
            )
            hessenberg = hessenberg.at[:, prior_index, term_index].set(coefs)
        new_length = jnp.sqrt(total(squares(image)))
        hessenberg = hessenberg.at[0, term_index + 1, term_index].set(new_length)
        krylov.append((image[0] / new_length, image[1] / new_length))
    return (krylov[-1][0], krylov[-1][1], hessenberg)


lanes = 128
margin = 8
reach = 2
vmem_bytes = 16 * 2**20


def whole():
    return pl.BlockSpec(memory_space=pltpu.VMEM)


def anywhere():
    return pl.BlockSpec(memory_space=pl.ANY)


def far():
    return pl.BlockSpec(memory_space=pltpu.HBM)


def in_one(shape):
    return pl.BlockSpec(shape, lambda i: (0,) * len(shape))


def scalars():
    return pl.BlockSpec(memory_space=pltpu.SMEM)


def run(kernel, outs, args, in_specs, scratch=()):
    return pl.pallas_call(
        kernel,
        out_shape=[jax.ShapeDtypeStruct(*out) if isinstance(out[0], tuple) else jax.ShapeDtypeStruct(out, jnp.float32) for out in outs],
        in_specs=in_specs,
        out_specs=[whole()] * len(outs),
        scratch_shapes=list(scratch),
        compiler_params=pltpu.CompilerParams(vmem_limit_bytes=vmem_bytes),
    )(*args)


def two(x):
    high = x.astype(jnp.bfloat16)
    return high, (x - high.astype(jnp.float32)).astype(jnp.bfloat16)


def both_halves(x):
    high, low = two(x)
    rest = jnp.zeros((16 - 2 * x.shape[0], x.shape[1]), jnp.float32)
    return jnp.concatenate([high.astype(jnp.float32), low.astype(jnp.float32), rest], axis=0).astype(jnp.bfloat16)


def few_rows_dot(x, weights, flipped=False):
    rows = x.shape[0]
    lhs = both_halves(x)
    dims = (((1,), (1 if flipped else 0,)), ((), ()))
    total = sum(lax.dot_general(lhs, part, dims, preferred_element_type=jnp.float32) for part in weights)
    return total[:rows] + total[rows : 2 * rows]


def mixed_with(high, low, mix_ref):
    lhs = jnp.concatenate([high, low, high], axis=1)
    return jnp.dot(lhs, mix_ref[...], preferred_element_type=jnp.float32)


def mix_parts(mix_ref):
    high, low = two(slope_coef * mix_ref[...])
    return jnp.concatenate([high, high, low], axis=0)


def write_chunk(out_ref, held_ref, written, inner_vec, ghosts, row):
    half = inner_vec.shape[1]
    held_ref[...] = jnp.concatenate(
        [
            ghosts[:, :half],
            ghosts[:, half:],
            inner_vec,
            row[:, :half],
            row[:, half:],
            jnp.zeros((2, half), jnp.float32),
        ],
        axis=0,
    )
    copies = [
        pltpu.make_async_copy(held_ref, out_ref.at[strip], written.at[strip]) for strip in range(out_ref.shape[0])
    ]
    for copy in copies:
        copy.start()
    for copy in copies:
        copy.wait()


def ghost_rows(inner_vec, amps, member):
    return jnp.concatenate([few_rows_dot(inner_vec, amp) * member for amp in amps], axis=0)


def member_of(group_ref, flags_ref):
    return jnp.where(group_ref[...] == flags_ref[0], 1.0, 0.0)


def start_kernel(
    flags_ref, inner_ref, head_ref, amp_ref, group_ref, chunk_ref, held_ref, written
):
    row = jnp.concatenate([head_ref[part, 0:1] for part in range(2)], axis=0)
    row = jnp.where(flags_ref[2] == 1, row, 0.0)
    inner_vec = inner_ref[...]
    amps = [two(amp_ref[0, radius]) for radius in range(2)]
    ghosts = ghost_rows(inner_vec, amps, member_of(group_ref, flags_ref))
    write_chunk(chunk_ref, held_ref, written, inner_vec, ghosts, row)


def stencils(window, pot):
    before_2, before_1, here, after_1, after_2 = window
    local = (pot - (30.0 * kinetic_coef + shift)) * here + (
        16.0 * kinetic_coef * (before_1 + after_1) - kinetic_coef * (before_2 + after_2)
    )
    return local, (before_2 - after_2) + 8.0 * (after_1 - before_1)


def first_outer_kernel(
    state_ref, pot_ref, mix_ref, out_ref, mix_out, first_out, last_out, wide_ref, pot_wide, slope_h, slope_l, ends_ref, written
):
    points, channels = state_ref.shape[1:]
    strips = channels // lanes
    length = points // 8
    for strip in range(strips):
        here = slice(strip * lanes, (strip + 1) * lanes)
        for part in range(3):
            source = pot_ref if part == 2 else state_ref.at[part]
            target = pot_wide.at[strip] if part == 2 else wide_ref.at[part, strip]
            target[margin : margin + points] = source[:, here]
            target[0:margin] = jnp.zeros((margin, lanes), jnp.float32)
            target[margin + points :] = jnp.zeros((margin, lanes), jnp.float32)
    for part in range(3):
        source = pot_ref if part == 2 else state_ref.at[part]
        ends_ref[0, part], ends_ref[1, part] = source[0:4], source[points - 4 : points]
    copies = [
        pltpu.make_async_copy(ends_ref.at[end], out, written.at[end]) for end, out in enumerate((first_out, last_out))
    ]
    for copy in copies:
        copy.start()

    def strip_step(step, _):
        part, strip = lax.div(step, strips), lax.rem(step, strips)

        def load(place):
            return wide_ref[part, strip, pl.ds(margin + place, 8, stride=length)]

        window = [load(place) for place in range(-2 * reach, 0)]
        columns = pl.ds(pl.multiple_of(strip * lanes, lanes), lanes)
        for first in range(-reach, length + reach, 2):
            slopes = []
            for place in (first, first + 1):
                window.append(load(place + reach))
                local, slope = stencils(window, pot_wide[strip, pl.ds(margin + place, 8, stride=length)])
                out_ref[part, strip, (place + reach) * 8 : (place + reach + 1) * 8] = local
                slopes.append(slope)
                window.pop(0)
            rows = slice((first + reach) * 8, (first + reach + 2) * 8)
            slope_h[part, rows, columns], slope_l[part, rows, columns] = two(jnp.concatenate(slopes, axis=0))
        return 0

    lax.fori_loop(0, 2 * strips, strip_step, 0)
    mix_out[...] = mix_parts(mix_ref)
    add_mixed(out_ref, slope_h, slope_l, mix_out)
    for copy in copies:
        copy.wait()


def add_mixed(out_ref, slope_h, slope_l, mix_ref):
    for part in range(2):
        mixed = mixed_with(slope_h[1 - part], slope_l[1 - part], mix_ref)
        for strip in range(out_ref.shape[1]):
            own = mixed[:, strip * lanes : (strip + 1) * lanes]
            out_ref[part, strip] = out_ref[part, strip] + (own if part == 0 else -own)


def products(s, p, q):
    return [
        s[0] * s[0] + s[1] * s[1],
        s[0] * p[0] + s[1] * p[1],
        s[0] * p[1] - s[1] * p[0],
        s[0] * q[0] + s[1] * q[1],
        s[0] * q[1] - s[1] * q[0],
        p[0] * p[0] + p[1] * p[1],
        p[0] * q[0] + p[1] * q[1],
        p[0] * q[1] - p[1] * q[0],
        q[0] * q[0] + q[1] * q[1],
    ]


def mend_edges(flags_ref, extra_ref, low_ref, high_ref, state_in, pot_in, mix_ref, wide_ref, edge_ref):
    points, channels = pot_in.shape
    strips, places = wide_ref.shape[1:3]
    local, slopes = [], []
    for part in range(2):
        for end in range(2):
            edge = edge_ref.at[part, end]
            edge[...] = jnp.zeros_like(edge)
            edge[4:8] = low_ref[part] if end == 0 else state_in[part, points - 4 : points]
            edge[8:12] = state_in[part, 0:4] if end == 0 else high_ref[part]
            if end == 0:
                pot = jnp.concatenate([low_ref[2], pot_in[0:4]], axis=0)
            else:
                pot = jnp.concatenate([pot_in[points - 4 : points], high_ref[2]], axis=0)
            inner, slope = stencils([edge[4 + k : 12 + k] for k in range(-reach, reach + 1)], pot)
            local.append(inner)
            slopes.append(slope)
    mixed = mixed_with(*two(jnp.concatenate(slopes, axis=0)), mix_ref)
    row = lax.broadcasted_iota(jnp.int32, (8, channels), 0)
    outside = [(row < 4) & (flags_ref[2] == 1), (row >= 4) & (flags_ref[3] == 1)]
    for part in range(2):
        for end in range(2):
            other = mixed[16 * (1 - part) + 8 * end : 16 * (1 - part) + 8 * end + 8]
            p = local[2 * part + end] + (other if part == 0 else -other)
            p = jnp.where(outside[end], 0.0, p)
            if end == 0:
                p = p + extra_ref[part]
            for strip in range(strips):
                first = 0 if end == 0 else places - 8 * 4 + 7
                wide_ref[part, strip, pl.ds(first, 4, stride=8)] = p[2:6, strip * lanes : (strip + 1) * lanes]


def second_outer_kernel(
    flags_ref, extra_ref, low_ref, high_ref, wide_in, state_in, pot_in, mix_ref,
    wide_ref, q_out, notes_out, slope_h, slope_l, state_ref, pot_ref, edge_ref, out_ref, notes_ref, written,
):
    mend_edges(flags_ref, extra_ref, low_ref, high_ref, state_in, pot_in, mix_ref, wide_ref, edge_ref)
    strips, places = out_ref.shape[1:3]
    length = places // 8
    for strip in range(strips):
        here = slice(strip * lanes, (strip + 1) * lanes)
        pot_ref[strip] = pot_in[:, here]
        for part in range(2):
            state_ref[part, strip] = state_in[part, :, here]

    def strip_step(step, _):
        part, strip = lax.div(step, strips), lax.rem(step, strips)

        def load(place):
            return wide_ref[part, strip, (place + reach) * 8 : (place + reach + 1) * 8]

        window = [load(place) for place in range(-reach, reach)]
        columns = pl.ds(pl.multiple_of(strip * lanes, lanes), lanes)
        for first in range(0, length, 2):
            slopes = []
            for place in (first, first + 1):
                window.append(load(place + reach))
                local, slope = stencils(window, pot_ref[strip, pl.ds(place, 8, stride=length)])
                out_ref[part, strip, place * 8 : (place + 1) * 8] = local
                slopes.append(slope)
                window.pop(0)
            rows = slice(first * 8, (first + 2) * 8)
            slope_h[part, rows, columns], slope_l[part, rows, columns] = two(jnp.concatenate(slopes, axis=0))
        return 0

    lax.fori_loop(0, 2 * strips, strip_step, 0)
    add_mixed(out_ref, slope_h, slope_l, mix_ref)
    copy = pltpu.make_async_copy(out_ref, q_out, written.at[0])
    copy.start()
    inside = lax.broadcasted_iota(jnp.int32, (8, lanes), 0) > 0

    def gram_step(strip, sums):
        for place in range(length):
            entries = products(
                [state_ref[part, strip, pl.ds(place, 8, stride=length)] for part in range(2)],
                [wide_ref[part, strip, (place + reach) * 8 : (place + reach + 1) * 8] for part in range(2)],
                [out_ref[part, strip, place * 8 : (place + 1) * 8] for part in range(2)],
            )
            if place < 4:
                entries = [jnp.where(inside, entry, 0.0) for entry in entries]
            sums = [total + entry for total, entry in zip(sums, entries)]
        return sums

    sums = lax.fori_loop(0, strips, gram_step, [jnp.zeros((8, lanes), jnp.float32)] * 9)
    for k in range(9):
        notes_ref[k] = sums[k]
    for strip in range(strips):
        here = slice(strip * lanes, (strip + 1) * lanes)
        notes_ref[9 + strip] = pot_in[0:8, here]
        for part in range(2):
            notes_ref[9 + strips * (part + 1) + strip] = state_in[part, 0:8, here]
    notes_copy = pltpu.make_async_copy(notes_ref, notes_out, written.at[1])
    notes_copy.start()
    copy.wait()
    notes_copy.wait()


def block_kernel(got_ref, ham_ref, out_ref, held_ref, arrived):
    rows = ham_ref.shape[2]
    pieces, size = held_ref.shape[:2]
    copies = [
        pltpu.make_async_copy(ham_ref.at[0, pl.ds(k * size, size)], held_ref.at[k], arrived.at[k]) for k in range(pieces)
    ]
    for copy in copies:
        copy.start()
    total = jnp.zeros((16, rows), jnp.float32)
    for k, copy in enumerate(copies):
        copy.wait()
        for part in range(size // rows):
            lhs = both_halves(got_ref[k * (size // rows) + part, 8:10])
            for weights in two(held_ref[k, part * rows : (part + 1) * rows]):
                total = total + jnp.dot(lhs, weights, preferred_element_type=jnp.float32)
    out_ref[...] = total[0:2] + total[2:4]


def gather_kernel(flags_ref, got_ref, after_ref, out_ref):
    strips = got_ref.shape[0]
    for k in range(4):
        strip = flags_ref[1] + (k - 2)
        there = (strip >= 0) & (strip < strips)
        near = got_ref[jnp.clip(strip, 0, strips - 1), 8:10]
        out_ref[2 * k : 2 * k + 2] = jnp.where(there, near, 0.0)
    out_ref[8:16] = sum(got_ref[strip, 0:8] for strip in range(strips))
    out_ref[16:20] = got_ref[0, 10:14]
    out_ref[20:24] = jnp.zeros((4, got_ref.shape[2]), jnp.float32)


def join_kernel(mine_ref, other_ref, out_ref):
    count = mine_ref.shape[0] - 16
    out_ref[0:count] = mine_ref[0:count]
    out_ref[count : 2 * count] = other_ref[0:count]
    out_ref[2 * count :] = mine_ref[count:] + other_ref[count:]


def join(mine, other):
    return run(join_kernel, [(2 * mine.shape[0] - 16, mine.shape[1])], (mine, other), [whole()] * 2)[0]


def inner_result(flags_ref, partners_ref, offsets_ref, block_ref, inner_ref, mine_ref, other_ref, coupling_ref, amp_ref, member, row):
    result = block_ref[...] - shift * inner_ref[...]
    couplings, band_width = coupling_ref.shape[1:3]
    block_index = flags_ref[0]
    for couple_index in range(couplings):
        apart = partners_ref[block_index, couple_index] ^ block_index
        far_pair = lax.shift_right_logical(apart, 2)
        slot = apart ^ (2 * far_pair)
        rows = pl.ds(pl.multiple_of(lax.rem(slot, 4) * 8, 8), 8)
        near = jnp.where(slot < 4, mine_ref[rows], other_ref[rows])
        near = jnp.concatenate([near[2 * k : 2 * k + 2] for k in range(4)], axis=1)
        near = jnp.concatenate([near, jnp.zeros((6, near.shape[1]), jnp.float32)], axis=0)
        first = offsets_ref[block_index, couple_index] + band_width
        window = pltpu.roll(near, near.shape[1] - first, 1)[0:2, :band_width]
        result = result + few_rows_dot(window, two(coupling_ref[0, couple_index]))
    return result + bloch_coef * few_rows_dot(row * member, two(amp_ref[0, 0]), flipped=True)


def unpacked(mine_ref, other_ref):
    sums = mine_ref[32:48] + other_ref[32:48]
    ghosts = jnp.concatenate([sums[0:4], sums[4:8]], axis=1)
    row = jnp.concatenate([sums[8:10], sums[10:12]], axis=1)
    return ghosts, row


def points_of(ref, part, first, count):
    return jnp.concatenate(
        [ref[part, strip, pl.ds(first * 8, count, stride=8)] for strip in range(ref.shape[1])], axis=1
    )


def between_kernel(
    flags_ref, partners_ref, offsets_ref, block_ref, inner_ref, mine_ref, other_ref, coupling_ref, amp_ref, group_ref, wide_ref, mix_ref,
    low_ref, high_ref, image_ref, chunk_ref, extra_out, held_ref, written, extra_ref, extra_written,
):
    member = member_of(group_ref, flags_ref)
    ghosts, row = unpacked(mine_ref, other_ref)
    image = inner_result(
        flags_ref, partners_ref, offsets_ref, block_ref, inner_ref, mine_ref, other_ref, coupling_ref, amp_ref, member, row
    )
    image_ref[...] = image
    near, far = ghosts[0:2], ghosts[2:4]
    kinetic = [kinetic_coef * (16.0 * near - far), -kinetic_coef * near]
    slope = jnp.concatenate([far - 8.0 * near, near, jnp.zeros((12, near.shape[1]), jnp.float32)], axis=0)
    mixed = mixed_with(*two(slope), mix_ref)
    is_first = flags_ref[2] == 1
    rows = []
    for part in range(2):
        extra = [
            kinetic[k][part : part + 1]
            + (mixed[2 * k + 1 : 2 * k + 2] if part == 0 else -mixed[2 * k : 2 * k + 1])
            for k in range(2)
        ]
        extra = jnp.concatenate(extra + [jnp.zeros((6, near.shape[1]), jnp.float32)], axis=0)
        extra = jnp.where(is_first, extra, 0.0)
        extra_ref[part] = jnp.concatenate([jnp.zeros((4, near.shape[1]), jnp.float32), extra[0:4]], axis=0)
        rows.append(points_of(wide_ref, part, reach, 8)[0:1] + extra[0:1])
    row = jnp.where(is_first, jnp.concatenate(rows, axis=0), 0.0)
    copy = pltpu.make_async_copy(extra_ref, extra_out, extra_written)
    copy.start()
    amps = [two(amp_ref[0, radius]) for radius in range(2)]
    write_chunk(chunk_ref, held_ref, written, image, ghost_rows(image, amps, member), row)
    copy.wait()


def last_kernel(
    flags_ref, partners_ref, offsets_ref, block_ref, inner_ref, mine_ref, other_ref, coupling_ref, amp_ref, group_ref, wide_ref, mix_ref,
    start_ref, second_ref, notes_ref,
    image_ref, out_ref, parts_ref, edge_ref,
):
    member = member_of(group_ref, flags_ref)
    ghosts, row = unpacked(mine_ref, other_ref)
    image = inner_result(
        flags_ref, partners_ref, offsets_ref, block_ref, inner_ref, mine_ref, other_ref, coupling_ref, amp_ref, member, row
    )
    image_ref[...] = image
    is_first = flags_ref[2] == 1
    strips = wide_ref.shape[1]
    noted = [
        jnp.concatenate([notes_ref[9 + strips * k + strip] for strip in range(strips)], axis=1) for k in range(3)
    ]
    local, slopes = [], []
    for part in range(2):
        ghost = jnp.concatenate([ghosts[2 + part : 3 + part], ghosts[part : part + 1]], axis=0)
        edge_ref[part, 0:8] = points_of(wide_ref, part, 0, 8)
        edge_ref[part, 6:8] = jnp.where(is_first, ghost, edge_ref[part, 0:2])
        edge_ref[part, 8:24] = points_of(wide_ref, part, reach, 16)
        inner, slope = stencils([edge_ref[part, 8 + k : 16 + k] for k in range(-reach, reach + 1)], noted[0])
        local.append(inner)
        slopes.append(slope)
    mixed = mixed_with(*two(jnp.concatenate(slopes, axis=0)), mix_parts(mix_ref))
    q = [local[0] + mixed[8:16], local[1] - mixed[0:8]]
    top = lax.broadcasted_iota(jnp.int32, q[0].shape, 0) < 4
    for part in range(2):
        q[part] = jnp.where(top, q[part], points_of(second_ref, part, 0, 8))
        out_ref[part] = q[part]
    edge = products(noted[1:], [edge_ref[part, 8:16] for part in range(2)], q)
    start, inner = start_ref[...], inner_ref[...]
    inside = products([start[0:1], start[1:2]], [inner[0:1], inner[1:2]], [image[0:1], image[1:2]])
    lane = lax.broadcasted_iota(jnp.int32, (1, lanes), 1)
    sums = jnp.zeros((1, lanes), jnp.float32)
    for k in range(9):
        tile = jnp.where(top, edge[k], 0.0)
        tile = notes_ref[k] + sum(tile[:, strip * lanes : (strip + 1) * lanes] for strip in range(strips))
        line = jnp.sum(tile, axis=0, keepdims=True) + inside[k][:, :lanes] + inside[k][:, lanes:]
        sums = jnp.where(lane == k, jnp.sum(line, axis=1, keepdims=True), sums)
    parts_ref[...] = jnp.broadcast_to(sums, parts_ref.shape)


def arnoldi_coefs(gram):
    ss, spr, spi, sqr, sqi, pp, pqr, pqi, qq = gram
    cr, ci = spr / ss, spi / ss
    left_1 = pp - (spr * cr + spi * ci)
    h10 = jnp.sqrt(left_1 / ss)
    sxr = sqr - (cr * spr - ci * spi)
    sxi = sqi - (cr * spi + ci * spr)
    h01r, h01i = sxr / (ss * h10), sxi / (ss * h10)
    pxr, pxi = pqr - cr * pp, pqi - ci * pp
    yxr = pxr - (cr * sxr + ci * sxi)
    yxi = pxi - (cr * sxi - ci * sxr)
    scale = 1.0 / left_1
    h11r, h11i = yxr * scale, yxi * scale
    xx = (qq - 2.0 * (cr * pqr + ci * pqi) + (cr * cr + ci * ci) * pp) * scale
    left_2 = xx - (h01r * h01r + h01i * h01i) - (h11r * h11r + h11i * h11i)
    h21 = jnp.sqrt(left_2)
    fine = (left_1 > least_left * pp) & (left_2 > least_left * xx)
    poor = jnp.where(fine, 0.0, 1.0)
    zero = jnp.zeros_like(ss)
    entries = [[[cr + shift, h10, zero], [h01r, h11r + shift, h21]], [[ci, zero, zero], [h01i, h11i, zero]]]
    a = jnp.sqrt(ss)
    coef_q = 1.0 / (a * h10 * h21)
    coef_p = (-(cr + h11r) * coef_q, -(ci + h11i) * coef_q)
    coef_s = (
        (h11r * cr - h11i * ci) * coef_q - h01r / (a * h21),
        (h11r * ci + h11i * cr) * coef_q - h01i / (a * h21),
    )
    return entries, (coef_q, coef_p, coef_s), poor


def combined(coefs, s, p, q):
    coef_q, coef_p, coef_s = coefs
    return (
        coef_q * q[0] + coef_p[0] * p[0] - coef_p[1] * p[1] + coef_s[0] * s[0] - coef_s[1] * s[1],
        coef_q * q[1] + coef_p[0] * p[1] + coef_p[1] * p[0] + coef_s[0] * s[1] + coef_s[1] * s[0],
    )


def finish_kernel(
    entries, parts_ref, start_ref, inner_ref, image_ref, state_ref, wide_ref, second_ref, edge_ref,
    inner_out, outer_out, hess_out, poor_out, coef_ref,
):
    step = pl.program_id(0)
    count = outer_out.shape[1]
    strips, places = second_ref.shape[1:3]
    length = places // 8

    @pl.when(step == 0)
    def _():
        sums = jnp.sum(parts_ref[...], axis=0, keepdims=True) * (1.0 / entries)
        lane = lax.broadcasted_iota(jnp.int32, sums.shape, 1)
        gram = [jnp.sum(jnp.where(lane == k, sums, 0.0), axis=1, keepdims=True) for k in range(9)]
        values, (coef_q, coef_p, coef_s), poor = arnoldi_coefs(gram)
        for k, coef in enumerate([coef_q, *coef_p, *coef_s]):
            coef_ref[k] = jnp.broadcast_to(coef, (8, lanes))
        lane = lax.broadcasted_iota(jnp.int32, (1, TERMS + 1), 1)
        for part in range(2):
            for column in range(TERMS):
                line = jnp.zeros((1, TERMS + 1), jnp.float32)
                for k, value in enumerate(values[part][column]):
                    line = jnp.where(lane == k, value, line)
                hess_out[part, column : column + 1] = line
        poor_out[...] = jnp.broadcast_to(poor, poor_out.shape)

    coefs = coef_ref[0], (coef_ref[1], coef_ref[2]), (coef_ref[3], coef_ref[4])
    few = count // length
    for run_index in range(few):
        own = step * few + run_index
        for first in range(0, length, 8):
            rows = pl.ds(pl.multiple_of(own * length + first, 8), 8)
            for strip in range(strips):
                result = combined(
                    coefs,
                    [state_ref[part, rows, strip * lanes : (strip + 1) * lanes] for part in range(2)],
                    [wide_ref[part, strip, pl.ds((first + reach) * 8 + own, 8, stride=8)] for part in range(2)],
                    [second_ref[part, strip, pl.ds(first * 8 + own, 8, stride=8)] for part in range(2)],
                )
                for part in range(2):
                    outer_out[
                        part,
                        run_index * length + first : run_index * length + first + 8,
                        strip * lanes : (strip + 1) * lanes,
                    ] = result[part]

    @pl.when(step == 0)
    def _():
        for strip in range(strips):
            here = slice(strip * lanes, (strip + 1) * lanes)
            result = combined(
                coefs,
                [state_ref[part, 0:8, here] for part in range(2)],
                [wide_ref[part, strip, pl.ds(reach * 8, 8, stride=8)] for part in range(2)],
                [edge_ref[part, :, here] for part in range(2)],
            )
            for part in range(2):
                outer_out[part, 0:8, here] = result[part]
        rows = inner_out.shape[1]
        for first in range(0, rows, lanes):
            here = slice(first, first + lanes)
            result = combined(
                [coefs[0][0:1], [c[0:1] for c in coefs[1]], [c[0:1] for c in coefs[2]]],
                *[[ref[0:1, here], ref[1:2, here]] for ref in (start_ref, inner_ref, image_ref)],
            )
            for part in range(2):
                inner_out[part : part + 1, here] = result[part]


def same_kernel(in_ref, out_ref):
    out_ref[...] = in_ref[...]


def across_blocks(mine):
    blocks = lax.axis_size("rad")
    last = blocks // 2 - 1
    mine = join(mine, lax.ppermute(mine, "rad", [(i, i ^ 1) for i in range(blocks)]))
    mine = join(mine, lax.ppermute(mine, "rad", [(i, i ^ 2) for i in range(blocks)]))
    return mine, lax.ppermute(mine, "rad", [(i, 2 * (last - i // 2) + i % 2) for i in range(blocks)])


def body(*inputs):
    (
        inner_state,
        outer_state,
        inner_ham,
        inner_coupling,
        surface_amp,
        potential,
        laser_mix,
        partners,
        band_offsets,
        channel_group,
    ) = inputs
    block_order, rows = inner_ham.shape[1:]
    points, channels = outer_state.shape[1:]
    count = lax.axis_size(both)
    blocks, strips = lax.axis_size("rad"), lax.axis_size("chan")
    entries = float(blocks * block_order + count * points * channels)
    block_index, chan_index = lax.axis_index("rad"), lax.axis_index("chan")
    position = lax.axis_index(both)
    flags = jnp.stack(
        [block_index, chan_index, (position == 0).astype(jnp.int32), (position == count - 1).astype(jnp.int32)]
    )
    group = channel_group.reshape(1, channels)
    f32, bf16 = jnp.float32, jnp.bfloat16
    out_strips = channels // lanes
    folded_rows = points + 2 * reach * 8

    chunk_scratch = [pltpu.VMEM((16, rows), f32), pltpu.SemaphoreType.DMA((strips,))]
    chunk = pl.pallas_call(
        start_kernel,
        grid=(1,),
        out_shape=pltpu.HBM((strips, 16, rows), f32),
        in_specs=[scalars(), whole(), in_one((2, 8, channels)), whole(), whole()],
        out_specs=far(),
        scratch_shapes=chunk_scratch,
        compiler_params=pltpu.CompilerParams(vmem_limit_bytes=vmem_bytes),
    )(flags, inner_state, outer_state, surface_amp, group)
    got = lax.all_to_all(chunk, "chan", 0, 0)
    wide, mix, first_rows, last_rows = pl.pallas_call(
        first_outer_kernel,
        out_shape=[
            jax.ShapeDtypeStruct((2, out_strips, folded_rows, lanes), f32),
            jax.ShapeDtypeStruct((3 * channels, channels), bf16),
            pltpu.HBM((3, 4, channels), f32),
            pltpu.HBM((3, 4, channels), f32),
        ],
        in_specs=[whole()] * 3,
        out_specs=[whole(), whole(), far(), far()],
        scratch_shapes=[
            pltpu.VMEM((2, out_strips, points + 2 * margin, lanes), f32),
            pltpu.VMEM((out_strips, points + 2 * margin, lanes), f32),
            pltpu.VMEM((2, folded_rows, channels), bf16),
            pltpu.VMEM((2, folded_rows, channels), bf16),
            pltpu.VMEM((2, 3, 4, channels), f32),
            pltpu.SemaphoreType.DMA((2,)),
        ],
        compiler_params=pltpu.CompilerParams(vmem_limit_bytes=vmem_bytes),
    )(outer_state, potential, laser_mix)

    def block_product(got):
        pieces = 8
        return run(
            block_kernel,
            [(2, rows)],
            (got, inner_ham),
            [whole(), anywhere()],
            [pltpu.VMEM((pieces, block_order // pieces, rows), f32), pltpu.SemaphoreType.DMA((pieces,))],
        )[0]

    (mine,) = run(gather_kernel, [(24, rows)], (flags, got, wide), [scalars(), whole(), anywhere()])
    mine, first_rows, last_rows = lax.optimization_barrier((mine, first_rows, last_rows))
    low, high = neighbours(last_rows, first_rows)
    mine, other = across_blocks(mine)
    block_part = block_product(got)
    p_inner, chunk, extra = pl.pallas_call(
        between_kernel,
        out_shape=[
            jax.ShapeDtypeStruct((2, rows), f32),
            pltpu.HBM((strips, 16, rows), f32),
            pltpu.HBM((2, 8, channels), f32),
        ],
        in_specs=[scalars()] * 3 + [whole()] * 9 + [anywhere()] * 2,
        out_specs=[whole(), far(), far()],
        scratch_shapes=chunk_scratch + [pltpu.VMEM((2, 8, channels), f32), pltpu.SemaphoreType.DMA],
        compiler_params=pltpu.CompilerParams(vmem_limit_bytes=vmem_bytes),
    )(
        flags, partners, band_offsets, block_part, inner_state, mine, other, inner_coupling, surface_amp, group, wide,
        mix, low, high,
    )
    got = lax.all_to_all(chunk, "chan", 0, 0)
    q_shape, notes_shape = (2, out_strips, points, lanes), (9 + 3 * out_strips, 8, lanes)
    wide, second, notes = pl.pallas_call(
        second_outer_kernel,
        grid=(1,),
        out_shape=[
            jax.ShapeDtypeStruct((2, out_strips, folded_rows, lanes), f32),
            pltpu.HBM(q_shape, f32),
            pltpu.HBM(notes_shape, f32),
        ],
        in_specs=[scalars(), in_one((2, 8, channels)), in_one((3, 4, channels)), in_one((3, 4, channels))]
        + [whole()] * 4,
        out_specs=[whole(), far(), far()],
        scratch_shapes=[pltpu.VMEM((2, points, channels), bf16)] * 2
        + [
            pltpu.VMEM(q_shape, f32),
            pltpu.VMEM((out_strips, points, lanes), f32),
            pltpu.VMEM((2, 2, 24, channels), f32),
            pltpu.VMEM(q_shape, f32),
            pltpu.VMEM(notes_shape, f32),
            pltpu.SemaphoreType.DMA((2,)),
        ],
        input_output_aliases={4: 0},
        compiler_params=pltpu.CompilerParams(vmem_limit_bytes=vmem_bytes),
    )(flags, pltpu.with_memory_space_constraint(extra, pltpu.HBM), low, high, wide, outer_state, potential, mix)
    (mine,) = run(
        gather_kernel, [(24, rows)], (flags, got, pltpu.with_memory_space_constraint(notes, pltpu.HBM)), [scalars(), whole(), far()]
    )
    mine, other = across_blocks(mine)
    block_part = block_product(got)
    q_inner, q_head, parts = run(
        last_kernel,
        [(2, rows), (2, 8, channels), (count, lanes)],
        (
            flags, partners, band_offsets, block_part, p_inner, mine, other, inner_coupling, surface_amp, group, wide,
            laser_mix, inner_state, second, notes,
        ),
        [scalars()] * 3 + [whole()] * 12,
        [pltpu.VMEM((2, 24, channels), f32)],
    )
    parts = lax.all_to_all(parts.reshape(count, 1, lanes), both, 0, 0).reshape(count, lanes)
    steps = 4
    last_inner, last_outer, columns, poor = pl.pallas_call(
        lambda *refs: finish_kernel(entries, *refs),
        grid=(steps,),
        out_shape=[
            jax.ShapeDtypeStruct(shape, f32)
            for shape in ((2, rows), (2, points, channels), (2, TERMS, TERMS + 1), (1, lanes))
        ],
        in_specs=[whole()] * 8,
        out_specs=[
            pl.BlockSpec((2, rows), lambda step: (0, 0)),
            pl.BlockSpec((2, points // steps, channels), lambda step: (0, step, 0)),
            pl.BlockSpec((2, TERMS, TERMS + 1), lambda step: (0, 0, 0)),
            pl.BlockSpec((1, lanes), lambda step: (0, 0)),
        ],
        scratch_shapes=[pltpu.VMEM((5, 8, lanes), f32)],
        compiler_params=pltpu.CompilerParams(vmem_limit_bytes=vmem_bytes),
    )(parts, inner_state, p_inner, q_inner, outer_state, wide, second, q_head)

    def again(state):
        last_inner, last_outer, hessenberg = step_by_step(*inputs)
        columns = hessenberg.transpose(0, 2, 1)
        (columns,) = run(same_kernel, [columns.shape], (columns,), [whole()])
        return jnp.zeros((), f32), last_inner, last_outer, columns

    _, last_inner, last_outer, columns = lax.while_loop(
        lambda state: state[0] > 0.0, again, (poor[0, 0], last_inner, last_outer, columns)
    )
    return last_inner, last_outer, columns.transpose(0, 2, 1)


def solution(mesh):
    return jax.shard_map(
        body,
        mesh=mesh,
        in_specs=(
            P(None, ("rad", "chan")),
            P(None, ("rad", "chan"), None),
            P("rad", None, "chan"),
            P("rad", None, None, "chan"),
            P("rad", None, "chan", None),
            P(("rad", "chan"), None),
            P(),
            P(),
            P(),
            P(),
        ),
        out_specs=(P(None, ("rad", "chan")), P(None, ("rad", "chan"), None), P()),
        check_vma=False,
    )
```

```python
import jax
import jax.numpy as jnp
from jax import lax
from jax.experimental import pallas as pl
from jax.experimental.pallas import tpu as pltpu
from jax.sharding import PartitionSpec as P

STRIP = 256
TERMS = 2

highest = lax.Precision.HIGHEST
kinetic_coef = -0.5 * 0.05 / (12.0 * 0.25 * 0.25)
slope_coef = 1.0 / (12.0 * 0.25)
bloch_coef = 2.0
shift = 1.5
least_left = 0.02
both = ("rad", "chan")


def spread(block, axis, holder):
    block = jnp.where(lax.axis_index(axis) == holder, block, jnp.zeros_like(block))
    return lax.psum(block, axis)


def local_parts(left, right):
    real_part = jnp.sum(left[0] * right[0]) + jnp.sum(left[1] * right[1])
    imag_part = jnp.sum(left[0][0] * right[0][1] - left[0][1] * right[0][0]) + jnp.sum(
        left[1][0] * right[1][1] - left[1][1] * right[1][0]
    )
    return jnp.stack([real_part, imag_part])


def rotate(vector, real_coef, imag_coef):
    return jnp.stack(
        [
            real_coef * vector[0] - imag_coef * vector[1],
            real_coef * vector[1] + imag_coef * vector[0],
        ]
    )


def neighbours(last_rows, first_rows):
    count = lax.axis_size(both)
    forward = [(i, i + 1) for i in range(count - 1)]
    backward = [(target, source) for source, target in forward]
    return lax.ppermute(last_rows, both, forward), lax.ppermute(first_rows, both, backward)


def outer_apply(extended, potential, laser_mix, moved):
    points = extended.shape[1] - 4
    far_left = extended[:, 0:points]
    near_left = extended[:, 1 : points + 1]
    centre_row = extended[:, 2 : points + 2]
    near_right = extended[:, 3 : points + 3]
    far_right = extended[:, 4 : points + 4]
    laplace = -far_left + 16.0 * near_left - 30.0 * centre_row + 16.0 * near_right - far_right
    slope_rows = slope_coef * (far_left - 8.0 * near_left + 8.0 * near_right - far_right)
    mixed_slope = jnp.einsum("prc,cd->prd", slope_rows, laser_mix, precision=highest)
    return (
        kinetic_coef * laplace
        + (potential - moved) * centre_row
        + jnp.stack([mixed_slope[1], -mixed_slope[0]])
    )


def inner_windows(shards, own_partners, own_offsets):
    windows = []
    for couple_index in range(own_partners.shape[0]):
        source = lax.dynamic_index_in_dim(shards, own_partners[couple_index], 0, keepdims=False)
        source = source.transpose(1, 0, 2).reshape(2, -1)
        band_width = source.shape[1] // 2
        windows.append(
            lax.dynamic_slice_in_dim(source, own_offsets[couple_index] + band_width, band_width, 1)
        )
    return windows


def exchange(inner_vec, ghost_part, row):
    rows = inner_vec.shape[1]
    blocks, strips = lax.axis_size("rad"), lax.axis_size("chan")
    chunk = jnp.concatenate(
        [
            inner_vec,
            ghost_part.reshape(-1, rows),
            row.reshape(-1, rows),
            jnp.zeros((2, rows), jnp.float32),
        ],
        axis=0,
    )
    got = lax.all_to_all(jnp.broadcast_to(chunk, (strips,) + chunk.shape), "chan", 0, 0)
    own = got[:, 0:2]
    ghost_sum = jnp.sum(got[:, 2:10], axis=0)
    padded = jnp.pad(own, ((2, 1), (0, 0), (0, 0)))
    near = lax.dynamic_slice_in_dim(padded, lax.axis_index("chan"), 4, 0)
    chunk = jnp.concatenate(
        [near.reshape(8, rows), ghost_sum, got[0, 10:14], jnp.zeros((4, rows), jnp.float32)],
        axis=0,
    )
    got_blocks = lax.all_to_all(jnp.broadcast_to(chunk, (blocks,) + chunk.shape), "rad", 0, 0)
    shards = got_blocks[:, 0:8].reshape(blocks, 4, 2, rows)
    ghost = jnp.sum(got_blocks[:, 8:16], axis=0).reshape(2, 2, -1)
    first_row = got_blocks[0, 16:20].reshape(2, -1)
    return own.transpose(1, 0, 2).reshape(2, -1), shards, ghost, first_row


def step_by_step(
    inner_state,
    outer_state,
    inner_ham,
    inner_coupling,
    surface_amp,
    potential,
    laser_mix,
    partners,
    band_offsets,
    channel_group,
):
    block_order = inner_ham.shape[1]
    points, channels = outer_state.shape[1:]
    entries = float(
        lax.axis_size("rad") * block_order + lax.axis_size(both) * points * channels
    )
    block_index = lax.axis_index("rad")
    is_first = lax.axis_index(both) == 0
    member = (channel_group == block_index).astype(jnp.float32)
    masked_amp = surface_amp[0] * member[None, None, :]
    own_partners = lax.dynamic_index_in_dim(partners, block_index, 0, keepdims=False)
    own_offsets = lax.dynamic_index_in_dim(band_offsets, block_index, 0, keepdims=False)

    def total(value):
        return lax.psum(value, both) / entries

    def squares(vector):
        return jnp.sum(vector[0] * vector[0]) + jnp.sum(vector[1] * vector[1])

    start_len = jnp.sqrt(total(squares((inner_state, outer_state))))
    krylov = [(inner_state / start_len, outer_state / start_len)]
    hessenberg = jnp.zeros((2, TERMS + 1, TERMS), jnp.float32)
    for term_index in range(TERMS):
        inner_vec, outer_vec = krylov[term_index]
        ghost_part = jnp.einsum("pk,mki->pmi", inner_vec, masked_amp, precision=highest)
        row = jnp.where(is_first, outer_vec[:, 0], 0.0)
        own_vec, shards, ghost, first_row = exchange(inner_vec, ghost_part, row)
        result_in = jnp.dot(own_vec, inner_ham[0], precision=highest)
        for couple_index, window in enumerate(inner_windows(shards, own_partners, own_offsets)):
            result_in = result_in + jnp.dot(window, inner_coupling[0, couple_index], precision=highest)
        result_in = result_in + bloch_coef * jnp.einsum(
            "pi,ki->pk", first_row, masked_amp[0], precision=highest
        )
        low, high = neighbours(outer_vec[:, points - 2 :], outer_vec[:, :2])
        low = jnp.where(is_first, ghost[:, ::-1], low)
        extended = jnp.concatenate([low, outer_vec, high], axis=1)
        image = (result_in, outer_apply(extended, potential, laser_mix, 0.0))
        for prior_index in range(term_index + 1):
            prior = krylov[prior_index]
            coefs = total(local_parts(prior, image))
            image = tuple(
                part - rotate(prior_part, coefs[0], coefs[1])
                for part, prior_part in zip(image, prior)
            )
            hessenberg = hessenberg.at[:, prior_index, term_index].set(coefs)
        new_length = jnp.sqrt(total(squares(image)))
        hessenberg = hessenberg.at[0, term_index + 1, term_index].set(new_length)
        krylov.append((image[0] / new_length, image[1] / new_length))
    return (krylov[-1][0], krylov[-1][1], hessenberg)


lanes = 128
margin = 8
reach = 2
vmem_bytes = 16 * 2**20


def whole():
    return pl.BlockSpec(memory_space=pltpu.VMEM)


def anywhere():
    return pl.BlockSpec(memory_space=pl.ANY)


def far():
    return pl.BlockSpec(memory_space=pltpu.HBM)


def in_one(shape):
    return pl.BlockSpec(shape, lambda i: (0,) * len(shape))


def scalars():
    return pl.BlockSpec(memory_space=pltpu.SMEM)


def run(kernel, outs, args, in_specs, scratch=()):
    return pl.pallas_call(
        kernel,
        out_shape=[jax.ShapeDtypeStruct(*out) if isinstance(out[0], tuple) else jax.ShapeDtypeStruct(out, jnp.float32) for out in outs],
        in_specs=in_specs,
        out_specs=[whole()] * len(outs),
        scratch_shapes=list(scratch),
        compiler_params=pltpu.CompilerParams(vmem_limit_bytes=vmem_bytes),
    )(*args)


def two(x):
    high = x.astype(jnp.bfloat16)
    return high, (x - high.astype(jnp.float32)).astype(jnp.bfloat16)


def both_halves(x):
    high, low = two(x)
    rest = jnp.zeros((16 - 2 * x.shape[0], x.shape[1]), jnp.float32)
    return jnp.concatenate([high.astype(jnp.float32), low.astype(jnp.float32), rest], axis=0).astype(jnp.bfloat16)


def few_rows_dot(x, weights, flipped=False):
    rows = x.shape[0]
    lhs = both_halves(x)
    dims = (((1,), (1 if flipped else 0,)), ((), ()))
    total = sum(lax.dot_general(lhs, part, dims, preferred_element_type=jnp.float32) for part in weights)
    return total[:rows] + total[rows : 2 * rows]


def mixed_with(high, low, mix_ref):
    count = high.shape[0]
    first = jnp.dot(jnp.concatenate([high, low], axis=0), mix_ref[0], preferred_element_type=jnp.float32)
    return first[:count] + first[count:] + jnp.dot(high, mix_ref[1], preferred_element_type=jnp.float32)


def write_chunk(out_ref, held_ref, written, inner_vec, ghosts, row, others=()):
    half = inner_vec.shape[1]
    held_ref[...] = jnp.concatenate(
        [
            ghosts[:, :half],
            ghosts[:, half:],
            inner_vec,
            row[:, :half],
            row[:, half:],
            jnp.zeros((2, half), jnp.float32),
        ],
        axis=0,
    )
    copies = [
        pltpu.make_async_copy(held_ref, out_ref.at[strip, pl.ds(0, 16)], written.at[strip])
        for strip in range(out_ref.shape[0])
    ]
    for copy in copies:
        copy.start()
    for copy in [*others, *copies]:
        copy.wait()


def ghost_rows(inner_vec, amps, member):
    return jnp.concatenate([few_rows_dot(inner_vec, amp) * member for amp in amps], axis=0)


def member_of(group_ref):
    return jnp.where(group_ref[...] == lax.axis_index("rad"), 1.0, 0.0)


def at_first():
    return (lax.axis_index("rad") == 0) & (lax.axis_index("chan") == 0)


def at_last():
    last = [lax.axis_index(axis) == lax.axis_size(axis) - 1 for axis in both]
    return last[0] & last[1]


def send_ends(chunk_ref, ends_ref, written, first_rows, last_rows):
    half = ends_ref.shape[2]
    for end, points in enumerate((last_rows, first_rows)):
        for k in range(2):
            for part in range(2):
                ends_ref[end, 4 * k + 2 * part : 4 * k + 2 * part + 2] = points[part][:, k * half : (k + 1) * half]
    strips = chunk_ref.shape[0]
    copies = [
        pltpu.make_async_copy(
            ends_ref.at[end],
            chunk_ref.at[lax.rem(lax.axis_index("chan") + there, strips), pl.ds(16, 8)],
            written.at[end],
        )
        for end, there in enumerate((1, strips - 1))
    ]
    for copy in copies:
        copy.start()
    return copies


def start_kernel(
    inner_ref, head_ref, tail_ref, amp_ref, group_ref, chunk_ref, held_ref, written, ends_ref, ends_written
):
    ends = send_ends(
        chunk_ref, ends_ref, ends_written, [head_ref[part, 0:2] for part in range(2)], [tail_ref[part, 6:8] for part in range(2)]
    )
    row = jnp.concatenate([head_ref[part, 0:1] for part in range(2)], axis=0)
    row = jnp.where(at_first(), row, 0.0)
    inner_vec = inner_ref[...]
    amps = [two(amp_ref[0, radius]) for radius in range(2)]
    ghosts = ghost_rows(inner_vec, amps, member_of(group_ref))
    write_chunk(chunk_ref, held_ref, written, inner_vec, ghosts, row, ends)


def stencils(window, pot):
    before_2, before_1, here, after_1, after_2 = window
    local = (pot - (30.0 * kinetic_coef + shift)) * here + (
        16.0 * kinetic_coef * (before_1 + after_1) - kinetic_coef * (before_2 + after_2)
    )
    return local, (before_2 - after_2) + 8.0 * (after_1 - before_1)


def first_outer_kernel(
    state_ref, pot_ref, mix_ref, out_ref, mix_out, edges_ref, wide_ref, pot_wide, slope_h, slope_l
):
    points, channels = state_ref.shape[1:]
    strips = channels // lanes
    length = points // 8
    for strip in range(strips):
        here = slice(strip * lanes, (strip + 1) * lanes)
        for part in range(3):
            source = pot_ref if part == 2 else state_ref.at[part]
            target = pot_wide.at[strip] if part == 2 else wide_ref.at[part, strip]
            target[margin : margin + points] = source[:, here]
            target[0:margin] = jnp.zeros((margin, lanes), jnp.float32)
            target[margin + points :] = jnp.zeros((margin, lanes), jnp.float32)
    for part in range(3):
        source = pot_ref if part == 2 else state_ref.at[part]
        edges_ref[0, part], edges_ref[1, part] = source[0:8], source[points - 8 : points]

    def strip_step(step, _):
        part, strip = lax.div(step, strips), lax.rem(step, strips)

        def load(place):
            return wide_ref[part, strip, pl.ds(margin + place, 8, stride=length)]

        window = [load(place) for place in range(-2 * reach, 0)]
        columns = pl.ds(pl.multiple_of(strip * lanes, lanes), lanes)
        for first in range(-reach, length + reach, 2):
            slopes = []
            for place in (first, first + 1):
                window.append(load(place + reach))
                local, slope = stencils(window, pot_wide[strip, pl.ds(margin + place, 8, stride=length)])
                out_ref[part, strip, (place + reach) * 8 : (place + reach + 1) * 8] = local
                slopes.append(slope)
                window.pop(0)
            rows = slice((first + reach) * 8, (first + reach + 2) * 8)
            slope_h[part, rows, columns], slope_l[part, rows, columns] = two(jnp.concatenate(slopes, axis=0))
        return 0

    lax.fori_loop(0, 2 * strips, strip_step, 0)
    mix_out[0], mix_out[1] = two(slope_coef * mix_ref[...])
    add_mixed(out_ref, slope_h, slope_l, mix_out)


def add_mixed(out_ref, slope_h, slope_l, mix_ref):
    for part in range(2):
        mixed = mixed_with(slope_h[1 - part], slope_l[1 - part], mix_ref)
        for strip in range(out_ref.shape[1]):
            own = mixed[:, strip * lanes : (strip + 1) * lanes]
            out_ref[part, strip] = out_ref[part, strip] + (own if part == 0 else -own)


def products(s, p, q):
    return [
        s[0] * s[0] + s[1] * s[1],
        s[0] * p[0] + s[1] * p[1],
        s[0] * p[1] - s[1] * p[0],
        s[0] * q[0] + s[1] * q[1],
        s[0] * q[1] - s[1] * q[0],
        p[0] * p[0] + p[1] * p[1],
        p[0] * q[0] + p[1] * q[1],
        p[0] * q[1] - p[1] * q[0],
        q[0] * q[0] + q[1] * q[1],
    ]


def second_outer_kernel(
    patch_ref, wide_in, state_in, pot_in, mix_ref,
    wide_ref, q_out, notes_out, slope_h, slope_l, state_ref, pot_ref, out_ref, notes_ref, written,
):
    strips, places = out_ref.shape[1:3]
    length = places // 8
    for part in range(2):
        for strip in range(strips):
            here = slice(strip * lanes, (strip + 1) * lanes)
            wide_ref[part, strip, pl.ds(reach * 8, 2, stride=8)] = patch_ref[part, 0:2, here]
            wide_ref[part, strip, pl.ds(length * 8 + 7, 2, stride=8)] = patch_ref[part, 2:4, here]
    for strip in range(strips):
        here = slice(strip * lanes, (strip + 1) * lanes)
        pot_ref[strip] = pot_in[:, here]
        for part in range(2):
            state_ref[part, strip] = state_in[part, :, here]

    def strip_step(step, _):
        part, strip = lax.div(step, strips), lax.rem(step, strips)

        def load(place):
            return wide_ref[part, strip, (place + reach) * 8 : (place + reach + 1) * 8]

        window = [load(place) for place in range(-reach, reach)]
        columns = pl.ds(pl.multiple_of(strip * lanes, lanes), lanes)
        for first in range(0, length, 2):
            slopes = []
            for place in (first, first + 1):
                window.append(load(place + reach))
                local, slope = stencils(window, pot_ref[strip, pl.ds(place, 8, stride=length)])
                out_ref[part, strip, place * 8 : (place + 1) * 8] = local
                slopes.append(slope)
                window.pop(0)
            rows = slice(first * 8, (first + 2) * 8)
            slope_h[part, rows, columns], slope_l[part, rows, columns] = two(jnp.concatenate(slopes, axis=0))
        return 0

    lax.fori_loop(0, 2 * strips, strip_step, 0)
    add_mixed(out_ref, slope_h, slope_l, mix_ref)
    copy = pltpu.make_async_copy(out_ref, q_out, written.at[0])
    copy.start()
    run_of = lax.broadcasted_iota(jnp.int32, (8, lanes), 0)

    def gram_step(strip, sums):
        for place in range(length):
            entries = products(
                [state_ref[part, strip, pl.ds(place, 8, stride=length)] for part in range(2)],
                [wide_ref[part, strip, (place + reach) * 8 : (place + reach + 1) * 8] for part in range(2)],
                [out_ref[part, strip, place * 8 : (place + 1) * 8] for part in range(2)],
            )
            if place < 4 or place >= length - 4:
                inside = run_of > 0 if place < 4 else run_of < 7
                entries = [jnp.where(inside, entry, 0.0) for entry in entries]
            sums = [total + entry for total, entry in zip(sums, entries)]
        return sums

    sums = lax.fori_loop(0, strips, gram_step, [jnp.zeros((8, lanes), jnp.float32)] * 9)
    for k in range(9):
        notes_ref[k] = sums[k]
    for strip in range(strips):
        here = slice(strip * lanes, (strip + 1) * lanes)
        for end, rows in enumerate((slice(0, 8), slice(places - 8, places))):
            notes_ref[9 + strips * 3 * end + strip] = pot_in[rows, here]
            for part in range(2):
                notes_ref[9 + strips * (3 * end + part + 1) + strip] = state_in[part, rows, here]
    notes_copy = pltpu.make_async_copy(notes_ref, notes_out, written.at[1])
    notes_copy.start()
    copy.wait()
    notes_copy.wait()


def block_kernel(first, got_ref, ham_ref, out_ref, held_ref, arrived):
    rows = ham_ref.shape[2]
    pieces, size = held_ref.shape[:2]
    copies = [
        pltpu.make_async_copy(ham_ref.at[0, pl.ds((first + k) * size, size)], held_ref.at[k], arrived.at[k])
        for k in range(pieces)
    ]
    for copy in copies:
        copy.start()
    total = jnp.zeros((16, rows), jnp.float32)
    for k, copy in enumerate(copies):
        copy.wait()
        for part in range(size // rows):
            lhs = both_halves(got_ref[(first + k) * (size // rows) + part, 8:10])
            for weights in two(held_ref[k, part * rows : (part + 1) * rows]):
                total = total + jnp.dot(lhs, weights, preferred_element_type=jnp.float32)
    out_ref[...] = total[0:2] + total[2:4]


def gather_kernel(got_ref, after_ref, out_ref, ends_ref):
    strips = got_ref.shape[0]
    own = lax.axis_index("chan")
    for k in range(4):
        strip = own + (k - 2)
        there = (strip >= 0) & (strip < strips)
        near = got_ref[jnp.clip(strip, 0, strips - 1), 8:10]
        out_ref[2 * k : 2 * k + 2] = jnp.where(there, near, 0.0)
    out_ref[8:16] = sum(got_ref[strip, 0:8] for strip in range(strips))
    out_ref[16:20] = got_ref[0, 10:14]
    out_ref[20:24] = jnp.zeros((4, got_ref.shape[2]), jnp.float32)
    before = got_ref[lax.rem(own + strips - 1, strips), 16:24]
    after = got_ref[lax.rem(own + 1, strips), 16:24]
    ends_ref[0], ends_ref[1] = before, after
    out_ref[24:32] = jnp.where(own == 0, before, after)


def join_kernel(mine_ref, other_ref, after_ref, out_ref):
    count = mine_ref.shape[0] - 24
    out_ref[0:count] = mine_ref[0:count]
    out_ref[count : 2 * count] = other_ref[0:count]
    out_ref[2 * count : 2 * count + 16] = mine_ref[count : count + 16] + other_ref[count : count + 16]
    keep = (count > 8) | ((lax.rem(lax.axis_index("rad"), 2) == 1) == (lax.axis_index("chan") == 0))
    out_ref[2 * count + 16 :] = jnp.where(keep, mine_ref[count + 16 :], other_ref[count + 16 :])


def join(mine, other, after):
    shape = (2 * mine.shape[0] - 24, mine.shape[1])
    return run(join_kernel, [shape], (mine, other, after), [whole()] * 2 + [anywhere()])[0]


def inner_result(partners_ref, offsets_ref, block_a, block_b, block_c, inner_ref, mine_ref, other_ref, coupling_ref, amp_ref, member, row):
    result = block_a[...] + block_b[...] + block_c[...] - shift * inner_ref[...]
    couplings, band_width = coupling_ref.shape[1:3]
    block_index = lax.axis_index("rad")
    for couple_index in range(couplings):
        apart = partners_ref[couple_index, block_index] ^ block_index
        far_pair = lax.shift_right_logical(apart, 2)
        slot = apart ^ (2 * far_pair)
        rows = pl.ds(pl.multiple_of(lax.rem(slot, 4) * 8, 8), 8)
        near = jnp.where(slot < 4, mine_ref[rows], other_ref[rows])
        near = jnp.concatenate([near[2 * k : 2 * k + 2] for k in range(4)], axis=1)
        near = jnp.concatenate([near, jnp.zeros((6, near.shape[1]), jnp.float32)], axis=0)
        first = offsets_ref[couple_index, block_index] + band_width
        window = pltpu.roll(near, near.shape[1] - first, 1)[0:2, :band_width]
        result = result + few_rows_dot(window, two(coupling_ref[0, couple_index]))
    return result + bloch_coef * few_rows_dot(row * member, two(amp_ref[0, 0]), flipped=True)


def unpacked(mine_ref, other_ref):
    sums = mine_ref[32:48] + other_ref[32:48]
    ghosts = jnp.concatenate([sums[0:4], sums[4:8]], axis=1)
    row = jnp.concatenate([sums[8:10], sums[10:12]], axis=1)
    return ghosts, row


def points_of(ref, part, first, count, run_index=0):
    return jnp.concatenate(
        [ref[part, strip, pl.ds(first * 8 + run_index, count, stride=8)] for strip in range(ref.shape[1])], axis=1
    )


def mend(edge_ref, pots, mix_ref, more=None):
    local, slopes = [], []
    for part in range(2):
        for end in range(2):
            inner, slope = stencils([edge_ref[part, end, 8 + k : 16 + k] for k in range(-reach, reach + 1)], pots[end])
            local.append(inner)
            slopes.append(slope)
    mixed = mixed_with(*two(jnp.concatenate(slopes + ([] if more is None else [more]), axis=0)), mix_ref)
    image = [
        [
            local[2 * part + end] + (mixed[16 + 8 * end : 24 + 8 * end] if part == 0 else -mixed[8 * end : 8 * end + 8])
            for end in range(2)
        ]
        for part in range(2)
    ]
    return image, mixed[32:]


def pick_ends(ends_ref, core_ref, near_ref, far_ref):
    block, strip = lax.axis_index("rad"), lax.axis_index("chan")
    core, chip = lax.rem(block, 2), lax.div(block, 2)
    is_low, is_high = strip == 0, strip == lax.axis_size("chan") - 1
    from_core = (core == 1) == is_low
    from_near = (lax.rem(chip, 2) == 1) == is_low
    came = jnp.where(from_core, core_ref[24:32], jnp.where(from_near, near_ref[32:40], far_ref[48:56]))
    before = jnp.where(at_first(), 0.0, jnp.where(is_low, came, ends_ref[0]))
    after = jnp.where(at_last(), 0.0, jnp.where(is_high, came, ends_ref[1]))
    return [
        [jnp.concatenate([x[2 * part : 2 * part + 2], x[4 + 2 * part : 6 + 2 * part]], axis=1) for part in range(2)]
        for x in (before, after)
    ]


def between_kernel(
    partners_ref, offsets_ref, block_a, block_b, block_c, inner_ref, mine_ref, other_ref, coupling_ref, amp_ref, group_ref,
    edges_ref, mix_ref, ends_ref, core_ref, near_ref,
    image_ref, chunk_ref, patch_out, held_ref, written, send_ref, ends_written, patch_ref, patch_written, edge_ref,
):
    member = member_of(group_ref)
    ghosts, row = unpacked(mine_ref, other_ref)
    before, after = pick_ends(ends_ref, core_ref, near_ref, other_ref)
    edge_ref[...] = jnp.zeros_like(edge_ref)
    for part in range(2):
        edge_ref[part, 0, 6:8] = before[part]
        edge_ref[part, 1, 16:18] = after[part]
        for end in range(2):
            edge_ref[part, end, 8:16] = edges_ref[end, part]
    near, far_off = ghosts[0:2], ghosts[2:4]
    kinetic = [kinetic_coef * (16.0 * near - far_off), -kinetic_coef * near]
    slope = jnp.concatenate([far_off - 8.0 * near, near, jnp.zeros((12, near.shape[1]), jnp.float32)], axis=0)
    p, mixed = mend(edge_ref, [edges_ref[end, 2] for end in range(2)], mix_ref, slope)
    first_rows, last_rows = [], []
    for part in range(2):
        extra = jnp.concatenate(
            [
                kinetic[k][part : part + 1]
                + (mixed[2 * k + 1 : 2 * k + 2] if part == 0 else -mixed[2 * k : 2 * k + 1])
                for k in range(2)
            ],
            axis=0,
        )
        first_rows.append(p[part][0][0:2] + jnp.where(at_first(), extra, 0.0))
        last_rows.append(p[part][1][6:8])
        patch_ref[part] = jnp.concatenate(
            [first_rows[part], last_rows[part], jnp.zeros((4, near.shape[1]), jnp.float32)], axis=0
        )
    copy = pltpu.make_async_copy(patch_ref, patch_out, patch_written)
    copy.start()
    copies = [copy] + send_ends(chunk_ref, send_ref, ends_written, first_rows, last_rows)
    image = inner_result(
        partners_ref, offsets_ref, block_a, block_b, block_c, inner_ref, mine_ref, other_ref, coupling_ref, amp_ref, member, row
    )
    image_ref[...] = image
    row = jnp.where(at_first(), jnp.concatenate([rows[0:1] for rows in first_rows], axis=0), 0.0)
    amps = [two(amp_ref[0, radius]) for radius in range(2)]
    write_chunk(chunk_ref, held_ref, written, image, ghost_rows(image, amps, member), row, copies)


def last_kernel(
    partners_ref, offsets_ref, block_a, block_b, block_c, inner_ref, mine_ref, other_ref, coupling_ref, amp_ref, group_ref,
    wide_ref, mix_ref, ends_ref, core_ref, near_ref, start_ref, second_ref, notes_ref,
    image_ref, out_ref, parts_ref, edge_ref,
):
    member = member_of(group_ref)
    ghosts, row = unpacked(mine_ref, other_ref)
    image = inner_result(
        partners_ref, offsets_ref, block_a, block_b, block_c, inner_ref, mine_ref, other_ref, coupling_ref, amp_ref, member, row
    )
    image_ref[...] = image
    strips = wide_ref.shape[1]
    length = second_ref.shape[2] // 8
    noted = [
        [
            jnp.concatenate([notes_ref[9 + strips * (3 * end + k) + strip] for strip in range(strips)], axis=1)
            for k in range(3)
        ]
        for end in range(2)
    ]
    before, after = pick_ends(ends_ref, core_ref, near_ref, other_ref)
    edge_ref[...] = jnp.zeros_like(edge_ref)
    for part in range(2):
        ghost = jnp.concatenate([ghosts[2 + part : 3 + part], ghosts[part : part + 1]], axis=0)
        edge_ref[part, 0, 6:8] = jnp.where(at_first(), ghost, before[part])
        edge_ref[part, 0, 8:24] = points_of(wide_ref, part, reach, 16)
        edge_ref[part, 1, 0:16] = points_of(wide_ref, part, length + reach - 16, 16, 7)
        edge_ref[part, 1, 16:18] = after[part]
    q, _ = mend(edge_ref, [noted[end][0] for end in range(2)], mix_ref)
    row_of = lax.broadcasted_iota(jnp.int32, q[0][0].shape, 0)
    mended = [row_of < 4, row_of >= 4]
    totals = [notes_ref[k] for k in range(9)]
    for end in range(2):
        for part in range(2):
            there = points_of(second_ref, part, 0 if end == 0 else length - 8, 8, 7 * end)
            q[part][end] = jnp.where(mended[end], q[part][end], there)
            out_ref[end, part] = q[part][end]
        entries = products(noted[end][1:], [edge_ref[part, end, 8:16] for part in range(2)], [q[part][end] for part in range(2)])
        for k, entry in enumerate(entries):
            entry = jnp.where(mended[end], entry, 0.0)
            totals[k] = totals[k] + sum(entry[:, strip * lanes : (strip + 1) * lanes] for strip in range(strips))
    start, inner = start_ref[...], inner_ref[...]
    inside = products([start[0:1], start[1:2]], [inner[0:1], inner[1:2]], [image[0:1], image[1:2]])
    lane = lax.broadcasted_iota(jnp.int32, (1, lanes), 1)
    sums = jnp.zeros((1, lanes), jnp.float32)
    for k in range(9):
        line = jnp.sum(totals[k], axis=0, keepdims=True) + inside[k][:, :lanes] + inside[k][:, lanes:]
        sums = jnp.where(lane == k, jnp.sum(line, axis=1, keepdims=True), sums)
    parts_ref[...] = jnp.broadcast_to(sums, parts_ref.shape)


def arnoldi_coefs(gram):
    ss, spr, spi, sqr, sqi, pp, pqr, pqi, qq = gram
    cr, ci = spr / ss, spi / ss
    left_1 = pp - (spr * cr + spi * ci)
    h10 = jnp.sqrt(left_1 / ss)
    sxr = sqr - (cr * spr - ci * spi)
    sxi = sqi - (cr * spi + ci * spr)
    h01r, h01i = sxr / (ss * h10), sxi / (ss * h10)
    pxr, pxi = pqr - cr * pp, pqi - ci * pp
    yxr = pxr - (cr * sxr + ci * sxi)
    yxi = pxi - (cr * sxi - ci * sxr)
    scale = 1.0 / left_1
    h11r, h11i = yxr * scale, yxi * scale
    xx = (qq - 2.0 * (cr * pqr + ci * pqi) + (cr * cr + ci * ci) * pp) * scale
    left_2 = xx - (h01r * h01r + h01i * h01i) - (h11r * h11r + h11i * h11i)
    h21 = jnp.sqrt(left_2)
    fine = (left_1 > least_left * pp) & (left_2 > least_left * xx)
    poor = jnp.where(fine, 0.0, 1.0)
    zero = jnp.zeros_like(ss)
    entries = [[[cr + shift, h10, zero], [h01r, h11r + shift, h21]], [[ci, zero, zero], [h01i, h11i, zero]]]
    a = jnp.sqrt(ss)
    coef_q = 1.0 / (a * h10 * h21)
    coef_p = (-(cr + h11r) * coef_q, -(ci + h11i) * coef_q)
    coef_s = (
        (h11r * cr - h11i * ci) * coef_q - h01r / (a * h21),
        (h11r * ci + h11i * cr) * coef_q - h01i / (a * h21),
    )
    return entries, (coef_q, coef_p, coef_s), poor


def combined(coefs, s, p, q):
    coef_q, coef_p, coef_s = coefs
    return (
        coef_q * q[0] + coef_p[0] * p[0] - coef_p[1] * p[1] + coef_s[0] * s[0] - coef_s[1] * s[1],
        coef_q * q[1] + coef_p[0] * p[1] + coef_p[1] * p[0] + coef_s[0] * s[1] + coef_s[1] * s[0],
    )


def finish_kernel(
    entries, parts_ref, start_ref, inner_ref, image_ref, state_ref, wide_ref, second_ref, edge_ref,
    inner_out, outer_out, hess_out, poor_out, coef_ref,
):
    step = pl.program_id(0)
    count = outer_out.shape[1]
    strips, places = second_ref.shape[1:3]
    length = places // 8

    @pl.when(step == 0)
    def _():
        sums = jnp.sum(parts_ref[...], axis=0, keepdims=True) * (1.0 / entries)
        lane = lax.broadcasted_iota(jnp.int32, sums.shape, 1)
        gram = [jnp.sum(jnp.where(lane == k, sums, 0.0), axis=1, keepdims=True) for k in range(9)]
        values, (coef_q, coef_p, coef_s), poor = arnoldi_coefs(gram)
        for k, coef in enumerate([coef_q, *coef_p, *coef_s]):
            coef_ref[k] = jnp.broadcast_to(coef, (8, lanes))
        lane = lax.broadcasted_iota(jnp.int32, (1, TERMS + 1), 1)
        for part in range(2):
            for column in range(TERMS):
                line = jnp.zeros((1, TERMS + 1), jnp.float32)
                for k, value in enumerate(values[part][column]):
                    line = jnp.where(lane == k, value, line)
                hess_out[part, column : column + 1] = line
        poor_out[...] = jnp.broadcast_to(poor, poor_out.shape)

    coefs = coef_ref[0], (coef_ref[1], coef_ref[2]), (coef_ref[3], coef_ref[4])
    few = count // length
    for run_index in range(few):
        own = step * few + run_index
        for first in range(0, length, 8):
            rows = pl.ds(pl.multiple_of(own * length + first, 8), 8)
            for strip in range(strips):
                result = combined(
                    coefs,
                    [state_ref[part, rows, strip * lanes : (strip + 1) * lanes] for part in range(2)],
                    [wide_ref[part, strip, pl.ds((first + reach) * 8 + own, 8, stride=8)] for part in range(2)],
                    [second_ref[part, strip, pl.ds(first * 8 + own, 8, stride=8)] for part in range(2)],
                )
                for part in range(2):
                    outer_out[
                        part,
                        run_index * length + first : run_index * length + first + 8,
                        strip * lanes : (strip + 1) * lanes,
                    ] = result[part]

    def put_end(end):
        first = 0 if end == 0 else length - 8
        rows = slice(0, 8) if end == 0 else slice(count - 8, count)
        for strip in range(strips):
            here = slice(strip * lanes, (strip + 1) * lanes)
            result = combined(
                coefs,
                [state_ref[part, 0:8, here] if end == 0 else state_ref[part, places - 8 : places, here] for part in range(2)],
                [wide_ref[part, strip, pl.ds((first + reach) * 8 + 7 * end, 8, stride=8)] for part in range(2)],
                [edge_ref[end, part, :, here] for part in range(2)],
            )
            for part in range(2):
                outer_out[part, rows, here] = result[part]

    @pl.when(step == pl.num_programs(0) - 1)
    def _():
        put_end(1)

    @pl.when(step == 0)
    def _():
        put_end(0)
        rows = inner_out.shape[1]
        for first in range(0, rows, lanes):
            here = slice(first, first + lanes)
            result = combined(
                [coefs[0][0:1], [c[0:1] for c in coefs[1]], [c[0:1] for c in coefs[2]]],
                *[[ref[0:1, here], ref[1:2, here]] for ref in (start_ref, inner_ref, image_ref)],
            )
            for part in range(2):
                inner_out[part : part + 1, here] = result[part]


def same_kernel(in_ref, out_ref):
    out_ref[...] = in_ref[...]


def across_blocks(mine, after):
    blocks = lax.axis_size("rad")
    last = blocks // 2 - 1
    core = lax.ppermute(mine, "rad", [(i, i ^ 1) for i in range(blocks)])
    mine = join(mine, core, after[0])
    near = lax.ppermute(mine, "rad", [(i, i ^ 2) for i in range(blocks)])
    mine = join(mine, near, after[1])
    return mine, (core, near, lax.ppermute(mine, "rad", [(i, 2 * (last - i // 2) + i % 2) for i in range(blocks)]))


def body(*inputs):
    (
        inner_state,
        outer_state,
        inner_ham,
        inner_coupling,
        surface_amp,
        potential,
        laser_mix,
        partners,
        band_offsets,
        channel_group,
    ) = inputs
    block_order, rows = inner_ham.shape[1:]
    points, channels = outer_state.shape[1:]
    count = lax.axis_size(both)
    blocks, strips = lax.axis_size("rad"), lax.axis_size("chan")
    entries = float(blocks * block_order + count * points * channels)
    group = channel_group.reshape(1, channels)
    by_coupling = partners.T, band_offsets.T
    f32, bf16 = jnp.float32, jnp.bfloat16
    out_strips = channels // lanes
    folded_rows = points + 2 * reach * 8

    ends_scratch = [pltpu.VMEM((2, 8, rows), f32), pltpu.SemaphoreType.DMA((2,))]
    chunk_scratch = [pltpu.VMEM((16, rows), f32), pltpu.SemaphoreType.DMA((strips,))]
    chunk = pl.pallas_call(
        start_kernel,
        grid=(1,),
        out_shape=pltpu.HBM((strips, 24, rows), f32),
        in_specs=[
            whole(),
            in_one((2, 8, channels)),
            pl.BlockSpec((2, 8, channels), lambda i: (0, points // 8 - 1, 0)),
            whole(),
            whole(),
        ],
        out_specs=far(),
        scratch_shapes=chunk_scratch + ends_scratch,
        compiler_params=pltpu.CompilerParams(vmem_limit_bytes=vmem_bytes),
    )(inner_state, outer_state, outer_state, surface_amp, group)
    got = lax.all_to_all(chunk, "chan", 0, 0)
    wide, mix, edges = pl.pallas_call(
        first_outer_kernel,
        out_shape=[
            jax.ShapeDtypeStruct((2, out_strips, folded_rows, lanes), f32),
            jax.ShapeDtypeStruct((2, channels, channels), bf16),
            jax.ShapeDtypeStruct((2, 3, 8, channels), f32),
        ],
        in_specs=[whole()] * 3,
        out_specs=[whole()] * 3,
        scratch_shapes=[
            pltpu.VMEM((2, out_strips, points + 2 * margin, lanes), f32),
            pltpu.VMEM((out_strips, points + 2 * margin, lanes), f32),
            pltpu.VMEM((2, folded_rows, channels), bf16),
            pltpu.VMEM((2, folded_rows, channels), bf16),
        ],
        compiler_params=pltpu.CompilerParams(vmem_limit_bytes=vmem_bytes),
    )(outer_state, potential, laser_mix)

    def block_product(got):
        size = 2 * rows
        parts = []
        for first, last in ((0, 2), (2, 5), (5, 8)):
            parts += run(
                lambda *refs, first=first: block_kernel(first, *refs),
                [(2, rows)],
                (got, inner_ham),
                [whole(), anywhere()],
                [pltpu.VMEM((last - first, size, rows), f32), pltpu.SemaphoreType.DMA((last - first,))],
            )
        return parts

    gathered = [(32, rows), (2, 8, rows)]
    mine, ends = run(gather_kernel, gathered, (got, wide), [whole(), anywhere()])
    block_parts = block_product(got)
    mine, came = across_blocks(mine, block_parts)
    p_inner, chunk, patch = pl.pallas_call(
        between_kernel,
        out_shape=[
            jax.ShapeDtypeStruct((2, rows), f32),
            pltpu.HBM((strips, 24, rows), f32),
            pltpu.HBM((2, 8, channels), f32),
        ],
        in_specs=[scalars()] * 2 + [whole()] * 14,
        out_specs=[whole()] + [far()] * 2,
        scratch_shapes=chunk_scratch
        + ends_scratch
        + [pltpu.VMEM((2, 8, channels), f32), pltpu.SemaphoreType.DMA, pltpu.VMEM((2, 2, 24, channels), f32)],
        compiler_params=pltpu.CompilerParams(vmem_limit_bytes=vmem_bytes),
    )(
        *by_coupling, *block_parts, inner_state, mine, came[2], inner_coupling, surface_amp, group,
        edges, mix, ends, came[0], came[1],
    )
    got = lax.all_to_all(chunk, "chan", 0, 0)
    q_shape, notes_shape = (2, out_strips, points, lanes), (9 + 6 * out_strips, 8, lanes)
    wide, second, notes = pl.pallas_call(
        second_outer_kernel,
        grid=(1,),
        out_shape=[
            jax.ShapeDtypeStruct((2, out_strips, folded_rows, lanes), f32),
            pltpu.HBM(q_shape, f32),
            pltpu.HBM(notes_shape, f32),
        ],
        in_specs=[in_one((2, 8, channels))] + [whole()] * 4,
        out_specs=[whole(), far(), far()],
        scratch_shapes=[pltpu.VMEM((2, points, channels), bf16)] * 2
        + [
            pltpu.VMEM(q_shape, f32),
            pltpu.VMEM((out_strips, points, lanes), f32),
            pltpu.VMEM(q_shape, f32),
            pltpu.VMEM(notes_shape, f32),
            pltpu.SemaphoreType.DMA((2,)),
        ],
        input_output_aliases={1: 0},
        compiler_params=pltpu.CompilerParams(vmem_limit_bytes=vmem_bytes),
    )(pltpu.with_memory_space_constraint(patch, pltpu.HBM), wide, outer_state, potential, mix)
    mine, ends = run(
        gather_kernel, gathered, (got, pltpu.with_memory_space_constraint(notes, pltpu.HBM)), [whole(), far()]
    )
    block_parts = block_product(got)
    mine, came = across_blocks(mine, block_parts)
    q_inner, q_ends, parts = run(
        last_kernel,
        [(2, rows), (2, 2, 8, channels), (count, lanes)],
        (
            *by_coupling, *block_parts, p_inner, mine, came[2], inner_coupling, surface_amp, group,
            wide, mix, ends, came[0], came[1], inner_state, second, notes,
        ),
        [scalars()] * 2 + [whole()] * 17,
        [pltpu.VMEM((2, 2, 24, channels), f32)],
    )
    parts = lax.all_to_all(parts.reshape(count, 1, lanes), both, 0, 0).reshape(count, lanes)
    steps = 4
    last_inner, last_outer, columns, poor = pl.pallas_call(
        lambda *refs: finish_kernel(entries, *refs),
        grid=(steps,),
        out_shape=[
            jax.ShapeDtypeStruct(shape, f32)
            for shape in ((2, rows), (2, points, channels), (2, TERMS, TERMS + 1), (1, lanes))
        ],
        in_specs=[whole()] * 8,
        out_specs=[
            pl.BlockSpec((2, rows), lambda step: (0, 0)),
            pl.BlockSpec((2, points // steps, channels), lambda step: (0, step, 0)),
            pl.BlockSpec((2, TERMS, TERMS + 1), lambda step: (0, 0, 0)),
            pl.BlockSpec((1, lanes), lambda step: (0, 0)),
        ],
        scratch_shapes=[pltpu.VMEM((5, 8, lanes), f32)],
        compiler_params=pltpu.CompilerParams(vmem_limit_bytes=vmem_bytes),
    )(parts, inner_state, p_inner, q_inner, outer_state, wide, second, q_ends)

    def again(state):
        last_inner, last_outer, hessenberg = step_by_step(*inputs)
        columns = hessenberg.transpose(0, 2, 1)
        (columns,) = run(same_kernel, [columns.shape], (columns,), [whole()])
        return jnp.zeros((), f32), last_inner, last_outer, columns

    _, last_inner, last_outer, columns = lax.while_loop(
        lambda state: state[0] > 0.0, again, (poor[0, 0], last_inner, last_outer, columns)
    )
    return last_inner, last_outer, columns.transpose(0, 2, 1)


def solution(mesh):
    return jax.shard_map(
        body,
        mesh=mesh,
        in_specs=(
            P(None, ("rad", "chan")),
            P(None, ("rad", "chan"), None),
            P("rad", None, "chan"),
            P("rad", None, None, "chan"),
            P("rad", None, "chan", None),
            P(("rad", "chan"), None),
            P(),
            P(),
            P(),
            P(),
        ),
        out_specs=(P(None, ("rad", "chan")), P(None, ("rad", "chan"), None), P()),
        check_vma=False,
    )
```

```python
import jax
import jax.numpy as jnp
from jax import lax
from jax.experimental import pallas as pl
from jax.experimental.pallas import tpu as pltpu
from jax.sharding import PartitionSpec as P

STRIP = 256
TERMS = 2

highest = lax.Precision.HIGHEST
kinetic_coef = -0.5 * 0.05 / (12.0 * 0.25 * 0.25)
slope_coef = 1.0 / (12.0 * 0.25)
bloch_coef = 2.0
shift = 1.5
least_left = 0.02
both = ("rad", "chan")


def spread(block, axis, holder):
    block = jnp.where(lax.axis_index(axis) == holder, block, jnp.zeros_like(block))
    return lax.psum(block, axis)


def local_parts(left, right):
    real_part = jnp.sum(left[0] * right[0]) + jnp.sum(left[1] * right[1])
    imag_part = jnp.sum(left[0][0] * right[0][1] - left[0][1] * right[0][0]) + jnp.sum(
        left[1][0] * right[1][1] - left[1][1] * right[1][0]
    )
    return jnp.stack([real_part, imag_part])


def rotate(vector, real_coef, imag_coef):
    return jnp.stack(
        [
            real_coef * vector[0] - imag_coef * vector[1],
            real_coef * vector[1] + imag_coef * vector[0],
        ]
    )


def neighbours(last_rows, first_rows):
    count = lax.axis_size(both)
    forward = [(i, i + 1) for i in range(count - 1)]
    backward = [(target, source) for source, target in forward]
    return lax.ppermute(last_rows, both, forward), lax.ppermute(first_rows, both, backward)


def outer_apply(extended, potential, laser_mix, moved):
    points = extended.shape[1] - 4
    far_left = extended[:, 0:points]
    near_left = extended[:, 1 : points + 1]
    centre_row = extended[:, 2 : points + 2]
    near_right = extended[:, 3 : points + 3]
    far_right = extended[:, 4 : points + 4]
    laplace = -far_left + 16.0 * near_left - 30.0 * centre_row + 16.0 * near_right - far_right
    slope_rows = slope_coef * (far_left - 8.0 * near_left + 8.0 * near_right - far_right)
    mixed_slope = jnp.einsum("prc,cd->prd", slope_rows, laser_mix, precision=highest)
    return (
        kinetic_coef * laplace
        + (potential - moved) * centre_row
        + jnp.stack([mixed_slope[1], -mixed_slope[0]])
    )


def inner_windows(shards, own_partners, own_offsets):
    windows = []
    for couple_index in range(own_partners.shape[0]):
        source = lax.dynamic_index_in_dim(shards, own_partners[couple_index], 0, keepdims=False)
        source = source.transpose(1, 0, 2).reshape(2, -1)
        band_width = source.shape[1] // 2
        windows.append(
            lax.dynamic_slice_in_dim(source, own_offsets[couple_index] + band_width, band_width, 1)
        )
    return windows


def exchange(inner_vec, ghost_part, row):
    rows = inner_vec.shape[1]
    blocks, strips = lax.axis_size("rad"), lax.axis_size("chan")
    chunk = jnp.concatenate(
        [
            inner_vec,
            ghost_part.reshape(-1, rows),
            row.reshape(-1, rows),
            jnp.zeros((2, rows), jnp.float32),
        ],
        axis=0,
    )
    got = lax.all_to_all(jnp.broadcast_to(chunk, (strips,) + chunk.shape), "chan", 0, 0)
    own = got[:, 0:2]
    ghost_sum = jnp.sum(got[:, 2:10], axis=0)
    padded = jnp.pad(own, ((2, 1), (0, 0), (0, 0)))
    near = lax.dynamic_slice_in_dim(padded, lax.axis_index("chan"), 4, 0)
    chunk = jnp.concatenate(
        [near.reshape(8, rows), ghost_sum, got[0, 10:14], jnp.zeros((4, rows), jnp.float32)],
        axis=0,
    )
    got_blocks = lax.all_to_all(jnp.broadcast_to(chunk, (blocks,) + chunk.shape), "rad", 0, 0)
    shards = got_blocks[:, 0:8].reshape(blocks, 4, 2, rows)
    ghost = jnp.sum(got_blocks[:, 8:16], axis=0).reshape(2, 2, -1)
    first_row = got_blocks[0, 16:20].reshape(2, -1)
    return own.transpose(1, 0, 2).reshape(2, -1), shards, ghost, first_row


def step_by_step(
    inner_state,
    outer_state,
    inner_ham,
    inner_coupling,
    surface_amp,
    potential,
    laser_mix,
    partners,
    band_offsets,
    channel_group,
):
    block_order = inner_ham.shape[1]
    points, channels = outer_state.shape[1:]
    entries = float(
        lax.axis_size("rad") * block_order + lax.axis_size(both) * points * channels
    )
    block_index = lax.axis_index("rad")
    is_first = lax.axis_index(both) == 0
    member = (channel_group == block_index).astype(jnp.float32)
    masked_amp = surface_amp[0] * member[None, None, :]
    own_partners = lax.dynamic_index_in_dim(partners, block_index, 0, keepdims=False)
    own_offsets = lax.dynamic_index_in_dim(band_offsets, block_index, 0, keepdims=False)

    def total(value):
        return lax.psum(value, both) / entries

    def squares(vector):
        return jnp.sum(vector[0] * vector[0]) + jnp.sum(vector[1] * vector[1])

    start_len = jnp.sqrt(total(squares((inner_state, outer_state))))
    krylov = [(inner_state / start_len, outer_state / start_len)]
    hessenberg = jnp.zeros((2, TERMS + 1, TERMS), jnp.float32)
    for term_index in range(TERMS):
        inner_vec, outer_vec = krylov[term_index]
        ghost_part = jnp.einsum("pk,mki->pmi", inner_vec, masked_amp, precision=highest)
        row = jnp.where(is_first, outer_vec[:, 0], 0.0)
        own_vec, shards, ghost, first_row = exchange(inner_vec, ghost_part, row)
        result_in = jnp.dot(own_vec, inner_ham[0], precision=highest)
        for couple_index, window in enumerate(inner_windows(shards, own_partners, own_offsets)):
            result_in = result_in + jnp.dot(window, inner_coupling[0, couple_index], precision=highest)
        result_in = result_in + bloch_coef * jnp.einsum(
            "pi,ki->pk", first_row, masked_amp[0], precision=highest
        )
        low, high = neighbours(outer_vec[:, points - 2 :], outer_vec[:, :2])
        low = jnp.where(is_first, ghost[:, ::-1], low)
        extended = jnp.concatenate([low, outer_vec, high], axis=1)
        image = (result_in, outer_apply(extended, potential, laser_mix, 0.0))
        for prior_index in range(term_index + 1):
            prior = krylov[prior_index]
            coefs = total(local_parts(prior, image))
            image = tuple(
                part - rotate(prior_part, coefs[0], coefs[1])
                for part, prior_part in zip(image, prior)
            )
            hessenberg = hessenberg.at[:, prior_index, term_index].set(coefs)
        new_length = jnp.sqrt(total(squares(image)))
        hessenberg = hessenberg.at[0, term_index + 1, term_index].set(new_length)
        krylov.append((image[0] / new_length, image[1] / new_length))
    return (krylov[-1][0], krylov[-1][1], hessenberg)


lanes = 128
margin = 8
reach = 2
vmem_bytes = 16 * 2**20


def whole():
    return pl.BlockSpec(memory_space=pltpu.VMEM)


def anywhere():
    return pl.BlockSpec(memory_space=pl.ANY)


def far():
    return pl.BlockSpec(memory_space=pltpu.HBM)


def in_one(shape):
    return pl.BlockSpec(shape, lambda i: (0,) * len(shape))


def scalars():
    return pl.BlockSpec(memory_space=pltpu.SMEM)


def run(kernel, outs, args, in_specs, scratch=()):
    return pl.pallas_call(
        kernel,
        out_shape=[jax.ShapeDtypeStruct(*out) if isinstance(out[0], tuple) else jax.ShapeDtypeStruct(out, jnp.float32) for out in outs],
        in_specs=in_specs,
        out_specs=[whole()] * len(outs),
        scratch_shapes=list(scratch),
        compiler_params=pltpu.CompilerParams(vmem_limit_bytes=vmem_bytes),
    )(*args)


def two(x):
    high = x.astype(jnp.bfloat16)
    return high, (x - high.astype(jnp.float32)).astype(jnp.bfloat16)


def both_halves(x):
    high, low = two(x)
    rest = jnp.zeros((16 - 2 * x.shape[0], x.shape[1]), jnp.float32)
    return jnp.concatenate([high.astype(jnp.float32), low.astype(jnp.float32), rest], axis=0).astype(jnp.bfloat16)


def few_rows_dot(x, weights, flipped=False):
    rows = x.shape[0]
    lhs = both_halves(x)
    dims = (((1,), (1 if flipped else 0,)), ((), ()))
    total = sum(lax.dot_general(lhs, part, dims, preferred_element_type=jnp.float32) for part in weights)
    return total[:rows] + total[rows : 2 * rows]


def mixed_with(high, low, mix_ref):
    count = high.shape[0]
    first = jnp.dot(jnp.concatenate([high, low], axis=0), mix_ref[0], preferred_element_type=jnp.float32)
    return first[:count] + first[count:] + jnp.dot(high, mix_ref[1], preferred_element_type=jnp.float32)


def write_chunk(out_ref, inner_vec, ghosts, row, held_ref=None, written=None):
    half = inner_vec.shape[1]
    chunk = jnp.concatenate(
        [
            ghosts[:, :half],
            ghosts[:, half:],
            inner_vec,
            row[:, :half],
            row[:, half:],
            jnp.zeros((2, half), jnp.float32),
        ],
        axis=0,
    )
    if held_ref is None:
        for strip in range(out_ref.shape[0]):
            out_ref[strip, 0:16] = chunk
        return []
    held_ref[...] = chunk
    copies = [
        pltpu.make_async_copy(held_ref, out_ref.at[strip, pl.ds(0, 16)], written.at[strip])
        for strip in range(out_ref.shape[0])
    ]
    for copy in copies:
        copy.start()
    return copies


def ghost_rows(inner_vec, amps, member):
    return jnp.concatenate([few_rows_dot(inner_vec, amp) * member for amp in amps], axis=0)


def member_of(group_ref):
    return jnp.where(group_ref[...] == lax.axis_index("rad"), 1.0, 0.0)


def at_first():
    return (lax.axis_index("rad") == 0) & (lax.axis_index("chan") == 0)


def at_last():
    last = [lax.axis_index(axis) == lax.axis_size(axis) - 1 for axis in both]
    return last[0] & last[1]


def send_ends(out_ref, first_rows, last_rows, held_ref=None, written=None):
    strips, _, half = out_ref.shape
    copies = []
    for end, (there, points) in enumerate(((1, last_rows), (strips - 1, first_rows))):
        both_parts = jnp.concatenate(points, axis=0)
        rows = jnp.concatenate([both_parts[:, :half], both_parts[:, half:]], axis=0)
        strip = lax.rem(lax.axis_index("chan") + there, strips)
        if held_ref is None:
            out_ref[strip, 16:24] = rows
        else:
            held_ref[end] = rows
            copies.append(pltpu.make_async_copy(held_ref.at[end], out_ref.at[strip, pl.ds(16, 8)], written.at[end]))
            copies[-1].start()
    return copies


def start_kernel(inner_ref, head_ref, tail_ref, amp_ref, group_ref, chunk_ref):
    send_ends(chunk_ref, [head_ref[part, 0:2] for part in range(2)], [tail_ref[part, 6:8] for part in range(2)])
    row = jnp.concatenate([head_ref[part, 0:1] for part in range(2)], axis=0)
    row = jnp.where(at_first(), row, 0.0)
    inner_vec = inner_ref[...]
    amps = [two(amp_ref[0, radius]) for radius in range(2)]
    ghosts = ghost_rows(inner_vec, amps, member_of(group_ref))
    write_chunk(chunk_ref, inner_vec, ghosts, row)


def stencils(window, pot):
    before_2, before_1, here, after_1, after_2 = window
    local = (pot - (30.0 * kinetic_coef + shift)) * here + (
        16.0 * kinetic_coef * (before_1 + after_1) - kinetic_coef * (before_2 + after_2)
    )
    return local, (before_2 - after_2) + 8.0 * (after_1 - before_1)


def first_outer_kernel(
    state_ref, pot_ref, mix_ref, out_ref, mix_out, edges_ref, wide_ref, pot_wide, slope_h, slope_l
):
    points, channels = state_ref.shape[1:]
    strips = channels // lanes
    length = points // 8
    for strip in range(strips):
        here = slice(strip * lanes, (strip + 1) * lanes)
        for part in range(3):
            source = pot_ref if part == 2 else state_ref.at[part]
            target = pot_wide.at[strip] if part == 2 else wide_ref.at[part, strip]
            target[margin : margin + points] = source[:, here]
            target[0:margin] = jnp.zeros((margin, lanes), jnp.float32)
            target[margin + points :] = jnp.zeros((margin, lanes), jnp.float32)
    for part in range(3):
        source = pot_ref if part == 2 else state_ref.at[part]
        edges_ref[0, part], edges_ref[1, part] = source[0:8], source[points - 8 : points]

    def strip_step(step, _):
        part, strip = lax.div(step, strips), lax.rem(step, strips)

        def load(place):
            return wide_ref[part, strip, pl.ds(margin + place, 8, stride=length)]

        window = [load(place) for place in range(-2 * reach, 0)]
        columns = pl.ds(pl.multiple_of(strip * lanes, lanes), lanes)
        for first in range(-reach, length + reach, 2):
            slopes = []
            for place in (first, first + 1):
                window.append(load(place + reach))
                local, slope = stencils(window, pot_wide[strip, pl.ds(margin + place, 8, stride=length)])
                out_ref[part, strip, (place + reach) * 8 : (place + reach + 1) * 8] = local
                slopes.append(slope)
                window.pop(0)
            rows = slice((first + reach) * 8, (first + reach + 2) * 8)
            slope_h[part, rows, columns], slope_l[part, rows, columns] = two(jnp.concatenate(slopes, axis=0))
        return 0

    lax.fori_loop(0, 2 * strips, strip_step, 0)
    mix_out[0], mix_out[1] = two(slope_coef * mix_ref[...])
    add_mixed(out_ref, slope_h, slope_l, mix_out)


def add_mixed(out_ref, slope_h, slope_l, mix_ref):
    for part in range(2):
        mixed = mixed_with(slope_h[1 - part], slope_l[1 - part], mix_ref)
        for strip in range(out_ref.shape[1]):
            own = mixed[:, strip * lanes : (strip + 1) * lanes]
            out_ref[part, strip] = out_ref[part, strip] + (own if part == 0 else -own)


def products(s, p, q):
    return [
        s[0] * s[0] + s[1] * s[1],
        s[0] * p[0] + s[1] * p[1],
        s[0] * p[1] - s[1] * p[0],
        s[0] * q[0] + s[1] * q[1],
        s[0] * q[1] - s[1] * q[0],
        p[0] * p[0] + p[1] * p[1],
        p[0] * q[0] + p[1] * q[1],
        p[0] * q[1] - p[1] * q[0],
        q[0] * q[0] + q[1] * q[1],
    ]


def second_outer_kernel(
    patch_ref, wide_in, state_in, pot_in, mix_ref,
    wide_ref, q_out, notes_out, slope_h, slope_l, state_ref, pot_ref, out_ref, notes_ref, written,
):
    strips, places = out_ref.shape[1:3]
    length = places // 8
    for part in range(2):
        for strip in range(strips):
            here = slice(strip * lanes, (strip + 1) * lanes)
            wide_ref[part, strip, pl.ds(reach * 8, 2, stride=8)] = patch_ref[part, 0:2, here]
            wide_ref[part, strip, pl.ds(length * 8 + 7, 2, stride=8)] = patch_ref[part, 2:4, here]
    for strip in range(strips):
        here = slice(strip * lanes, (strip + 1) * lanes)
        pot_ref[strip] = pot_in[:, here]
        for part in range(2):
            state_ref[part, strip] = state_in[part, :, here]

    def strip_step(step, _):
        part, strip = lax.div(step, strips), lax.rem(step, strips)

        def load(place):
            return wide_ref[part, strip, (place + reach) * 8 : (place + reach + 1) * 8]

        window = [load(place) for place in range(-reach, reach)]
        columns = pl.ds(pl.multiple_of(strip * lanes, lanes), lanes)
        for first in range(0, length, 2):
            slopes = []
            for place in (first, first + 1):
                window.append(load(place + reach))
                local, slope = stencils(window, pot_ref[strip, pl.ds(place, 8, stride=length)])
                out_ref[part, strip, place * 8 : (place + 1) * 8] = local
                slopes.append(slope)
                window.pop(0)
            rows = slice(first * 8, (first + 2) * 8)
            slope_h[part, rows, columns], slope_l[part, rows, columns] = two(jnp.concatenate(slopes, axis=0))
        return 0

    lax.fori_loop(0, 2 * strips, strip_step, 0)
    add_mixed(out_ref, slope_h, slope_l, mix_ref)
    copy = pltpu.make_async_copy(out_ref, q_out, written.at[0])
    copy.start()
    run_of = lax.broadcasted_iota(jnp.int32, (8, lanes), 0)

    def gram_step(strip, sums):
        for place in range(length):
            entries = products(
                [state_ref[part, strip, pl.ds(place, 8, stride=length)] for part in range(2)],
                [wide_ref[part, strip, (place + reach) * 8 : (place + reach + 1) * 8] for part in range(2)],
                [out_ref[part, strip, place * 8 : (place + 1) * 8] for part in range(2)],
            )
            if place < 4 or place >= length - 4:
                inside = run_of > 0 if place < 4 else run_of < 7
                entries = [jnp.where(inside, entry, 0.0) for entry in entries]
            sums = [total + entry for total, entry in zip(sums, entries)]
        return sums

    sums = lax.fori_loop(0, strips, gram_step, [jnp.zeros((8, lanes), jnp.float32)] * 9)
    for k in range(9):
        notes_ref[k] = sums[k]
    for strip in range(strips):
        here = slice(strip * lanes, (strip + 1) * lanes)
        for end, rows in enumerate((slice(0, 8), slice(places - 8, places))):
            notes_ref[9 + strips * 3 * end + strip] = pot_in[rows, here]
            for part in range(2):
                notes_ref[9 + strips * (3 * end + part + 1) + strip] = state_in[part, rows, here]
    notes_copy = pltpu.make_async_copy(notes_ref, notes_out, written.at[1])
    notes_copy.start()
    copy.wait()
    notes_copy.wait()


def block_kernel(first, got_ref, ham_ref, out_ref, held_ref, arrived):
    rows = ham_ref.shape[2]
    pieces, size = held_ref.shape[:2]
    copies = [
        pltpu.make_async_copy(ham_ref.at[0, pl.ds((first + k) * size, size)], held_ref.at[k], arrived.at[k])
        for k in range(pieces)
    ]
    for copy in copies:
        copy.start()
    total = jnp.zeros((16, rows), jnp.float32)
    for k, copy in enumerate(copies):
        copy.wait()
        for part in range(size // rows):
            lhs = both_halves(got_ref[(first + k) * (size // rows) + part, 8:10])
            for weights in two(held_ref[k, part * rows : (part + 1) * rows]):
                total = total + jnp.dot(lhs, weights, preferred_element_type=jnp.float32)
    out_ref[...] = total[0:2] + total[2:4]


def chip_index():
    return lax.div(lax.axis_index("rad"), 2)


def core_index():
    return lax.rem(lax.axis_index("rad"), 2)


def gather_kernel(got_ref, after_ref, out_ref, kept_ref, ends_ref):
    strips = got_ref.shape[0]
    own = lax.axis_index("chan")
    for k in range(4):
        strip = own + (k - 2)
        there = (strip >= 0) & (strip < strips)
        near = got_ref[jnp.clip(strip, 0, strips - 1), 8:10]
        out_ref[2 * k : 2 * k + 2] = jnp.where(there, near, 0.0)
    kept_ref[0:8] = sum(got_ref[strip, 0:8] for strip in range(strips))
    kept_ref[8:12] = got_ref[0, 10:14]
    kept_ref[12:16] = jnp.zeros((4, got_ref.shape[2]), jnp.float32)
    out_ref[8:16] = jnp.where(chip_index() == 0, kept_ref[8:16], kept_ref[0:8])
    before = got_ref[lax.rem(own + strips - 1, strips), 16:24]
    after = got_ref[lax.rem(own + 1, strips), 16:24]
    ends_ref[0], ends_ref[1] = before, after
    out_ref[16:24] = jnp.where(own == 0, before, after)


def joined(kept_ref, came, add_ghosts, take_row):
    ghosts = kept_ref[0:8] + jnp.where(add_ghosts, came, 0.0)
    return ghosts, jnp.where(take_row, came, kept_ref[8:16])


def join_kernel(mine_ref, other_ref, kept_ref, after_ref, out_ref, kept_out):
    chip = chip_index()
    out_ref[0:8], out_ref[8:16] = mine_ref[0:8], other_ref[0:8]
    ghosts, row = joined(kept_ref, other_ref[8:16], (chip == 0) | (chip == 3), chip == 1)
    kept_out[0:8], kept_out[8:16] = ghosts, row
    out_ref[16:24] = jnp.where(chip <= 1, row, ghosts)
    out_ref[24:32] = mine_ref[16:24]


def last_join_kernel(mine_ref, other_ref, kept_ref, near_ref, after_ref, out_ref, kept_out):
    chip, core = chip_index(), core_index()
    out_ref[0:16], out_ref[16:32] = mine_ref[0:16], other_ref[0:16]
    ghosts, row = joined(kept_ref, other_ref[16:24], chip == 0, chip >= 2)
    kept_out[0:8], kept_out[8:16] = ghosts, row
    out_ref[32:40] = jnp.where(core == 0, row, ghosts)
    is_low = lax.axis_index("chan") == 0
    from_own = (core == 0) == is_low
    from_near = (lax.rem(chip, 2) == 1) == is_low
    out_ref[40:48] = jnp.where(from_own, mine_ref[24:32], jnp.where(from_near, near_ref[16:24], other_ref[24:32]))


def join(kernel, count, *args):
    width = args[0].shape[1]
    return run(kernel, [(count, width), (16, width)], args, [whole()] * (len(args) - 1) + [anywhere()])


def inner_result(partners_ref, offsets_ref, block_a, block_b, inner_ref, mine_ref, other_ref, coupling_ref, amp_ref, member, row):
    result = block_a[...] + block_b[...] - shift * inner_ref[...]
    couplings, band_width = coupling_ref.shape[1:3]
    block_index = lax.axis_index("rad")
    for couple_index in range(couplings):
        apart = partners_ref[couple_index, block_index] ^ block_index
        far_pair = lax.shift_right_logical(apart, 2)
        slot = 4 * (apart & 1) + lax.shift_right_logical(apart ^ (2 * far_pair), 1)
        rows = pl.ds(pl.multiple_of(lax.rem(slot, 4) * 8, 8), 8)
        near = jnp.where(slot < 4, mine_ref[rows], other_ref[rows])
        near = jnp.concatenate([near[2 * k : 2 * k + 2] for k in range(4)], axis=1)
        near = jnp.concatenate([near, jnp.zeros((6, near.shape[1]), jnp.float32)], axis=0)
        first = offsets_ref[couple_index, block_index] + band_width
        window = pltpu.roll(near, near.shape[1] - first, 1)[0:2, :band_width]
        result = result + few_rows_dot(window, two(coupling_ref[0, couple_index]))
    return result + bloch_coef * few_rows_dot(row * member, two(amp_ref[0, 0]), flipped=True)


def unpacked(kept_ref, other_ref):
    ghosts, row = joined(kept_ref, other_ref[32:40], True, core_index() == 1)
    return jnp.concatenate([ghosts[0:4], ghosts[4:8]], axis=1), jnp.concatenate([row[0:2], row[2:4]], axis=1)


def points_of(ref, part, first, count, run_index=0):
    return jnp.concatenate(
        [ref[part, strip, pl.ds(first * 8 + run_index, count, stride=8)] for strip in range(ref.shape[1])], axis=1
    )


def mend(edge_ref, pots, mix_ref, more=None):
    local, slopes = [], []
    for part in range(2):
        for end in range(2):
            inner, slope = stencils([edge_ref[part, end, 8 + k : 16 + k] for k in range(-reach, reach + 1)], pots[end])
            local.append(inner)
            slopes.append(slope)
    mixed = mixed_with(*two(jnp.concatenate(slopes + ([] if more is None else [more]), axis=0)), mix_ref)
    image = [
        [
            local[2 * part + end] + (mixed[16 + 8 * end : 24 + 8 * end] if part == 0 else -mixed[8 * end : 8 * end + 8])
            for end in range(2)
        ]
        for part in range(2)
    ]
    return image, mixed[32:]


def pick_ends(ends_ref, other_ref):
    strip = lax.axis_index("chan")
    is_low, is_high = strip == 0, strip == lax.axis_size("chan") - 1
    came = other_ref[40:48]
    before = jnp.where(at_first(), 0.0, jnp.where(is_low, came, ends_ref[0]))
    after = jnp.where(at_last(), 0.0, jnp.where(is_high, came, ends_ref[1]))
    return [
        [jnp.concatenate([x[2 * part : 2 * part + 2], x[4 + 2 * part : 6 + 2 * part]], axis=1) for part in range(2)]
        for x in (before, after)
    ]


def between_kernel(
    partners_ref, offsets_ref, block_a, block_b, inner_ref, mine_ref, other_ref, coupling_ref, amp_ref, group_ref,
    edges_ref, mix_ref, ends_ref, kept_ref,
    image_ref, chunk_ref, patch_out, held_ref, written, ends_held, ends_written, patch_ref, patch_written, edge_ref,
):
    member = member_of(group_ref)
    ghosts, row = unpacked(kept_ref, other_ref)
    before, after = pick_ends(ends_ref, other_ref)
    edge_ref[...] = jnp.zeros_like(edge_ref)
    for part in range(2):
        edge_ref[part, 0, 6:8] = before[part]
        edge_ref[part, 1, 16:18] = after[part]
        for end in range(2):
            edge_ref[part, end, 8:16] = edges_ref[end, part]
    near, far_off = ghosts[0:2], ghosts[2:4]
    kinetic = [kinetic_coef * (16.0 * near - far_off), -kinetic_coef * near]
    slope = jnp.concatenate([far_off - 8.0 * near, near, jnp.zeros((12, near.shape[1]), jnp.float32)], axis=0)
    p, mixed = mend(edge_ref, [edges_ref[end, 2] for end in range(2)], mix_ref, slope)
    first_rows, last_rows = [], []
    for part in range(2):
        extra = jnp.concatenate(
            [
                kinetic[k][part : part + 1]
                + (mixed[2 * k + 1 : 2 * k + 2] if part == 0 else -mixed[2 * k : 2 * k + 1])
                for k in range(2)
            ],
            axis=0,
        )
        first_rows.append(p[part][0][0:2] + jnp.where(at_first(), extra, 0.0))
        last_rows.append(p[part][1][6:8])
        patch_ref[part] = jnp.concatenate(
            [first_rows[part], last_rows[part], jnp.zeros((4, near.shape[1]), jnp.float32)], axis=0
        )
    copy = pltpu.make_async_copy(patch_ref, patch_out, patch_written)
    copy.start()
    copies = [copy] + send_ends(chunk_ref, first_rows, last_rows, ends_held, ends_written)
    image = inner_result(
        partners_ref, offsets_ref, block_a, block_b, inner_ref, mine_ref, other_ref, coupling_ref, amp_ref, member, row
    )
    image_ref[...] = image
    row = jnp.where(at_first(), jnp.concatenate([rows[0:1] for rows in first_rows], axis=0), 0.0)
    amps = [two(amp_ref[0, radius]) for radius in range(2)]
    copies += write_chunk(chunk_ref, image, ghost_rows(image, amps, member), row, held_ref, written)
    for copy in copies:
        copy.wait()


def last_kernel(
    partners_ref, offsets_ref, block_a, block_b, inner_ref, mine_ref, other_ref, coupling_ref, amp_ref, group_ref,
    wide_ref, mix_ref, ends_ref, kept_ref, start_ref, second_ref, notes_ref,
    image_ref, out_ref, parts_ref, edge_ref,
):
    member = member_of(group_ref)
    ghosts, row = unpacked(kept_ref, other_ref)
    image = inner_result(
        partners_ref, offsets_ref, block_a, block_b, inner_ref, mine_ref, other_ref, coupling_ref, amp_ref, member, row
    )
    image_ref[...] = image
    strips = wide_ref.shape[1]
    length = second_ref.shape[2] // 8
    noted = [
        [
            jnp.concatenate([notes_ref[9 + strips * (3 * end + k) + strip] for strip in range(strips)], axis=1)
            for k in range(3)
        ]
        for end in range(2)
    ]
    before, after = pick_ends(ends_ref, other_ref)
    edge_ref[...] = jnp.zeros_like(edge_ref)
    for part in range(2):
        ghost = jnp.concatenate([ghosts[2 + part : 3 + part], ghosts[part : part + 1]], axis=0)
        edge_ref[part, 0, 6:8] = jnp.where(at_first(), ghost, before[part])
        edge_ref[part, 0, 8:24] = points_of(wide_ref, part, reach, 16)
        edge_ref[part, 1, 0:16] = points_of(wide_ref, part, length + reach - 16, 16, 7)
        edge_ref[part, 1, 16:18] = after[part]
    q, _ = mend(edge_ref, [noted[end][0] for end in range(2)], mix_ref)
    row_of = lax.broadcasted_iota(jnp.int32, q[0][0].shape, 0)
    mended = [row_of < 4, row_of >= 4]
    totals = [notes_ref[k] for k in range(9)]
    for end in range(2):
        for part in range(2):
            there = points_of(second_ref, part, 0 if end == 0 else length - 8, 8, 7 * end)
            q[part][end] = jnp.where(mended[end], q[part][end], there)
            out_ref[end, part] = q[part][end]
        entries = products(noted[end][1:], [edge_ref[part, end, 8:16] for part in range(2)], [q[part][end] for part in range(2)])
        for k, entry in enumerate(entries):
            entry = jnp.where(mended[end], entry, 0.0)
            totals[k] = totals[k] + sum(entry[:, strip * lanes : (strip + 1) * lanes] for strip in range(strips))
    start, inner = start_ref[...], inner_ref[...]
    inside = products([start[0:1], start[1:2]], [inner[0:1], inner[1:2]], [image[0:1], image[1:2]])
    lane = lax.broadcasted_iota(jnp.int32, (1, lanes), 1)
    sums = jnp.zeros((1, lanes), jnp.float32)
    for k in range(9):
        line = jnp.sum(totals[k], axis=0, keepdims=True) + inside[k][:, :lanes] + inside[k][:, lanes:]
        sums = jnp.where(lane == k, jnp.sum(line, axis=1, keepdims=True), sums)
    parts_ref[...] = jnp.broadcast_to(sums, parts_ref.shape)


def arnoldi_coefs(gram):
    ss, spr, spi, sqr, sqi, pp, pqr, pqi, qq = gram
    cr, ci = spr / ss, spi / ss
    left_1 = pp - (spr * cr + spi * ci)
    h10 = jnp.sqrt(left_1 / ss)
    sxr = sqr - (cr * spr - ci * spi)
    sxi = sqi - (cr * spi + ci * spr)
    h01r, h01i = sxr / (ss * h10), sxi / (ss * h10)
    pxr, pxi = pqr - cr * pp, pqi - ci * pp
    yxr = pxr - (cr * sxr + ci * sxi)
    yxi = pxi - (cr * sxi - ci * sxr)
    scale = 1.0 / left_1
    h11r, h11i = yxr * scale, yxi * scale
    xx = (qq - 2.0 * (cr * pqr + ci * pqi) + (cr * cr + ci * ci) * pp) * scale
    left_2 = xx - (h01r * h01r + h01i * h01i) - (h11r * h11r + h11i * h11i)
    h21 = jnp.sqrt(left_2)
    fine = (left_1 > least_left * pp) & (left_2 > least_left * xx)
    poor = jnp.where(fine, 0.0, 1.0)
    zero = jnp.zeros_like(ss)
    entries = [[[cr + shift, h10, zero], [h01r, h11r + shift, h21]], [[ci, zero, zero], [h01i, h11i, zero]]]
    a = jnp.sqrt(ss)
    coef_q = 1.0 / (a * h10 * h21)
    coef_p = (-(cr + h11r) * coef_q, -(ci + h11i) * coef_q)
    coef_s = (
        (h11r * cr - h11i * ci) * coef_q - h01r / (a * h21),
        (h11r * ci + h11i * cr) * coef_q - h01i / (a * h21),
    )
    return entries, (coef_q, coef_p, coef_s), poor


def combined(coefs, s, p, q):
    coef_q, coef_p, coef_s = coefs
    return (
        coef_q * q[0] + coef_p[0] * p[0] - coef_p[1] * p[1] + coef_s[0] * s[0] - coef_s[1] * s[1],
        coef_q * q[1] + coef_p[0] * p[1] + coef_p[1] * p[0] + coef_s[0] * s[1] + coef_s[1] * s[0],
    )


def finish_kernel(
    entries, parts_ref, start_ref, inner_ref, image_ref, state_ref, wide_ref, second_ref, edge_ref,
    inner_out, result_out, hess_out, poor_out, outer_out, written,
):
    strips, places = second_ref.shape[1:3]
    length = places // 8
    sums = jnp.sum(parts_ref[...], axis=0, keepdims=True) * (1.0 / entries)
    lane = lax.broadcasted_iota(jnp.int32, sums.shape, 1)
    gram = [jnp.sum(jnp.where(lane == k, sums, 0.0), axis=1, keepdims=True) for k in range(9)]
    values, (coef_q, coef_p, coef_s), poor = arnoldi_coefs(gram)
    tile = lambda coef: jnp.broadcast_to(coef, (8, lanes))
    coefs = tile(coef_q), [tile(coef) for coef in coef_p], [tile(coef) for coef in coef_s]

    def put(rows, p_first, q_first, run_index, edge=None):
        for strip in range(strips):
            here = slice(strip * lanes, (strip + 1) * lanes)
            result = combined(
                coefs,
                [state_ref[part, rows, here] for part in range(2)],
                [wide_ref[part, strip, pl.ds(p_first * 8 + run_index, 8, stride=8)] for part in range(2)],
                [
                    second_ref[part, strip, pl.ds(q_first * 8 + run_index, 8, stride=8)]
                    if edge is None
                    else edge_ref[edge, part, :, here]
                    for part in range(2)
                ],
            )
            for part in range(2):
                outer_out[part, rows, here] = result[part]

    copies = []
    for run_index in range(8):
        for first in range(0, length, 8):
            row = run_index * length + first
            edge = 0 if row == 0 else 1 if row == places - 8 else None
            put(slice(row, row + 8), first + reach, first, run_index, edge)
        rows = pl.ds(run_index * length, length)
        copies.append(
            pltpu.make_async_copy(outer_out.at[:, rows], result_out.at[:, rows], written.at[run_index])
        )
        copies[-1].start()
    for first in range(0, inner_out.shape[1], lanes):
        here = slice(first, first + lanes)
        result = combined(
            [coefs[0][0:1], [c[0:1] for c in coefs[1]], [c[0:1] for c in coefs[2]]],
            *[[ref[0:1, here], ref[1:2, here]] for ref in (start_ref, inner_ref, image_ref)],
        )
        for part in range(2):
            inner_out[part : part + 1, here] = result[part]
    lane = lax.broadcasted_iota(jnp.int32, (1, TERMS + 1), 1)
    for part in range(2):
        for column in range(TERMS):
            line = jnp.zeros((1, TERMS + 1), jnp.float32)
            for k, value in enumerate(values[part][column]):
                line = jnp.where(lane == k, value, line)
            hess_out[part, column : column + 1] = line
    poor_out[...] = jnp.broadcast_to(poor, poor_out.shape)
    for copy in copies:
        copy.wait()


def same_kernel(in_ref, out_ref):
    out_ref[...] = in_ref[...]


def across_blocks(mine, kept, after):
    blocks = lax.axis_size("rad")
    last = blocks // 2 - 1
    near = lax.ppermute(mine, "rad", [(i, i ^ 2) for i in range(blocks)])
    mine, kept = join(join_kernel, 32, mine, near, kept, after[0])
    other = lax.ppermute(mine, "rad", [(i, 2 * (last - i // 2) + i % 2) for i in range(blocks)])
    mine, kept = join(last_join_kernel, 48, mine, other, kept, near, after[1])
    return mine, lax.ppermute(mine, "rad", [(i, i ^ 1) for i in range(blocks)]), kept


def body(*inputs):
    (
        inner_state,
        outer_state,
        inner_ham,
        inner_coupling,
        surface_amp,
        potential,
        laser_mix,
        partners,
        band_offsets,
        channel_group,
    ) = inputs
    block_order, rows = inner_ham.shape[1:]
    points, channels = outer_state.shape[1:]
    count = lax.axis_size(both)
    blocks, strips = lax.axis_size("rad"), lax.axis_size("chan")
    entries = float(blocks * block_order + count * points * channels)
    group = channel_group.reshape(1, channels)
    by_coupling = partners.T, band_offsets.T
    f32, bf16 = jnp.float32, jnp.bfloat16
    out_strips = channels // lanes
    folded_rows = points + 2 * reach * 8

    chunk = pl.pallas_call(
        start_kernel,
        grid=(1,),
        out_shape=jax.ShapeDtypeStruct((strips, 24, rows), f32),
        in_specs=[
            whole(),
            in_one((2, 8, channels)),
            pl.BlockSpec((2, 8, channels), lambda i: (0, points // 8 - 1, 0)),
            whole(),
            whole(),
        ],
        out_specs=whole(),
        compiler_params=pltpu.CompilerParams(vmem_limit_bytes=vmem_bytes),
    )(inner_state, outer_state, outer_state, surface_amp, group)
    got = lax.all_to_all(chunk, "chan", 0, 0)
    wide, mix, edges = pl.pallas_call(
        first_outer_kernel,
        out_shape=[
            jax.ShapeDtypeStruct((2, out_strips, folded_rows, lanes), f32),
            jax.ShapeDtypeStruct((2, channels, channels), bf16),
            jax.ShapeDtypeStruct((2, 3, 8, channels), f32),
        ],
        in_specs=[whole()] * 3,
        out_specs=[whole()] * 3,
        scratch_shapes=[
            pltpu.VMEM((2, out_strips, points + 2 * margin, lanes), f32),
            pltpu.VMEM((out_strips, points + 2 * margin, lanes), f32),
            pltpu.VMEM((2, folded_rows, channels), bf16),
            pltpu.VMEM((2, folded_rows, channels), bf16),
        ],
        compiler_params=pltpu.CompilerParams(vmem_limit_bytes=vmem_bytes),
    )(outer_state, potential, laser_mix)

    def block_product(got):
        size = 2 * rows
        parts = []
        for first, last in ((0, 4), (4, 8)):
            parts += run(
                lambda *refs, first=first: block_kernel(first, *refs),
                [(2, rows)],
                (got, pltpu.with_memory_space_constraint(inner_ham, pltpu.HBM)),
                [whole(), far()],
                [pltpu.VMEM((last - first, size, rows), f32), pltpu.SemaphoreType.DMA((last - first,))],
            )
        return parts

    gathered = [(24, rows), (16, rows), (2, 8, rows)]
    mine, kept, ends = run(gather_kernel, gathered, (got, wide), [whole(), anywhere()])
    block_parts = block_product(got)
    mine, other, kept = across_blocks(mine, kept, block_parts)
    p_inner, chunk, patch = pl.pallas_call(
        between_kernel,
        out_shape=[
            jax.ShapeDtypeStruct((2, rows), f32),
            pltpu.HBM((strips, 24, rows), f32),
            pltpu.HBM((2, 8, channels), f32),
        ],
        in_specs=[scalars()] * 2 + [whole()] * 12,
        out_specs=[whole()] + [far()] * 2,
        scratch_shapes=[
            pltpu.VMEM((16, rows), f32),
            pltpu.SemaphoreType.DMA((strips,)),
            pltpu.VMEM((2, 8, rows), f32),
            pltpu.SemaphoreType.DMA((2,)),
        ]
        + [pltpu.VMEM((2, 8, channels), f32), pltpu.SemaphoreType.DMA, pltpu.VMEM((2, 2, 24, channels), f32)],
        compiler_params=pltpu.CompilerParams(vmem_limit_bytes=vmem_bytes),
    )(
        *by_coupling, *block_parts, inner_state, mine, other, inner_coupling, surface_amp, group,
        edges, mix, ends, kept,
    )
    got = lax.all_to_all(chunk, "chan", 0, 0)
    q_shape, notes_shape = (2, out_strips, points, lanes), (9 + 6 * out_strips, 8, lanes)
    wide, second, notes = pl.pallas_call(
        second_outer_kernel,
        grid=(1,),
        out_shape=[
            jax.ShapeDtypeStruct((2, out_strips, folded_rows, lanes), f32),
            pltpu.HBM(q_shape, f32),
            pltpu.HBM(notes_shape, f32),
        ],
        in_specs=[in_one((2, 8, channels))] + [whole()] * 4,
        out_specs=[whole(), far(), far()],
        scratch_shapes=[pltpu.VMEM((2, points, channels), bf16)] * 2
        + [
            pltpu.VMEM(q_shape, f32),
            pltpu.VMEM((out_strips, points, lanes), f32),
            pltpu.VMEM(q_shape, f32),
            pltpu.VMEM(notes_shape, f32),
            pltpu.SemaphoreType.DMA((2,)),
        ],
        input_output_aliases={1: 0},
        compiler_params=pltpu.CompilerParams(vmem_limit_bytes=vmem_bytes),
    )(pltpu.with_memory_space_constraint(patch, pltpu.HBM), wide, outer_state, potential, mix)
    mine, kept, ends = run(
        gather_kernel, gathered, (got, pltpu.with_memory_space_constraint(notes, pltpu.HBM)), [whole(), far()]
    )
    block_parts = block_product(got)
    mine, other, kept = across_blocks(mine, kept, block_parts)
    q_inner, q_ends, parts = run(
        last_kernel,
        [(2, rows), (2, 2, 8, channels), (count, lanes)],
        (
            *by_coupling, *block_parts, p_inner, mine, other, inner_coupling, surface_amp, group,
            wide, mix, ends, kept, inner_state, second, notes,
        ),
        [scalars()] * 2 + [whole()] * 15,
        [pltpu.VMEM((2, 2, 24, channels), f32)],
    )
    parts = lax.all_to_all(parts.reshape(count, 1, lanes), both, 0, 0).reshape(count, lanes)
    last_inner, last_outer, columns, poor = pl.pallas_call(
        lambda *refs: finish_kernel(entries, *refs),
        out_shape=[
            jax.ShapeDtypeStruct((2, rows), f32),
            pltpu.HBM((2, points, channels), f32),
            jax.ShapeDtypeStruct((2, TERMS, TERMS + 1), f32),
            jax.ShapeDtypeStruct((1, lanes), f32),
        ],
        in_specs=[whole()] * 8,
        out_specs=[whole(), far(), whole(), whole()],
        scratch_shapes=[pltpu.VMEM((2, points, channels), f32), pltpu.SemaphoreType.DMA((8,))],
        compiler_params=pltpu.CompilerParams(vmem_limit_bytes=vmem_bytes),
    )(parts, inner_state, p_inner, q_inner, outer_state, wide, second, q_ends)

    def again(state):
        last_inner, last_outer, hessenberg = step_by_step(*inputs)
        columns = hessenberg.transpose(0, 2, 1)
        (columns,) = run(same_kernel, [columns.shape], (columns,), [whole()])
        return jnp.zeros((), f32), last_inner, last_outer, columns

    _, last_inner, last_outer, columns = lax.while_loop(
        lambda state: state[0] > 0.0, again, (poor[0, 0], last_inner, last_outer, columns)
    )
    return last_inner, last_outer, columns.transpose(0, 2, 1)


def solution(mesh):
    return jax.shard_map(
        body,
        mesh=mesh,
        in_specs=(
            P(None, ("rad", "chan")),
            P(None, ("rad", "chan"), None),
            P("rad", None, "chan"),
            P("rad", None, None, "chan"),
            P("rad", None, "chan", None),
            P(("rad", "chan"), None),
            P(),
            P(),
            P(),
            P(),
        ),
        out_specs=(P(None, ("rad", "chan")), P(None, ("rad", "chan"), None), P()),
        check_vma=False,
    )
```

```python
import jax
import jax.numpy as jnp
from jax import lax
from jax.experimental import pallas as pl
from jax.experimental.pallas import tpu as pltpu
from jax.sharding import PartitionSpec as P

STRIP = 256
TERMS = 2

highest = lax.Precision.HIGHEST
kinetic_coef = -0.5 * 0.05 / (12.0 * 0.25 * 0.25)
slope_coef = 1.0 / (12.0 * 0.25)
bloch_coef = 2.0
shift = 1.5
least_left = 0.1
both = ("rad", "chan")


def spread(block, axis, holder):
    block = jnp.where(lax.axis_index(axis) == holder, block, jnp.zeros_like(block))
    return lax.psum(block, axis)


def local_parts(left, right):
    real_part = jnp.sum(left[0] * right[0]) + jnp.sum(left[1] * right[1])
    imag_part = jnp.sum(left[0][0] * right[0][1] - left[0][1] * right[0][0]) + jnp.sum(
        left[1][0] * right[1][1] - left[1][1] * right[1][0]
    )
    return jnp.stack([real_part, imag_part])


def rotate(vector, real_coef, imag_coef):
    return jnp.stack(
        [
            real_coef * vector[0] - imag_coef * vector[1],
            real_coef * vector[1] + imag_coef * vector[0],
        ]
    )


def neighbours(last_rows, first_rows):
    count = lax.axis_size(both)
    forward = [(i, i + 1) for i in range(count - 1)]
    backward = [(target, source) for source, target in forward]
    return lax.ppermute(last_rows, both, forward), lax.ppermute(first_rows, both, backward)


def outer_apply(extended, potential, laser_mix, moved):
    points = extended.shape[1] - 4
    far_left = extended[:, 0:points]
    near_left = extended[:, 1 : points + 1]
    centre_row = extended[:, 2 : points + 2]
    near_right = extended[:, 3 : points + 3]
    far_right = extended[:, 4 : points + 4]
    laplace = -far_left + 16.0 * near_left - 30.0 * centre_row + 16.0 * near_right - far_right
    slope_rows = slope_coef * (far_left - 8.0 * near_left + 8.0 * near_right - far_right)
    mixed_slope = jnp.einsum("prc,cd->prd", slope_rows, laser_mix, precision=highest)
    return (
        kinetic_coef * laplace
        + (potential - moved) * centre_row
        + jnp.stack([mixed_slope[1], -mixed_slope[0]])
    )


def inner_windows(shards, own_partners, own_offsets):
    windows = []
    for couple_index in range(own_partners.shape[0]):
        source = lax.dynamic_index_in_dim(shards, own_partners[couple_index], 0, keepdims=False)
        source = source.transpose(1, 0, 2).reshape(2, -1)
        band_width = source.shape[1] // 2
        windows.append(
            lax.dynamic_slice_in_dim(source, own_offsets[couple_index] + band_width, band_width, 1)
        )
    return windows


def exchange(inner_vec, ghost_part, row):
    rows = inner_vec.shape[1]
    blocks, strips = lax.axis_size("rad"), lax.axis_size("chan")
    chunk = jnp.concatenate(
        [
            inner_vec,
            ghost_part.reshape(-1, rows),
            row.reshape(-1, rows),
            jnp.zeros((2, rows), jnp.float32),
        ],
        axis=0,
    )
    got = lax.all_to_all(jnp.broadcast_to(chunk, (strips,) + chunk.shape), "chan", 0, 0)
    own = got[:, 0:2]
    ghost_sum = jnp.sum(got[:, 2:10], axis=0)
    padded = jnp.pad(own, ((2, 1), (0, 0), (0, 0)))
    near = lax.dynamic_slice_in_dim(padded, lax.axis_index("chan"), 4, 0)
    chunk = jnp.concatenate(
        [near.reshape(8, rows), ghost_sum, got[0, 10:14], jnp.zeros((4, rows), jnp.float32)],
        axis=0,
    )
    got_blocks = lax.all_to_all(jnp.broadcast_to(chunk, (blocks,) + chunk.shape), "rad", 0, 0)
    shards = got_blocks[:, 0:8].reshape(blocks, 4, 2, rows)
    ghost = jnp.sum(got_blocks[:, 8:16], axis=0).reshape(2, 2, -1)
    first_row = got_blocks[0, 16:20].reshape(2, -1)
    return own.transpose(1, 0, 2).reshape(2, -1), shards, ghost, first_row


def step_by_step(
    inner_state,
    outer_state,
    inner_ham,
    inner_coupling,
    surface_amp,
    potential,
    laser_mix,
    partners,
    band_offsets,
    channel_group,
):
    block_order = inner_ham.shape[1]
    points, channels = outer_state.shape[1:]
    entries = float(
        lax.axis_size("rad") * block_order + lax.axis_size(both) * points * channels
    )
    block_index = lax.axis_index("rad")
    is_first = lax.axis_index(both) == 0
    member = (channel_group == block_index).astype(jnp.float32)
    masked_amp = surface_amp[0] * member[None, None, :]
    own_partners = lax.dynamic_index_in_dim(partners, block_index, 0, keepdims=False)
    own_offsets = lax.dynamic_index_in_dim(band_offsets, block_index, 0, keepdims=False)

    def total(value):
        return lax.psum(value, both) / entries

    def squares(vector):
        return jnp.sum(vector[0] * vector[0]) + jnp.sum(vector[1] * vector[1])

    start_len = jnp.sqrt(total(squares((inner_state, outer_state))))
    krylov = [(inner_state / start_len, outer_state / start_len)]
    hessenberg = jnp.zeros((2, TERMS + 1, TERMS), jnp.float32)
    for term_index in range(TERMS):
        inner_vec, outer_vec = krylov[term_index]
        ghost_part = jnp.einsum("pk,mki->pmi", inner_vec, masked_amp, precision=highest)
        row = jnp.where(is_first, outer_vec[:, 0], 0.0)
        own_vec, shards, ghost, first_row = exchange(inner_vec, ghost_part, row)
        result_in = jnp.dot(own_vec, inner_ham[0], precision=highest)
        for couple_index, window in enumerate(inner_windows(shards, own_partners, own_offsets)):
            result_in = result_in + jnp.dot(window, inner_coupling[0, couple_index], precision=highest)
        result_in = result_in + bloch_coef * jnp.einsum(
            "pi,ki->pk", first_row, masked_amp[0], precision=highest
        )
        low, high = neighbours(outer_vec[:, points - 2 :], outer_vec[:, :2])
        low = jnp.where(is_first, ghost[:, ::-1], low)
        extended = jnp.concatenate([low, outer_vec, high], axis=1)
        image = (result_in, outer_apply(extended, potential, laser_mix, 0.0))
        for prior_index in range(term_index + 1):
            prior = krylov[prior_index]
            coefs = total(local_parts(prior, image))
            image = tuple(
                part - rotate(prior_part, coefs[0], coefs[1])
                for part, prior_part in zip(image, prior)
            )
            hessenberg = hessenberg.at[:, prior_index, term_index].set(coefs)
        new_length = jnp.sqrt(total(squares(image)))
        hessenberg = hessenberg.at[0, term_index + 1, term_index].set(new_length)
        krylov.append((image[0] / new_length, image[1] / new_length))
    return (krylov[-1][0], krylov[-1][1], hessenberg)


lanes = 128
margin = 8
reach = 2
vmem_bytes = 16 * 2**20


def whole():
    return pl.BlockSpec(memory_space=pltpu.VMEM)


def anywhere():
    return pl.BlockSpec(memory_space=pl.ANY)


def far():
    return pl.BlockSpec(memory_space=pltpu.HBM)


def in_one(shape):
    return pl.BlockSpec(shape, lambda i: (0,) * len(shape))


def scalars():
    return pl.BlockSpec(memory_space=pltpu.SMEM)


def run(kernel, outs, args, in_specs, scratch=()):
    return pl.pallas_call(
        kernel,
        out_shape=[jax.ShapeDtypeStruct(*out) if isinstance(out[0], tuple) else jax.ShapeDtypeStruct(out, jnp.float32) for out in outs],
        in_specs=in_specs,
        out_specs=[whole()] * len(outs),
        scratch_shapes=list(scratch),
        compiler_params=pltpu.CompilerParams(vmem_limit_bytes=vmem_bytes),
    )(*args)


def two(x):
    high = x.astype(jnp.bfloat16)
    return high, (x - high.astype(jnp.float32)).astype(jnp.bfloat16)


def both_halves(x):
    high, low = two(x)
    rest = jnp.zeros((16 - 2 * x.shape[0], x.shape[1]), jnp.float32)
    return jnp.concatenate([high.astype(jnp.float32), low.astype(jnp.float32), rest], axis=0).astype(jnp.bfloat16)


def few_rows_dot(x, weights, flipped=False):
    rows = x.shape[0]
    lhs = both_halves(x)
    dims = (((1,), (1 if flipped else 0,)), ((), ()))
    total = sum(lax.dot_general(lhs, part, dims, preferred_element_type=jnp.float32) for part in weights)
    return total[:rows] + total[rows : 2 * rows]


def mixed_with(high, low, mix_ref):
    count = high.shape[0]
    first = jnp.dot(jnp.concatenate([high, low], axis=0), mix_ref[0], preferred_element_type=jnp.float32)
    return first[:count] + first[count:] + jnp.dot(high, mix_ref[1], preferred_element_type=jnp.float32)


def write_chunk(out_ref, inner_vec, ghosts, row, held_ref=None, written=None):
    half = inner_vec.shape[1]
    chunk = jnp.concatenate(
        [
            ghosts[:, :half],
            ghosts[:, half:],
            inner_vec,
            row[:, :half],
            row[:, half:],
            jnp.zeros((2, half), jnp.float32),
        ],
        axis=0,
    )
    if held_ref is None:
        for strip in range(out_ref.shape[0]):
            out_ref[strip, 0:16] = chunk
        return []
    held_ref[...] = chunk
    copies = [
        pltpu.make_async_copy(held_ref, out_ref.at[strip, pl.ds(0, 16)], written.at[strip])
        for strip in range(out_ref.shape[0])
    ]
    for copy in copies:
        copy.start()
    return copies


def ghost_rows(inner_vec, amps, member):
    return jnp.concatenate([few_rows_dot(inner_vec, amp) * member for amp in amps], axis=0)


def member_of(group_ref):
    return jnp.where(group_ref[...] == lax.axis_index("rad"), 1.0, 0.0)


def at_first():
    return (lax.axis_index("rad") == 0) & (lax.axis_index("chan") == 0)


def at_last():
    last = [lax.axis_index(axis) == lax.axis_size(axis) - 1 for axis in both]
    return last[0] & last[1]


def send_ends(out_ref, first_rows, last_rows, held_ref=None, written=None):
    strips, _, half = out_ref.shape
    copies = []
    for end, (there, points) in enumerate(((1, last_rows), (strips - 1, first_rows))):
        both_parts = jnp.concatenate(points, axis=0)
        rows = jnp.concatenate([both_parts[:, :half], both_parts[:, half:]], axis=0)
        strip = lax.rem(lax.axis_index("chan") + there, strips)
        if held_ref is None:
            out_ref[strip, 16:24] = rows
        else:
            held_ref[end] = rows
            copies.append(pltpu.make_async_copy(held_ref.at[end], out_ref.at[strip, pl.ds(16, 8)], written.at[end]))
            copies[-1].start()
    return copies


def start_kernel(inner_ref, head_ref, tail_ref, amp_ref, group_ref, chunk_ref):
    send_ends(chunk_ref, [head_ref[part, 0:2] for part in range(2)], [tail_ref[part, 6:8] for part in range(2)])
    row = jnp.concatenate([head_ref[part, 0:1] for part in range(2)], axis=0)
    row = jnp.where(at_first(), row, 0.0)
    inner_vec = inner_ref[...]
    amps = [two(amp_ref[0, radius]) for radius in range(2)]
    ghosts = ghost_rows(inner_vec, amps, member_of(group_ref))
    write_chunk(chunk_ref, inner_vec, ghosts, row)


def stencils(window, pot):
    before_2, before_1, here, after_1, after_2 = window
    local = (pot - (30.0 * kinetic_coef + shift)) * here + (
        16.0 * kinetic_coef * (before_1 + after_1) - kinetic_coef * (before_2 + after_2)
    )
    return local, (before_2 - after_2) + 8.0 * (after_1 - before_1)


def first_outer_kernel(
    state_ref, pot_ref, mix_ref, out_ref, mix_out, edges_ref, wide_ref, pot_wide, slope_h, slope_l
):
    points, channels = state_ref.shape[1:]
    strips = channels // lanes
    length = points // 8
    for strip in range(strips):
        here = slice(strip * lanes, (strip + 1) * lanes)
        for part in range(3):
            source = pot_ref if part == 2 else state_ref.at[part]
            target = pot_wide.at[strip] if part == 2 else wide_ref.at[part, strip]
            target[margin : margin + points] = source[:, here]
            target[0:margin] = jnp.zeros((margin, lanes), jnp.float32)
            target[margin + points :] = jnp.zeros((margin, lanes), jnp.float32)
    for part in range(3):
        source = pot_ref if part == 2 else state_ref.at[part]
        edges_ref[0, part], edges_ref[1, part] = source[0:8], source[points - 8 : points]

    def strip_step(step, _):
        part, strip = lax.div(step, strips), lax.rem(step, strips)

        def load(place):
            return wide_ref[part, strip, pl.ds(margin + place, 8, stride=length)]

        window = [load(place) for place in range(-2 * reach, 0)]
        columns = pl.ds(pl.multiple_of(strip * lanes, lanes), lanes)
        for first in range(-reach, length + reach, 2):
            slopes = []
            for place in (first, first + 1):
                window.append(load(place + reach))
                local, slope = stencils(window, pot_wide[strip, pl.ds(margin + place, 8, stride=length)])
                out_ref[part, strip, (place + reach) * 8 : (place + reach + 1) * 8] = local
                slopes.append(slope)
                window.pop(0)
            rows = slice((first + reach) * 8, (first + reach + 2) * 8)
            slope_h[part, rows, columns], slope_l[part, rows, columns] = two(jnp.concatenate(slopes, axis=0))
        return 0

    lax.fori_loop(0, 2 * strips, strip_step, 0)
    mix_out[0], mix_out[1] = two(slope_coef * mix_ref[...])
    add_mixed(out_ref, slope_h, slope_l, mix_out)


def add_mixed(out_ref, slope_h, slope_l, mix_ref):
    for part in range(2):
        mixed = mixed_with(slope_h[1 - part], slope_l[1 - part], mix_ref)
        for strip in range(out_ref.shape[1]):
            own = mixed[:, strip * lanes : (strip + 1) * lanes]
            out_ref[part, strip] = out_ref[part, strip] + (own if part == 0 else -own)


def products(s, p, q):
    return [
        s[0] * s[0] + s[1] * s[1],
        s[0] * p[0] + s[1] * p[1],
        s[0] * p[1] - s[1] * p[0],
        s[0] * q[0] + s[1] * q[1],
        s[0] * q[1] - s[1] * q[0],
        p[0] * p[0] + p[1] * p[1],
        p[0] * q[0] + p[1] * q[1],
        p[0] * q[1] - p[1] * q[0],
        q[0] * q[0] + q[1] * q[1],
    ]


def second_outer_kernel(
    patch_ref, wide_in, state_in, pot_in, mix_ref,
    wide_ref, q_out, notes_out, slope_h, slope_l, state_ref, pot_ref, out_ref, notes_ref, written,
):
    strips, places = out_ref.shape[1:3]
    length = places // 8
    for part in range(2):
        for strip in range(strips):
            here = slice(strip * lanes, (strip + 1) * lanes)
            wide_ref[part, strip, pl.ds(reach * 8, 2, stride=8)] = patch_ref[part, 0:2, here]
            wide_ref[part, strip, pl.ds(length * 8 + 7, 2, stride=8)] = patch_ref[part, 2:4, here]
    for strip in range(strips):
        here = slice(strip * lanes, (strip + 1) * lanes)
        pot_ref[strip] = pot_in[:, here]
        for part in range(2):
            state_ref[part, strip] = state_in[part, :, here]

    def strip_step(step, _):
        part, strip = lax.div(step, strips), lax.rem(step, strips)

        def load(place):
            return wide_ref[part, strip, (place + reach) * 8 : (place + reach + 1) * 8]

        window = [load(place) for place in range(-reach, reach)]
        columns = pl.ds(pl.multiple_of(strip * lanes, lanes), lanes)
        for first in range(0, length, 2):
            slopes = []
            for place in (first, first + 1):
                window.append(load(place + reach))
                local, slope = stencils(window, pot_ref[strip, pl.ds(place, 8, stride=length)])
                out_ref[part, strip, place * 8 : (place + 1) * 8] = local
                slopes.append(slope)
                window.pop(0)
            rows = slice(first * 8, (first + 2) * 8)
            slope_h[part, rows, columns], slope_l[part, rows, columns] = two(jnp.concatenate(slopes, axis=0))
        return 0

    lax.fori_loop(0, 2 * strips, strip_step, 0)
    add_mixed(out_ref, slope_h, slope_l, mix_ref)
    copy = pltpu.make_async_copy(out_ref, q_out, written.at[0])
    copy.start()
    run_of = lax.broadcasted_iota(jnp.int32, (8, lanes), 0)

    def gram_step(strip, sums):
        for place in range(length):
            entries = products(
                [state_ref[part, strip, pl.ds(place, 8, stride=length)] for part in range(2)],
                [wide_ref[part, strip, (place + reach) * 8 : (place + reach + 1) * 8] for part in range(2)],
                [out_ref[part, strip, place * 8 : (place + 1) * 8] for part in range(2)],
            )
            if place < 4 or place >= length - 4:
                inside = run_of > 0 if place < 4 else run_of < 7
                entries = [jnp.where(inside, entry, 0.0) for entry in entries]
            sums = [total + entry for total, entry in zip(sums, entries)]
        return sums

    sums = lax.fori_loop(0, strips, gram_step, [jnp.zeros((8, lanes), jnp.float32)] * 9)
    for k in range(9):
        notes_ref[k] = sums[k]
    for strip in range(strips):
        here = slice(strip * lanes, (strip + 1) * lanes)
        for end, rows in enumerate((slice(0, 8), slice(places - 8, places))):
            notes_ref[9 + strips * 3 * end + strip] = pot_in[rows, here]
            for part in range(2):
                notes_ref[9 + strips * (3 * end + part + 1) + strip] = state_in[part, rows, here]
    notes_copy = pltpu.make_async_copy(notes_ref, notes_out, written.at[1])
    notes_copy.start()
    copy.wait()
    notes_copy.wait()


def block_kernel(first, got_ref, ham_ref, out_ref, held_ref, arrived):
    rows = ham_ref.shape[2]
    pieces, size = held_ref.shape[:2]
    copies = [
        pltpu.make_async_copy(ham_ref.at[0, pl.ds((first + k) * size, size)], held_ref.at[k], arrived.at[k])
        for k in range(pieces)
    ]
    for copy in copies:
        copy.start()
    total = jnp.zeros((16, rows), jnp.float32)
    for k, copy in enumerate(copies):
        copy.wait()
        for part in range(size // rows):
            lhs = both_halves(got_ref[(first + k) * (size // rows) + part, 8:10])
            for weights in two(held_ref[k, part * rows : (part + 1) * rows]):
                total = total + jnp.dot(lhs, weights, preferred_element_type=jnp.float32)
    out_ref[...] = total[0:2] + total[2:4]


def chip_index():
    return lax.div(lax.axis_index("rad"), 2)


def core_index():
    return lax.rem(lax.axis_index("rad"), 2)


def gather_kernel(got_ref, after_ref, out_ref, kept_ref, ends_ref):
    strips = got_ref.shape[0]
    own = lax.axis_index("chan")
    for k in range(4):
        strip = own + (k - 2)
        there = (strip >= 0) & (strip < strips)
        near = got_ref[jnp.clip(strip, 0, strips - 1), 8:10]
        out_ref[2 * k : 2 * k + 2] = jnp.where(there, near, 0.0)
    kept_ref[0:8] = sum(got_ref[strip, 0:8] for strip in range(strips))
    kept_ref[8:12] = got_ref[0, 10:14]
    kept_ref[12:16] = jnp.zeros((4, got_ref.shape[2]), jnp.float32)
    out_ref[8:16] = jnp.where(chip_index() == 0, kept_ref[8:16], kept_ref[0:8])
    before = got_ref[lax.rem(own + strips - 1, strips), 16:24]
    after = got_ref[lax.rem(own + 1, strips), 16:24]
    ends_ref[0], ends_ref[1] = before, after
    out_ref[16:24] = jnp.where(own == 0, before, after)


def joined(kept_ref, came, add_ghosts, take_row):
    ghosts = kept_ref[0:8] + jnp.where(add_ghosts, came, 0.0)
    return ghosts, jnp.where(take_row, came, kept_ref[8:16])


def join_kernel(mine_ref, other_ref, kept_ref, after_ref, out_ref, kept_out):
    chip = chip_index()
    out_ref[0:8], out_ref[8:16] = mine_ref[0:8], other_ref[0:8]
    ghosts, row = joined(kept_ref, other_ref[8:16], (chip == 0) | (chip == 3), chip == 1)
    kept_out[0:8], kept_out[8:16] = ghosts, row
    out_ref[16:24] = jnp.where(chip <= 1, row, ghosts)
    out_ref[24:32] = mine_ref[16:24]


def last_join_kernel(mine_ref, other_ref, kept_ref, near_ref, after_ref, out_ref, kept_out):
    chip, core = chip_index(), core_index()
    out_ref[0:16], out_ref[16:32] = mine_ref[0:16], other_ref[0:16]
    ghosts, row = joined(kept_ref, other_ref[16:24], chip == 0, chip >= 2)
    kept_out[0:8], kept_out[8:16] = ghosts, row
    out_ref[32:40] = jnp.where(core == 0, row, ghosts)
    is_low = lax.axis_index("chan") == 0
    from_own = (core == 0) == is_low
    from_near = (lax.rem(chip, 2) == 1) == is_low
    out_ref[40:48] = jnp.where(from_own, mine_ref[24:32], jnp.where(from_near, near_ref[16:24], other_ref[24:32]))


def join(kernel, count, *args):
    width = args[0].shape[1]
    return run(kernel, [(count, width), (16, width)], args, [whole()] * (len(args) - 1) + [anywhere()])


def inner_result(partners_ref, offsets_ref, block_a, block_b, inner_ref, mine_ref, other_ref, coupling_ref, amp_ref, member, row):
    result = block_a[...] + block_b[...] - shift * inner_ref[...]
    couplings, band_width = coupling_ref.shape[1:3]
    block_index = lax.axis_index("rad")
    for couple_index in range(couplings):
        apart = partners_ref[couple_index, block_index] ^ block_index
        far_pair = lax.shift_right_logical(apart, 2)
        slot = 4 * (apart & 1) + lax.shift_right_logical(apart ^ (2 * far_pair), 1)
        rows = pl.ds(pl.multiple_of(lax.rem(slot, 4) * 8, 8), 8)
        near = jnp.where(slot < 4, mine_ref[rows], other_ref[rows])
        near = jnp.concatenate([near[2 * k : 2 * k + 2] for k in range(4)], axis=1)
        near = jnp.concatenate([near, jnp.zeros((6, near.shape[1]), jnp.float32)], axis=0)
        first = offsets_ref[couple_index, block_index] + band_width
        window = pltpu.roll(near, near.shape[1] - first, 1)[0:2, :band_width]
        result = result + few_rows_dot(window, two(coupling_ref[0, couple_index]))
    return result + bloch_coef * few_rows_dot(row * member, two(amp_ref[0, 0]), flipped=True)


def unpacked(kept_ref, other_ref):
    ghosts, row = joined(kept_ref, other_ref[32:40], True, core_index() == 1)
    return jnp.concatenate([ghosts[0:4], ghosts[4:8]], axis=1), jnp.concatenate([row[0:2], row[2:4]], axis=1)


def points_of(ref, part, first, count, run_index=0):
    return jnp.concatenate(
        [ref[part, strip, pl.ds(first * 8 + run_index, count, stride=8)] for strip in range(ref.shape[1])], axis=1
    )


def mend(edge_ref, pots, mix_ref, more=None):
    local, slopes = [], []
    for part in range(2):
        for end in range(2):
            inner, slope = stencils([edge_ref[part, end, 8 + k : 16 + k] for k in range(-reach, reach + 1)], pots[end])
            local.append(inner)
            slopes.append(slope)
    mixed = mixed_with(*two(jnp.concatenate(slopes + ([] if more is None else [more]), axis=0)), mix_ref)
    image = [
        [
            local[2 * part + end] + (mixed[16 + 8 * end : 24 + 8 * end] if part == 0 else -mixed[8 * end : 8 * end + 8])
            for end in range(2)
        ]
        for part in range(2)
    ]
    return image, mixed[32:]


def pick_ends(ends_ref, other_ref):
    strip = lax.axis_index("chan")
    is_low, is_high = strip == 0, strip == lax.axis_size("chan") - 1
    came = other_ref[40:48]
    before = jnp.where(at_first(), 0.0, jnp.where(is_low, came, ends_ref[0]))
    after = jnp.where(at_last(), 0.0, jnp.where(is_high, came, ends_ref[1]))
    return [
        [jnp.concatenate([x[2 * part : 2 * part + 2], x[4 + 2 * part : 6 + 2 * part]], axis=1) for part in range(2)]
        for x in (before, after)
    ]


def between_kernel(
    partners_ref, offsets_ref, block_a, block_b, inner_ref, mine_ref, other_ref, coupling_ref, amp_ref, group_ref,
    edges_ref, mix_ref, ends_ref, kept_ref,
    image_ref, chunk_ref, patch_out, held_ref, written, ends_held, ends_written, patch_ref, patch_written, edge_ref,
):
    member = member_of(group_ref)
    ghosts, row = unpacked(kept_ref, other_ref)
    before, after = pick_ends(ends_ref, other_ref)
    edge_ref[...] = jnp.zeros_like(edge_ref)
    for part in range(2):
        edge_ref[part, 0, 6:8] = before[part]
        edge_ref[part, 1, 16:18] = after[part]
        for end in range(2):
            edge_ref[part, end, 8:16] = edges_ref[end, part]
    near, far_off = ghosts[0:2], ghosts[2:4]
    kinetic = [kinetic_coef * (16.0 * near - far_off), -kinetic_coef * near]
    slope = jnp.concatenate([far_off - 8.0 * near, near, jnp.zeros((12, near.shape[1]), jnp.float32)], axis=0)
    p, mixed = mend(edge_ref, [edges_ref[end, 2] for end in range(2)], mix_ref, slope)
    first_rows, last_rows = [], []
    for part in range(2):
        extra = jnp.concatenate(
            [
                kinetic[k][part : part + 1]
                + (mixed[2 * k + 1 : 2 * k + 2] if part == 0 else -mixed[2 * k : 2 * k + 1])
                for k in range(2)
            ],
            axis=0,
        )
        first_rows.append(p[part][0][0:2] + jnp.where(at_first(), extra, 0.0))
        last_rows.append(p[part][1][6:8])
        patch_ref[part] = jnp.concatenate(
            [first_rows[part], last_rows[part], jnp.zeros((4, near.shape[1]), jnp.float32)], axis=0
        )
    copy = pltpu.make_async_copy(patch_ref, patch_out, patch_written)
    copy.start()
    copies = [copy] + send_ends(chunk_ref, first_rows, last_rows, ends_held, ends_written)
    image = inner_result(
        partners_ref, offsets_ref, block_a, block_b, inner_ref, mine_ref, other_ref, coupling_ref, amp_ref, member, row
    )
    image_ref[...] = image
    row = jnp.where(at_first(), jnp.concatenate([rows[0:1] for rows in first_rows], axis=0), 0.0)
    amps = [two(amp_ref[0, radius]) for radius in range(2)]
    copies += write_chunk(chunk_ref, image, ghost_rows(image, amps, member), row, held_ref, written)
    for copy in copies:
        copy.wait()


def last_kernel(
    partners_ref, offsets_ref, block_a, block_b, inner_ref, mine_ref, other_ref, coupling_ref, amp_ref, group_ref,
    wide_ref, mix_ref, ends_ref, kept_ref, start_ref, second_ref, notes_ref,
    image_ref, out_ref, parts_ref, edge_ref,
):
    member = member_of(group_ref)
    ghosts, row = unpacked(kept_ref, other_ref)
    image = inner_result(
        partners_ref, offsets_ref, block_a, block_b, inner_ref, mine_ref, other_ref, coupling_ref, amp_ref, member, row
    )
    image_ref[...] = image
    strips = wide_ref.shape[1]
    length = second_ref.shape[2] // 8
    noted = [
        [
            jnp.concatenate([notes_ref[9 + strips * (3 * end + k) + strip] for strip in range(strips)], axis=1)
            for k in range(3)
        ]
        for end in range(2)
    ]
    before, after = pick_ends(ends_ref, other_ref)
    edge_ref[...] = jnp.zeros_like(edge_ref)
    for part in range(2):
        ghost = jnp.concatenate([ghosts[2 + part : 3 + part], ghosts[part : part + 1]], axis=0)
        edge_ref[part, 0, 6:8] = jnp.where(at_first(), ghost, before[part])
        edge_ref[part, 0, 8:24] = points_of(wide_ref, part, reach, 16)
        edge_ref[part, 1, 0:16] = points_of(wide_ref, part, length + reach - 16, 16, 7)
        edge_ref[part, 1, 16:18] = after[part]
    q, _ = mend(edge_ref, [noted[end][0] for end in range(2)], mix_ref)
    row_of = lax.broadcasted_iota(jnp.int32, q[0][0].shape, 0)
    mended = [row_of < 4, row_of >= 4]
    totals = [notes_ref[k] for k in range(9)]
    for end in range(2):
        for part in range(2):
            there = points_of(second_ref, part, 0 if end == 0 else length - 8, 8, 7 * end)
            q[part][end] = jnp.where(mended[end], q[part][end], there)
            out_ref[end, part] = q[part][end]
        entries = products(noted[end][1:], [edge_ref[part, end, 8:16] for part in range(2)], [q[part][end] for part in range(2)])
        for k, entry in enumerate(entries):
            entry = jnp.where(mended[end], entry, 0.0)
            totals[k] = totals[k] + sum(entry[:, strip * lanes : (strip + 1) * lanes] for strip in range(strips))
    start, inner = start_ref[...], inner_ref[...]
    inside = products([start[0:1], start[1:2]], [inner[0:1], inner[1:2]], [image[0:1], image[1:2]])
    lane = lax.broadcasted_iota(jnp.int32, (1, lanes), 1)
    sums = jnp.zeros((1, lanes), jnp.float32)
    for k in range(9):
        line = jnp.sum(totals[k], axis=0, keepdims=True) + inside[k][:, :lanes] + inside[k][:, lanes:]
        sums = jnp.where(lane == k, jnp.sum(line, axis=1, keepdims=True), sums)
    parts_ref[...] = jnp.broadcast_to(sums, parts_ref.shape)


def arnoldi_coefs(gram):
    ss, spr, spi, sqr, sqi, pp, pqr, pqi, qq = gram
    cr, ci = spr / ss, spi / ss
    left_1 = pp - (spr * cr + spi * ci)
    h10 = jnp.sqrt(left_1 / ss)
    sxr = sqr - (cr * spr - ci * spi)
    sxi = sqi - (cr * spi + ci * spr)
    h01r, h01i = sxr / (ss * h10), sxi / (ss * h10)
    pxr, pxi = pqr - cr * pp, pqi - ci * pp
    yxr = pxr - (cr * sxr + ci * sxi)
    yxi = pxi - (cr * sxi - ci * sxr)
    scale = 1.0 / left_1
    h11r, h11i = yxr * scale, yxi * scale
    xx = (qq - 2.0 * (cr * pqr + ci * pqi) + (cr * cr + ci * ci) * pp) * scale
    left_2 = xx - (h01r * h01r + h01i * h01i) - (h11r * h11r + h11i * h11i)
    h21 = jnp.sqrt(left_2)
    fine = (left_1 > least_left * pp) & (left_2 > least_left * xx)
    poor = jnp.where(fine, 0.0, 1.0)
    zero = jnp.zeros_like(ss)
    entries = [[[cr + shift, h10, zero], [h01r, h11r + shift, h21]], [[ci, zero, zero], [h01i, h11i, zero]]]
    a = jnp.sqrt(ss)
    coef_q = 1.0 / (a * h10 * h21)
    coef_p = (-(cr + h11r) * coef_q, -(ci + h11i) * coef_q)
    coef_s = (
        (h11r * cr - h11i * ci) * coef_q - h01r / (a * h21),
        (h11r * ci + h11i * cr) * coef_q - h01i / (a * h21),
    )
    return entries, (coef_q, coef_p, coef_s), poor


def combined(coefs, s, p, q):
    coef_q, coef_p, coef_s = coefs
    return (
        coef_q * q[0] + coef_p[0] * p[0] - coef_p[1] * p[1] + coef_s[0] * s[0] - coef_s[1] * s[1],
        coef_q * q[1] + coef_p[0] * p[1] + coef_p[1] * p[0] + coef_s[0] * s[1] + coef_s[1] * s[0],
    )


def finish_kernel(
    entries, parts_ref, start_ref, inner_ref, image_ref, state_ref, wide_ref, second_ref, edge_ref,
    inner_out, result_out, hess_out, poor_out, outer_out, written,
):
    strips, places = second_ref.shape[1:3]
    length = places // 8
    sums = jnp.sum(parts_ref[...], axis=0, keepdims=True) * (1.0 / entries)
    lane = lax.broadcasted_iota(jnp.int32, sums.shape, 1)
    gram = [jnp.sum(jnp.where(lane == k, sums, 0.0), axis=1, keepdims=True) for k in range(9)]
    values, (coef_q, coef_p, coef_s), poor = arnoldi_coefs(gram)
    tile = lambda coef: jnp.broadcast_to(coef, (8, lanes))
    coefs = tile(coef_q), [tile(coef) for coef in coef_p], [tile(coef) for coef in coef_s]

    def put(rows, p_first, q_first, run_index, edge=None):
        for strip in range(strips):
            here = slice(strip * lanes, (strip + 1) * lanes)
            result = combined(
                coefs,
                [state_ref[part, rows, here] for part in range(2)],
                [wide_ref[part, strip, pl.ds(p_first * 8 + run_index, 8, stride=8)] for part in range(2)],
                [
                    second_ref[part, strip, pl.ds(q_first * 8 + run_index, 8, stride=8)]
                    if edge is None
                    else edge_ref[edge, part, :, here]
                    for part in range(2)
                ],
            )
            for part in range(2):
                outer_out[part, rows, here] = result[part]

    copies = []
    for run_index in range(8):
        for first in range(0, length, 8):
            row = run_index * length + first
            edge = 0 if row == 0 else 1 if row == places - 8 else None
            put(slice(row, row + 8), first + reach, first, run_index, edge)
        rows = pl.ds(run_index * length, length)
        copies.append(
            pltpu.make_async_copy(outer_out.at[:, rows], result_out.at[:, rows], written.at[run_index])
        )
        copies[-1].start()
    for first in range(0, inner_out.shape[1], lanes):
        here = slice(first, first + lanes)
        result = combined(
            [coefs[0][0:1], [c[0:1] for c in coefs[1]], [c[0:1] for c in coefs[2]]],
            *[[ref[0:1, here], ref[1:2, here]] for ref in (start_ref, inner_ref, image_ref)],
        )
        for part in range(2):
            inner_out[part : part + 1, here] = result[part]
    lane = lax.broadcasted_iota(jnp.int32, (1, TERMS + 1), 1)
    for part in range(2):
        for column in range(TERMS):
            line = jnp.zeros((1, TERMS + 1), jnp.float32)
            for k, value in enumerate(values[part][column]):
                line = jnp.where(lane == k, value, line)
            hess_out[part, column : column + 1] = line
    poor_out[...] = jnp.broadcast_to(poor, poor_out.shape)
    for copy in copies:
        copy.wait()


def same_kernel(in_ref, out_ref):
    out_ref[...] = in_ref[...]


def across_blocks(mine, kept, after):
    blocks = lax.axis_size("rad")
    last = blocks // 2 - 1
    near = lax.ppermute(mine, "rad", [(i, i ^ 2) for i in range(blocks)])
    mine, kept = join(join_kernel, 32, mine, near, kept, after[0])
    other = lax.ppermute(mine, "rad", [(i, 2 * (last - i // 2) + i % 2) for i in range(blocks)])
    mine, kept = join(last_join_kernel, 48, mine, other, kept, near, after[1])
    return mine, lax.ppermute(mine, "rad", [(i, i ^ 1) for i in range(blocks)]), kept


def body(*inputs):
    (
        inner_state,
        outer_state,
        inner_ham,
        inner_coupling,
        surface_amp,
        potential,
        laser_mix,
        partners,
        band_offsets,
        channel_group,
    ) = inputs
    block_order, rows = inner_ham.shape[1:]
    points, channels = outer_state.shape[1:]
    count = lax.axis_size(both)
    blocks, strips = lax.axis_size("rad"), lax.axis_size("chan")
    entries = float(blocks * block_order + count * points * channels)
    group = channel_group.reshape(1, channels)
    by_coupling = partners.T, band_offsets.T
    f32, bf16 = jnp.float32, jnp.bfloat16
    out_strips = channels // lanes
    folded_rows = points + 2 * reach * 8

    chunk = pl.pallas_call(
        start_kernel,
        grid=(1,),
        out_shape=jax.ShapeDtypeStruct((strips, 24, rows), f32),
        in_specs=[
            whole(),
            in_one((2, 8, channels)),
            pl.BlockSpec((2, 8, channels), lambda i: (0, points // 8 - 1, 0)),
            whole(),
            whole(),
        ],
        out_specs=whole(),
        compiler_params=pltpu.CompilerParams(vmem_limit_bytes=vmem_bytes),
    )(inner_state, outer_state, outer_state, surface_amp, group)
    got = lax.all_to_all(chunk, "chan", 0, 0)
    wide, mix, edges = pl.pallas_call(
        first_outer_kernel,
        out_shape=[
            jax.ShapeDtypeStruct((2, out_strips, folded_rows, lanes), f32),
            jax.ShapeDtypeStruct((2, channels, channels), bf16),
            jax.ShapeDtypeStruct((2, 3, 8, channels), f32),
        ],
        in_specs=[whole()] * 3,
        out_specs=[whole()] * 3,
        scratch_shapes=[
            pltpu.VMEM((2, out_strips, points + 2 * margin, lanes), f32),
            pltpu.VMEM((out_strips, points + 2 * margin, lanes), f32),
            pltpu.VMEM((2, folded_rows, channels), bf16),
            pltpu.VMEM((2, folded_rows, channels), bf16),
        ],
        compiler_params=pltpu.CompilerParams(vmem_limit_bytes=vmem_bytes),
    )(outer_state, potential, laser_mix)

    def block_product(got):
        size = 2 * rows
        parts = []
        for first, last in ((0, 4), (4, 8)):
            parts += run(
                lambda *refs, first=first: block_kernel(first, *refs),
                [(2, rows)],
                (got, pltpu.with_memory_space_constraint(inner_ham, pltpu.HBM)),
                [whole(), far()],
                [pltpu.VMEM((last - first, size, rows), f32), pltpu.SemaphoreType.DMA((last - first,))],
            )
        return parts

    gathered = [(24, rows), (16, rows), (2, 8, rows)]
    mine, kept, ends = run(gather_kernel, gathered, (got, wide), [whole(), anywhere()])
    block_parts = block_product(got)
    mine, other, kept = across_blocks(mine, kept, block_parts)
    p_inner, chunk, patch = pl.pallas_call(
        between_kernel,
        out_shape=[
            jax.ShapeDtypeStruct((2, rows), f32),
            pltpu.HBM((strips, 24, rows), f32),
            pltpu.HBM((2, 8, channels), f32),
        ],
        in_specs=[scalars()] * 2 + [whole()] * 12,
        out_specs=[whole()] + [far()] * 2,
        scratch_shapes=[
            pltpu.VMEM((16, rows), f32),
            pltpu.SemaphoreType.DMA((strips,)),
            pltpu.VMEM((2, 8, rows), f32),
            pltpu.SemaphoreType.DMA((2,)),
        ]
        + [pltpu.VMEM((2, 8, channels), f32), pltpu.SemaphoreType.DMA, pltpu.VMEM((2, 2, 24, channels), f32)],
        compiler_params=pltpu.CompilerParams(vmem_limit_bytes=vmem_bytes),
    )(
        *by_coupling, *block_parts, inner_state, mine, other, inner_coupling, surface_amp, group,
        edges, mix, ends, kept,
    )
    got = lax.all_to_all(chunk, "chan", 0, 0)
    q_shape, notes_shape = (2, out_strips, points, lanes), (9 + 6 * out_strips, 8, lanes)
    wide, second, notes = pl.pallas_call(
        second_outer_kernel,
        grid=(1,),
        out_shape=[
            jax.ShapeDtypeStruct((2, out_strips, folded_rows, lanes), f32),
            pltpu.HBM(q_shape, f32),
            pltpu.HBM(notes_shape, f32),
        ],
        in_specs=[in_one((2, 8, channels))] + [whole()] * 4,
        out_specs=[whole(), far(), far()],
        scratch_shapes=[pltpu.VMEM((2, points, channels), bf16)] * 2
        + [
            pltpu.VMEM(q_shape, f32),
            pltpu.VMEM((out_strips, points, lanes), f32),
            pltpu.VMEM(q_shape, f32),
            pltpu.VMEM(notes_shape, f32),
            pltpu.SemaphoreType.DMA((2,)),
        ],
        input_output_aliases={1: 0},
        compiler_params=pltpu.CompilerParams(vmem_limit_bytes=vmem_bytes),
    )(pltpu.with_memory_space_constraint(patch, pltpu.HBM), wide, outer_state, potential, mix)
    mine, kept, ends = run(
        gather_kernel, gathered, (got, pltpu.with_memory_space_constraint(notes, pltpu.HBM)), [whole(), far()]
    )
    block_parts = block_product(got)
    mine, other, kept = across_blocks(mine, kept, block_parts)
    q_inner, q_ends, parts = run(
        last_kernel,
        [(2, rows), (2, 2, 8, channels), (count, lanes)],
        (
            *by_coupling, *block_parts, p_inner, mine, other, inner_coupling, surface_amp, group,
            wide, mix, ends, kept, inner_state, second, notes,
        ),
        [scalars()] * 2 + [whole()] * 15,
        [pltpu.VMEM((2, 2, 24, channels), f32)],
    )
    parts = lax.all_to_all(parts.reshape(count, 1, lanes), both, 0, 0).reshape(count, lanes)
    last_inner, last_outer, columns, poor = pl.pallas_call(
        lambda *refs: finish_kernel(entries, *refs),
        out_shape=[
            jax.ShapeDtypeStruct((2, rows), f32),
            pltpu.HBM((2, points, channels), f32),
            jax.ShapeDtypeStruct((2, TERMS, TERMS + 1), f32),
            jax.ShapeDtypeStruct((1, lanes), f32),
        ],
        in_specs=[whole()] * 8,
        out_specs=[whole(), far(), whole(), whole()],
        scratch_shapes=[pltpu.VMEM((2, points, channels), f32), pltpu.SemaphoreType.DMA((8,))],
        compiler_params=pltpu.CompilerParams(vmem_limit_bytes=vmem_bytes),
    )(parts, inner_state, p_inner, q_inner, outer_state, wide, second, q_ends)

    def again(state):
        last_inner, last_outer, hessenberg = step_by_step(*inputs)
        columns = hessenberg.transpose(0, 2, 1)
        (columns,) = run(same_kernel, [columns.shape], (columns,), [whole()])
        return jnp.zeros((), f32), last_inner, last_outer, columns

    _, last_inner, last_outer, columns = lax.while_loop(
        lambda state: state[0] > 0.0, again, (poor[0, 0], last_inner, last_outer, columns)
    )
    return last_inner, last_outer, columns.transpose(0, 2, 1)


def solution(mesh):
    return jax.shard_map(
        body,
        mesh=mesh,
        in_specs=(
            P(None, ("rad", "chan")),
            P(None, ("rad", "chan"), None),
            P("rad", None, "chan"),
            P("rad", None, None, "chan"),
            P("rad", None, "chan", None),
            P(("rad", "chan"), None),
            P(),
            P(),
            P(),
            P(),
        ),
        out_specs=(P(None, ("rad", "chan")), P(None, ("rad", "chan"), None), P()),
        check_vma=False,
    )
```

```python
import jax
import jax.numpy as jnp
from jax import lax
from jax.experimental import pallas as pl
from jax.experimental.pallas import tpu as pltpu
from jax.sharding import PartitionSpec as P

STRIP = 256
TERMS = 2

highest = lax.Precision.HIGHEST
kinetic_coef = -0.5 * 0.05 / (12.0 * 0.25 * 0.25)
slope_coef = 1.0 / (12.0 * 0.25)
bloch_coef = 2.0
shift = 1.5
least_left = 0.1
both = ("rad", "chan")


def spread(block, axis, holder):
    block = jnp.where(lax.axis_index(axis) == holder, block, jnp.zeros_like(block))
    return lax.psum(block, axis)


def local_parts(left, right):
    real_part = jnp.sum(left[0] * right[0]) + jnp.sum(left[1] * right[1])
    imag_part = jnp.sum(left[0][0] * right[0][1] - left[0][1] * right[0][0]) + jnp.sum(
        left[1][0] * right[1][1] - left[1][1] * right[1][0]
    )
    return jnp.stack([real_part, imag_part])


def rotate(vector, real_coef, imag_coef):
    return jnp.stack(
        [
            real_coef * vector[0] - imag_coef * vector[1],
            real_coef * vector[1] + imag_coef * vector[0],
        ]
    )


def neighbours(last_rows, first_rows):
    count = lax.axis_size(both)
    forward = [(i, i + 1) for i in range(count - 1)]
    backward = [(target, source) for source, target in forward]
    return lax.ppermute(last_rows, both, forward), lax.ppermute(first_rows, both, backward)


def outer_apply(extended, potential, laser_mix, moved):
    points = extended.shape[1] - 4
    far_left = extended[:, 0:points]
    near_left = extended[:, 1 : points + 1]
    centre_row = extended[:, 2 : points + 2]
    near_right = extended[:, 3 : points + 3]
    far_right = extended[:, 4 : points + 4]
    laplace = -far_left + 16.0 * near_left - 30.0 * centre_row + 16.0 * near_right - far_right
    slope_rows = slope_coef * (far_left - 8.0 * near_left + 8.0 * near_right - far_right)
    mixed_slope = jnp.einsum("prc,cd->prd", slope_rows, laser_mix, precision=highest)
    return (
        kinetic_coef * laplace
        + (potential - moved) * centre_row
        + jnp.stack([mixed_slope[1], -mixed_slope[0]])
    )


def inner_windows(shards, own_partners, own_offsets):
    windows = []
    for couple_index in range(own_partners.shape[0]):
        source = lax.dynamic_index_in_dim(shards, own_partners[couple_index], 0, keepdims=False)
        source = source.transpose(1, 0, 2).reshape(2, -1)
        band_width = source.shape[1] // 2
        windows.append(
            lax.dynamic_slice_in_dim(source, own_offsets[couple_index] + band_width, band_width, 1)
        )
    return windows


def exchange(inner_vec, ghost_part, row):
    rows = inner_vec.shape[1]
    blocks, strips = lax.axis_size("rad"), lax.axis_size("chan")
    chunk = jnp.concatenate(
        [
            inner_vec,
            ghost_part.reshape(-1, rows),
            row.reshape(-1, rows),
            jnp.zeros((2, rows), jnp.float32),
        ],
        axis=0,
    )
    got = lax.all_to_all(jnp.broadcast_to(chunk, (strips,) + chunk.shape), "chan", 0, 0)
    own = got[:, 0:2]
    ghost_sum = jnp.sum(got[:, 2:10], axis=0)
    padded = jnp.pad(own, ((2, 1), (0, 0), (0, 0)))
    near = lax.dynamic_slice_in_dim(padded, lax.axis_index("chan"), 4, 0)
    chunk = jnp.concatenate(
        [near.reshape(8, rows), ghost_sum, got[0, 10:14], jnp.zeros((4, rows), jnp.float32)],
        axis=0,
    )
    got_blocks = lax.all_to_all(jnp.broadcast_to(chunk, (blocks,) + chunk.shape), "rad", 0, 0)
    shards = got_blocks[:, 0:8].reshape(blocks, 4, 2, rows)
    ghost = jnp.sum(got_blocks[:, 8:16], axis=0).reshape(2, 2, -1)
    first_row = got_blocks[0, 16:20].reshape(2, -1)
    return own.transpose(1, 0, 2).reshape(2, -1), shards, ghost, first_row


def step_by_step(
    inner_state,
    outer_state,
    inner_ham,
    inner_coupling,
    surface_amp,
    potential,
    laser_mix,
    partners,
    band_offsets,
    channel_group,
):
    block_order = inner_ham.shape[1]
    points, channels = outer_state.shape[1:]
    entries = float(
        lax.axis_size("rad") * block_order + lax.axis_size(both) * points * channels
    )
    block_index = lax.axis_index("rad")
    is_first = lax.axis_index(both) == 0
    member = (channel_group == block_index).astype(jnp.float32)
    masked_amp = surface_amp[0] * member[None, None, :]
    own_partners = lax.dynamic_index_in_dim(partners, block_index, 0, keepdims=False)
    own_offsets = lax.dynamic_index_in_dim(band_offsets, block_index, 0, keepdims=False)

    def total(value):
        return lax.psum(value, both) / entries

    def squares(vector):
        return jnp.sum(vector[0] * vector[0]) + jnp.sum(vector[1] * vector[1])

    start_len = jnp.sqrt(total(squares((inner_state, outer_state))))
    krylov = [(inner_state / start_len, outer_state / start_len)]
    hessenberg = jnp.zeros((2, TERMS + 1, TERMS), jnp.float32)
    for term_index in range(TERMS):
        inner_vec, outer_vec = krylov[term_index]
        ghost_part = jnp.einsum("pk,mki->pmi", inner_vec, masked_amp, precision=highest)
        row = jnp.where(is_first, outer_vec[:, 0], 0.0)
        own_vec, shards, ghost, first_row = exchange(inner_vec, ghost_part, row)
        result_in = jnp.dot(own_vec, inner_ham[0], precision=highest)
        for couple_index, window in enumerate(inner_windows(shards, own_partners, own_offsets)):
            result_in = result_in + jnp.dot(window, inner_coupling[0, couple_index], precision=highest)
        result_in = result_in + bloch_coef * jnp.einsum(
            "pi,ki->pk", first_row, masked_amp[0], precision=highest
        )
        low, high = neighbours(outer_vec[:, points - 2 :], outer_vec[:, :2])
        low = jnp.where(is_first, ghost[:, ::-1], low)
        extended = jnp.concatenate([low, outer_vec, high], axis=1)
        image = (result_in, outer_apply(extended, potential, laser_mix, 0.0))
        for prior_index in range(term_index + 1):
            prior = krylov[prior_index]
            coefs = total(local_parts(prior, image))
            image = tuple(
                part - rotate(prior_part, coefs[0], coefs[1])
                for part, prior_part in zip(image, prior)
            )
            hessenberg = hessenberg.at[:, prior_index, term_index].set(coefs)
        new_length = jnp.sqrt(total(squares(image)))
        hessenberg = hessenberg.at[0, term_index + 1, term_index].set(new_length)
        krylov.append((image[0] / new_length, image[1] / new_length))
    return (krylov[-1][0], krylov[-1][1], hessenberg)


lanes = 128
margin = 8
reach = 2
vmem_bytes = 16 * 2**20


def whole():
    return pl.BlockSpec(memory_space=pltpu.VMEM)


def anywhere():
    return pl.BlockSpec(memory_space=pl.ANY)


def far():
    return pl.BlockSpec(memory_space=pltpu.HBM)


def in_one(shape):
    return pl.BlockSpec(shape, lambda i: (0,) * len(shape))


def scalars():
    return pl.BlockSpec(memory_space=pltpu.SMEM)


def run(kernel, outs, args, in_specs, scratch=()):
    return pl.pallas_call(
        kernel,
        out_shape=[jax.ShapeDtypeStruct(*out) if isinstance(out[0], tuple) else jax.ShapeDtypeStruct(out, jnp.float32) for out in outs],
        in_specs=in_specs,
        out_specs=[whole()] * len(outs),
        scratch_shapes=list(scratch),
        compiler_params=pltpu.CompilerParams(vmem_limit_bytes=vmem_bytes),
    )(*args)


def two(x):
    high = x.astype(jnp.bfloat16)
    return high, (x - high.astype(jnp.float32)).astype(jnp.bfloat16)


def both_halves(x):
    high, low = two(x)
    rest = jnp.zeros((16 - 2 * x.shape[0], x.shape[1]), jnp.float32)
    return jnp.concatenate([high.astype(jnp.float32), low.astype(jnp.float32), rest], axis=0).astype(jnp.bfloat16)


def few_rows_dot(x, weights, flipped=False):
    rows = x.shape[0]
    lhs = both_halves(x)
    dims = (((1,), (1 if flipped else 0,)), ((), ()))
    total = sum(lax.dot_general(lhs, part, dims, preferred_element_type=jnp.float32) for part in weights)
    return total[:rows] + total[rows : 2 * rows]


def mixed_with(high, low, mix_ref):
    count = high.shape[0]
    first = jnp.dot(jnp.concatenate([high, low], axis=0), mix_ref[0], preferred_element_type=jnp.float32)
    return first[:count] + first[count:] + jnp.dot(high, mix_ref[1], preferred_element_type=jnp.float32)


def write_chunk(out_ref, inner_vec, ghosts, row, held_ref=None, written=None):
    half = inner_vec.shape[1]
    chunk = jnp.concatenate(
        [
            ghosts[:, :half],
            ghosts[:, half:],
            inner_vec,
            row[:, :half],
            row[:, half:],
            jnp.zeros((2, half), jnp.float32),
        ],
        axis=0,
    )
    if held_ref is None:
        for strip in range(out_ref.shape[0]):
            out_ref[strip, 0:16] = chunk
        return []
    held_ref[...] = chunk
    copies = [
        pltpu.make_async_copy(held_ref, out_ref.at[strip, pl.ds(0, 16)], written.at[strip])
        for strip in range(out_ref.shape[0])
    ]
    for copy in copies:
        copy.start()
    return copies


def ghost_rows(inner_vec, amps, member):
    return jnp.concatenate([few_rows_dot(inner_vec, amp) * member for amp in amps], axis=0)


def member_of(group_ref):
    return jnp.where(group_ref[...] == lax.axis_index("rad"), 1.0, 0.0)


def at_first():
    return (lax.axis_index("rad") == 0) & (lax.axis_index("chan") == 0)


def at_last():
    last = [lax.axis_index(axis) == lax.axis_size(axis) - 1 for axis in both]
    return last[0] & last[1]


def send_ends(out_ref, first_rows, last_rows, held_ref=None, written=None):
    strips, _, half = out_ref.shape
    copies = []
    for end, (there, points) in enumerate(((1, last_rows), (strips - 1, first_rows))):
        both_parts = jnp.concatenate(points, axis=0)
        rows = jnp.concatenate([both_parts[:, :half], both_parts[:, half:]], axis=0)
        strip = lax.rem(lax.axis_index("chan") + there, strips)
        if held_ref is None:
            out_ref[strip, 16:24] = rows
        else:
            held_ref[end] = rows
            copies.append(pltpu.make_async_copy(held_ref.at[end], out_ref.at[strip, pl.ds(16, 8)], written.at[end]))
            copies[-1].start()
    return copies


def start_kernel(inner_ref, head_ref, tail_ref, amp_ref, group_ref, chunk_ref):
    send_ends(chunk_ref, [head_ref[part, 0:2] for part in range(2)], [tail_ref[part, 6:8] for part in range(2)])
    row = jnp.concatenate([head_ref[part, 0:1] for part in range(2)], axis=0)
    row = jnp.where(at_first(), row, 0.0)
    inner_vec = inner_ref[...]
    amps = [two(amp_ref[0, radius]) for radius in range(2)]
    ghosts = ghost_rows(inner_vec, amps, member_of(group_ref))
    write_chunk(chunk_ref, inner_vec, ghosts, row)


def stencils(window, pot):
    before_2, before_1, here, after_1, after_2 = window
    local = (pot - (30.0 * kinetic_coef + shift)) * here + (
        16.0 * kinetic_coef * (before_1 + after_1) - kinetic_coef * (before_2 + after_2)
    )
    return local, (before_2 - after_2) + 8.0 * (after_1 - before_1)


def first_outer_kernel(
    state_ref, pot_ref, mix_ref, out_ref, mix_out, edges_ref, wide_ref, pot_wide, slope_h, slope_l
):
    points, channels = state_ref.shape[1:]
    strips = channels // lanes
    length = points // 8
    for strip in range(strips):
        here = slice(strip * lanes, (strip + 1) * lanes)
        for part in range(3):
            source = pot_ref if part == 2 else state_ref.at[part]
            target = pot_wide.at[strip] if part == 2 else wide_ref.at[part, strip]
            target[margin : margin + points] = source[:, here]
            target[0:margin] = jnp.zeros((margin, lanes), jnp.float32)
            target[margin + points :] = jnp.zeros((margin, lanes), jnp.float32)
    for part in range(3):
        source = pot_ref if part == 2 else state_ref.at[part]
        edges_ref[0, part], edges_ref[1, part] = source[0:8], source[points - 8 : points]

    def strip_step(step, _):
        part, strip = lax.div(step, strips), lax.rem(step, strips)

        def load(place):
            return wide_ref[part, strip, pl.ds(margin + place, 8, stride=length)]

        window = [load(place) for place in range(-2 * reach, 0)]
        columns = pl.ds(pl.multiple_of(strip * lanes, lanes), lanes)
        for first in range(-reach, length + reach, 2):
            slopes = []
            for place in (first, first + 1):
                window.append(load(place + reach))
                local, slope = stencils(window, pot_wide[strip, pl.ds(margin + place, 8, stride=length)])
                out_ref[part, strip, (place + reach) * 8 : (place + reach + 1) * 8] = local
                slopes.append(slope)
                window.pop(0)
            rows = slice((first + reach) * 8, (first + reach + 2) * 8)
            slope_h[part, rows, columns], slope_l[part, rows, columns] = two(jnp.concatenate(slopes, axis=0))
        return 0

    lax.fori_loop(0, 2 * strips, strip_step, 0)
    mix_out[0], mix_out[1] = two(slope_coef * mix_ref[...])
    add_mixed(out_ref, slope_h, slope_l, mix_out)


def add_mixed(out_ref, slope_h, slope_l, mix_ref):
    for part in range(2):
        mixed = mixed_with(slope_h[1 - part], slope_l[1 - part], mix_ref)
        for strip in range(out_ref.shape[1]):
            own = mixed[:, strip * lanes : (strip + 1) * lanes]
            out_ref[part, strip] = out_ref[part, strip] + (own if part == 0 else -own)


def products(s, p, q):
    return [
        s[0] * s[0] + s[1] * s[1],
        s[0] * p[0] + s[1] * p[1],
        s[0] * p[1] - s[1] * p[0],
        s[0] * q[0] + s[1] * q[1],
        s[0] * q[1] - s[1] * q[0],
        p[0] * p[0] + p[1] * p[1],
        p[0] * q[0] + p[1] * q[1],
        p[0] * q[1] - p[1] * q[0],
        q[0] * q[0] + q[1] * q[1],
    ]


def second_outer_kernel(
    patch_ref, wide_in, state_in, pot_in, mix_ref,
    wide_ref, q_out, notes_out, slope_h, slope_l, state_ref, pot_ref, out_ref, notes_ref, written,
):
    strips, places = out_ref.shape[1:3]
    length = places // 8
    for part in range(2):
        for strip in range(strips):
            here = slice(strip * lanes, (strip + 1) * lanes)
            wide_ref[part, strip, pl.ds(reach * 8, 2, stride=8)] = patch_ref[part, 0:2, here]
            wide_ref[part, strip, pl.ds(length * 8 + 7, 2, stride=8)] = patch_ref[part, 2:4, here]
    for strip in range(strips):
        here = slice(strip * lanes, (strip + 1) * lanes)
        pot_ref[strip] = pot_in[:, here]
        for part in range(2):
            state_ref[part, strip] = state_in[part, :, here]

    def strip_step(step, _):
        part, strip = lax.div(step, strips), lax.rem(step, strips)

        def load(place):
            return wide_ref[part, strip, (place + reach) * 8 : (place + reach + 1) * 8]

        window = [load(place) for place in range(-reach, reach)]
        columns = pl.ds(pl.multiple_of(strip * lanes, lanes), lanes)
        for first in range(0, length, 2):
            slopes = []
            for place in (first, first + 1):
                window.append(load(place + reach))
                local, slope = stencils(window, pot_ref[strip, pl.ds(place, 8, stride=length)])
                out_ref[part, strip, place * 8 : (place + 1) * 8] = local
                slopes.append(slope)
                window.pop(0)
            rows = slice(first * 8, (first + 2) * 8)
            slope_h[part, rows, columns], slope_l[part, rows, columns] = two(jnp.concatenate(slopes, axis=0))
        return 0

    lax.fori_loop(0, 2 * strips, strip_step, 0)
    add_mixed(out_ref, slope_h, slope_l, mix_ref)
    copy = pltpu.make_async_copy(out_ref, q_out, written.at[0])
    copy.start()
    run_of = lax.broadcasted_iota(jnp.int32, (8, lanes), 0)

    def gram_step(strip, sums):
        for place in range(length):
            entries = products(
                [state_ref[part, strip, pl.ds(place, 8, stride=length)] for part in range(2)],
                [wide_ref[part, strip, (place + reach) * 8 : (place + reach + 1) * 8] for part in range(2)],
                [out_ref[part, strip, place * 8 : (place + 1) * 8] for part in range(2)],
            )
            if place < 4 or place >= length - 4:
                inside = run_of > 0 if place < 4 else run_of < 7
                entries = [jnp.where(inside, entry, 0.0) for entry in entries]
            sums = [total + entry for total, entry in zip(sums, entries)]
        return sums

    sums = lax.fori_loop(0, strips, gram_step, [jnp.zeros((8, lanes), jnp.float32)] * 9)
    for k in range(9):
        notes_ref[k] = sums[k]
    for strip in range(strips):
        here = slice(strip * lanes, (strip + 1) * lanes)
        for end, rows in enumerate((slice(0, 8), slice(places - 8, places))):
            notes_ref[9 + strips * 3 * end + strip] = pot_in[rows, here]
            for part in range(2):
                notes_ref[9 + strips * (3 * end + part + 1) + strip] = state_in[part, rows, here]
    notes_copy = pltpu.make_async_copy(notes_ref, notes_out, written.at[1])
    notes_copy.start()
    copy.wait()
    notes_copy.wait()


def block_kernel(first, got_ref, ham_ref, out_ref, held_ref, arrived):
    rows = ham_ref.shape[2]
    pieces, size = held_ref.shape[:2]
    copies = [
        pltpu.make_async_copy(ham_ref.at[0, pl.ds((first + k) * size, size)], held_ref.at[k], arrived.at[k])
        for k in range(pieces)
    ]
    for copy in copies:
        copy.start()
    total = jnp.zeros((16, rows), jnp.float32)
    for k, copy in enumerate(copies):
        copy.wait()
        for part in range(size // rows):
            lhs = both_halves(got_ref[(first + k) * (size // rows) + part, 8:10])
            for weights in two(held_ref[k, part * rows : (part + 1) * rows]):
                total = total + jnp.dot(lhs, weights, preferred_element_type=jnp.float32)
    out_ref[...] = total[0:2] + total[2:4]


def chip_index():
    return lax.div(lax.axis_index("rad"), 2)


def core_index():
    return lax.rem(lax.axis_index("rad"), 2)


def gather_kernel(got_ref, after_ref, out_ref, kept_ref, ends_ref):
    strips = got_ref.shape[0]
    own = lax.axis_index("chan")
    for k in range(4):
        strip = own + (k - 2)
        there = (strip >= 0) & (strip < strips)
        near = got_ref[jnp.clip(strip, 0, strips - 1), 8:10]
        out_ref[2 * k : 2 * k + 2] = jnp.where(there, near, 0.0)
    kept_ref[0:8] = sum(got_ref[strip, 0:8] for strip in range(strips))
    kept_ref[8:12] = got_ref[0, 10:14]
    kept_ref[12:16] = jnp.zeros((4, got_ref.shape[2]), jnp.float32)
    out_ref[8:16] = jnp.where(chip_index() == 0, kept_ref[8:16], kept_ref[0:8])
    before = got_ref[lax.rem(own + strips - 1, strips), 16:24]
    after = got_ref[lax.rem(own + 1, strips), 16:24]
    ends_ref[0], ends_ref[1] = before, after
    out_ref[16:24] = jnp.where(own == 0, before, after)


def joined(kept_ref, came, add_ghosts, take_row):
    ghosts = kept_ref[0:8] + jnp.where(add_ghosts, came, 0.0)
    return ghosts, jnp.where(take_row, came, kept_ref[8:16])


def join_kernel(mine_ref, other_ref, kept_ref, after_ref, out_ref, kept_out):
    chip = chip_index()
    out_ref[0:8], out_ref[8:16] = mine_ref[0:8], other_ref[0:8]
    ghosts, row = joined(kept_ref, other_ref[8:16], (chip == 0) | (chip == 3), chip == 1)
    kept_out[0:8], kept_out[8:16] = ghosts, row
    out_ref[16:24] = jnp.where(chip <= 1, row, ghosts)
    out_ref[24:32] = mine_ref[16:24]


def last_join_kernel(mine_ref, other_ref, kept_ref, near_ref, after_ref, out_ref, kept_out):
    chip, core = chip_index(), core_index()
    out_ref[0:16], out_ref[16:32] = mine_ref[0:16], other_ref[0:16]
    ghosts, row = joined(kept_ref, other_ref[16:24], chip == 0, chip >= 2)
    kept_out[0:8], kept_out[8:16] = ghosts, row
    out_ref[32:40] = jnp.where(core == 0, row, ghosts)
    is_low = lax.axis_index("chan") == 0
    from_own = (core == 0) == is_low
    from_near = (lax.rem(chip, 2) == 1) == is_low
    out_ref[40:48] = jnp.where(from_own, mine_ref[24:32], jnp.where(from_near, near_ref[16:24], other_ref[24:32]))


def join(kernel, count, *args):
    width = args[0].shape[1]
    return run(kernel, [(count, width), (16, width)], args, [whole()] * (len(args) - 1) + [anywhere()])


def inner_result(partners_ref, offsets_ref, block_a, block_b, inner_ref, mine_ref, other_ref, coupling_ref, amp_ref, member, row):
    result = block_a[...] + block_b[...] - shift * inner_ref[...]
    couplings, _, band_width = coupling_ref.shape[:3]
    block_index = lax.axis_index("rad")
    for couple_index in range(couplings):
        apart = partners_ref[couple_index, block_index] ^ block_index
        far_pair = lax.shift_right_logical(apart, 2)
        slot = 4 * (apart & 1) + lax.shift_right_logical(apart ^ (2 * far_pair), 1)
        rows = pl.ds(pl.multiple_of(lax.rem(slot, 4) * 8, 8), 8)
        near = jnp.where(slot < 4, mine_ref[rows], other_ref[rows])
        near = jnp.concatenate([near[2 * k : 2 * k + 2] for k in range(4)], axis=1)
        near = jnp.concatenate([near, jnp.zeros((6, near.shape[1]), jnp.float32)], axis=0)
        first = offsets_ref[couple_index, block_index] + band_width
        window = pltpu.roll(near, near.shape[1] - first, 1)[0:2, :band_width]
        result = result + few_rows_dot(window, [coupling_ref[couple_index, part] for part in range(2)])
    return result + bloch_coef * few_rows_dot(row * member, [amp_ref[0, part] for part in range(2)], flipped=True)


def unpacked(kept_ref, other_ref):
    ghosts, row = joined(kept_ref, other_ref[32:40], True, core_index() == 1)
    return jnp.concatenate([ghosts[0:4], ghosts[4:8]], axis=1), jnp.concatenate([row[0:2], row[2:4]], axis=1)


def points_of(ref, part, first, count, run_index=0):
    return jnp.concatenate(
        [ref[part, strip, pl.ds(first * 8 + run_index, count, stride=8)] for strip in range(ref.shape[1])], axis=1
    )


def mend(edge_ref, pots, mix_ref, more=None):
    local, slopes = [], []
    for part in range(2):
        for end in range(2):
            inner, slope = stencils([edge_ref[part, end, 8 + k : 16 + k] for k in range(-reach, reach + 1)], pots[end])
            local.append(inner)
            slopes.append(slope)
    mixed = mixed_with(*two(jnp.concatenate(slopes + ([] if more is None else [more]), axis=0)), mix_ref)
    image = [
        [
            local[2 * part + end] + (mixed[16 + 8 * end : 24 + 8 * end] if part == 0 else -mixed[8 * end : 8 * end + 8])
            for end in range(2)
        ]
        for part in range(2)
    ]
    return image, mixed[32:]


def pick_ends(ends_ref, other_ref):
    strip = lax.axis_index("chan")
    is_low, is_high = strip == 0, strip == lax.axis_size("chan") - 1
    came = other_ref[40:48]
    before = jnp.where(at_first(), 0.0, jnp.where(is_low, came, ends_ref[0]))
    after = jnp.where(at_last(), 0.0, jnp.where(is_high, came, ends_ref[1]))
    return [
        [jnp.concatenate([x[2 * part : 2 * part + 2], x[4 + 2 * part : 6 + 2 * part]], axis=1) for part in range(2)]
        for x in (before, after)
    ]


def between_kernel(
    partners_ref, offsets_ref, block_a, block_b, inner_ref, mine_ref, other_ref, coupling_ref, amp_ref, group_ref,
    edges_ref, mix_ref, ends_ref, kept_ref,
    image_ref, chunk_ref, patch_out, held_ref, written, ends_held, ends_written, patch_ref, patch_written, edge_ref,
):
    member = member_of(group_ref)
    ghosts, row = unpacked(kept_ref, other_ref)
    before, after = pick_ends(ends_ref, other_ref)
    edge_ref[...] = jnp.zeros_like(edge_ref)
    for part in range(2):
        edge_ref[part, 0, 6:8] = before[part]
        edge_ref[part, 1, 16:18] = after[part]
        for end in range(2):
            edge_ref[part, end, 8:16] = edges_ref[end, part]
    near, far_off = ghosts[0:2], ghosts[2:4]
    kinetic = [kinetic_coef * (16.0 * near - far_off), -kinetic_coef * near]
    slope = jnp.concatenate([far_off - 8.0 * near, near, jnp.zeros((12, near.shape[1]), jnp.float32)], axis=0)
    p, mixed = mend(edge_ref, [edges_ref[end, 2] for end in range(2)], mix_ref, slope)
    first_rows, last_rows = [], []
    for part in range(2):
        extra = jnp.concatenate(
            [
                kinetic[k][part : part + 1]
                + (mixed[2 * k + 1 : 2 * k + 2] if part == 0 else -mixed[2 * k : 2 * k + 1])
                for k in range(2)
            ],
            axis=0,
        )
        first_rows.append(p[part][0][0:2] + jnp.where(at_first(), extra, 0.0))
        last_rows.append(p[part][1][6:8])
        patch_ref[part] = jnp.concatenate(
            [first_rows[part], last_rows[part], jnp.zeros((4, near.shape[1]), jnp.float32)], axis=0
        )
    image = inner_result(
        partners_ref, offsets_ref, block_a, block_b, inner_ref, mine_ref, other_ref, coupling_ref, amp_ref, member, row
    )
    image_ref[...] = image
    row = jnp.where(at_first(), jnp.concatenate([rows[0:1] for rows in first_rows], axis=0), 0.0)
    amps = [[amp_ref[radius, part] for part in range(2)] for radius in range(2)]
    copies = write_chunk(chunk_ref, image, ghost_rows(image, amps, member), row, held_ref, written)
    copies += send_ends(chunk_ref, first_rows, last_rows, ends_held, ends_written)
    copies.append(pltpu.make_async_copy(patch_ref, patch_out, patch_written))
    copies[-1].start()
    for copy in copies:
        copy.wait()


def last_kernel(
    partners_ref, offsets_ref, block_a, block_b, inner_ref, mine_ref, other_ref, coupling_ref, amp_ref, group_ref,
    wide_ref, mix_ref, ends_ref, kept_ref, start_ref, second_ref, notes_ref,
    image_ref, out_ref, parts_ref, edge_ref,
):
    member = member_of(group_ref)
    ghosts, row = unpacked(kept_ref, other_ref)
    image = inner_result(
        partners_ref, offsets_ref, block_a, block_b, inner_ref, mine_ref, other_ref, coupling_ref, amp_ref, member, row
    )
    image_ref[...] = image
    strips = wide_ref.shape[1]
    length = second_ref.shape[2] // 8
    noted = [
        [
            jnp.concatenate([notes_ref[9 + strips * (3 * end + k) + strip] for strip in range(strips)], axis=1)
            for k in range(3)
        ]
        for end in range(2)
    ]
    before, after = pick_ends(ends_ref, other_ref)
    edge_ref[...] = jnp.zeros_like(edge_ref)
    for part in range(2):
        ghost = jnp.concatenate([ghosts[2 + part : 3 + part], ghosts[part : part + 1]], axis=0)
        edge_ref[part, 0, 6:8] = jnp.where(at_first(), ghost, before[part])
        edge_ref[part, 0, 8:24] = points_of(wide_ref, part, reach, 16)
        edge_ref[part, 1, 0:16] = points_of(wide_ref, part, length + reach - 16, 16, 7)
        edge_ref[part, 1, 16:18] = after[part]
    q, _ = mend(edge_ref, [noted[end][0] for end in range(2)], mix_ref)
    row_of = lax.broadcasted_iota(jnp.int32, q[0][0].shape, 0)
    mended = [row_of < 4, row_of >= 4]
    totals = [notes_ref[k] for k in range(9)]
    for end in range(2):
        for part in range(2):
            there = points_of(second_ref, part, 0 if end == 0 else length - 8, 8, 7 * end)
            q[part][end] = jnp.where(mended[end], q[part][end], there)
            out_ref[end, part] = q[part][end]
        entries = products(noted[end][1:], [edge_ref[part, end, 8:16] for part in range(2)], [q[part][end] for part in range(2)])
        for k, entry in enumerate(entries):
            entry = jnp.where(mended[end], entry, 0.0)
            totals[k] = totals[k] + sum(entry[:, strip * lanes : (strip + 1) * lanes] for strip in range(strips))
    start, inner = start_ref[...], inner_ref[...]
    inside = products([start[0:1], start[1:2]], [inner[0:1], inner[1:2]], [image[0:1], image[1:2]])
    lane = lax.broadcasted_iota(jnp.int32, (1, lanes), 1)
    sums = jnp.zeros((1, lanes), jnp.float32)
    for k in range(9):
        line = jnp.sum(totals[k], axis=0, keepdims=True) + inside[k][:, :lanes] + inside[k][:, lanes:]
        sums = jnp.where(lane == k, jnp.sum(line, axis=1, keepdims=True), sums)
    parts_ref[...] = jnp.broadcast_to(sums, parts_ref.shape)


def arnoldi_coefs(gram):
    ss, spr, spi, sqr, sqi, pp, pqr, pqi, qq = gram
    cr, ci = spr / ss, spi / ss
    left_1 = pp - (spr * cr + spi * ci)
    h10 = jnp.sqrt(left_1 / ss)
    sxr = sqr - (cr * spr - ci * spi)
    sxi = sqi - (cr * spi + ci * spr)
    h01r, h01i = sxr / (ss * h10), sxi / (ss * h10)
    pxr, pxi = pqr - cr * pp, pqi - ci * pp
    yxr = pxr - (cr * sxr + ci * sxi)
    yxi = pxi - (cr * sxi - ci * sxr)
    scale = 1.0 / left_1
    h11r, h11i = yxr * scale, yxi * scale
    xx = (qq - 2.0 * (cr * pqr + ci * pqi) + (cr * cr + ci * ci) * pp) * scale
    left_2 = xx - (h01r * h01r + h01i * h01i) - (h11r * h11r + h11i * h11i)
    h21 = jnp.sqrt(left_2)
    fine = (left_1 > least_left * pp) & (left_2 > least_left * xx)
    poor = jnp.where(fine, 0.0, 1.0)
    zero = jnp.zeros_like(ss)
    entries = [[[cr + shift, h10, zero], [h01r, h11r + shift, h21]], [[ci, zero, zero], [h01i, h11i, zero]]]
    a = jnp.sqrt(ss)
    coef_q = 1.0 / (a * h10 * h21)
    coef_p = (-(cr + h11r) * coef_q, -(ci + h11i) * coef_q)
    coef_s = (
        (h11r * cr - h11i * ci) * coef_q - h01r / (a * h21),
        (h11r * ci + h11i * cr) * coef_q - h01i / (a * h21),
    )
    return entries, (coef_q, coef_p, coef_s), poor


def combined(coefs, s, p, q):
    coef_q, coef_p, coef_s = coefs
    return (
        coef_q * q[0] + coef_p[0] * p[0] - coef_p[1] * p[1] + coef_s[0] * s[0] - coef_s[1] * s[1],
        coef_q * q[1] + coef_p[0] * p[1] + coef_p[1] * p[0] + coef_s[0] * s[1] + coef_s[1] * s[0],
    )


def finish_kernel(
    entries, parts_ref, start_ref, inner_ref, image_ref, state_ref, wide_ref, second_ref, edge_ref,
    inner_out, result_out, hess_out, poor_out, outer_out, written,
):
    strips, places = second_ref.shape[1:3]
    length = places // 8
    sums = jnp.sum(parts_ref[...], axis=0, keepdims=True) * (1.0 / entries)
    lane = lax.broadcasted_iota(jnp.int32, sums.shape, 1)
    gram = [jnp.sum(jnp.where(lane == k, sums, 0.0), axis=1, keepdims=True) for k in range(9)]
    values, (coef_q, coef_p, coef_s), poor = arnoldi_coefs(gram)
    tile = lambda coef: jnp.broadcast_to(coef, (8, lanes))
    coefs = tile(coef_q), [tile(coef) for coef in coef_p], [tile(coef) for coef in coef_s]

    def put(rows, p_first, q_first, run_index, edge=None):
        for strip in range(strips):
            here = slice(strip * lanes, (strip + 1) * lanes)
            result = combined(
                coefs,
                [state_ref[part, rows, here] for part in range(2)],
                [wide_ref[part, strip, pl.ds(p_first * 8 + run_index, 8, stride=8)] for part in range(2)],
                [
                    second_ref[part, strip, pl.ds(q_first * 8 + run_index, 8, stride=8)]
                    if edge is None
                    else edge_ref[edge, part, :, here]
                    for part in range(2)
                ],
            )
            for part in range(2):
                outer_out[part, rows, here] = result[part]

    copies = []
    for run_index in range(8):
        for first in range(0, length, 8):
            row = run_index * length + first
            edge = 0 if row == 0 else 1 if row == places - 8 else None
            put(slice(row, row + 8), first + reach, first, run_index, edge)
        rows = pl.ds(run_index * length, length)
        copies.append(
            pltpu.make_async_copy(outer_out.at[:, rows], result_out.at[:, rows], written.at[run_index])
        )
        copies[-1].start()
    for first in range(0, inner_out.shape[1], lanes):
        here = slice(first, first + lanes)
        result = combined(
            [coefs[0][0:1], [c[0:1] for c in coefs[1]], [c[0:1] for c in coefs[2]]],
            *[[ref[0:1, here], ref[1:2, here]] for ref in (start_ref, inner_ref, image_ref)],
        )
        for part in range(2):
            inner_out[part : part + 1, here] = result[part]
    lane = lax.broadcasted_iota(jnp.int32, (1, TERMS + 1), 1)
    for part in range(2):
        for column in range(TERMS):
            line = jnp.zeros((1, TERMS + 1), jnp.float32)
            for k, value in enumerate(values[part][column]):
                line = jnp.where(lane == k, value, line)
            hess_out[part, column : column + 1] = line
    poor_out[...] = jnp.broadcast_to(poor, poor_out.shape)
    for copy in copies:
        copy.wait()


def weights_kernel(coupling_ref, amp_ref, after_ref, coupling_out, amp_out):
    for k in range(2):
        coupling_out[k, 0], coupling_out[k, 1] = two(coupling_ref[0, k])
        amp_out[k, 0], amp_out[k, 1] = two(amp_ref[0, k])


def same_kernel(in_ref, out_ref):
    out_ref[...] = in_ref[...]


def across_blocks(mine, kept, after):
    blocks = lax.axis_size("rad")
    last = blocks // 2 - 1
    near = lax.ppermute(mine, "rad", [(i, i ^ 2) for i in range(blocks)])
    mine, kept = join(join_kernel, 32, mine, near, kept, after[0])
    other = lax.ppermute(mine, "rad", [(i, 2 * (last - i // 2) + i % 2) for i in range(blocks)])
    mine, kept = join(last_join_kernel, 48, mine, other, kept, near, after[1])
    return mine, lax.ppermute(mine, "rad", [(i, i ^ 1) for i in range(blocks)]), kept


def body(*inputs):
    (
        inner_state,
        outer_state,
        inner_ham,
        inner_coupling,
        surface_amp,
        potential,
        laser_mix,
        partners,
        band_offsets,
        channel_group,
    ) = inputs
    block_order, rows = inner_ham.shape[1:]
    points, channels = outer_state.shape[1:]
    count = lax.axis_size(both)
    blocks, strips = lax.axis_size("rad"), lax.axis_size("chan")
    entries = float(blocks * block_order + count * points * channels)
    group = channel_group.reshape(1, channels)
    by_coupling = partners.T, band_offsets.T
    f32, bf16 = jnp.float32, jnp.bfloat16
    out_strips = channels // lanes
    folded_rows = points + 2 * reach * 8

    chunk = pl.pallas_call(
        start_kernel,
        grid=(1,),
        out_shape=jax.ShapeDtypeStruct((strips, 24, rows), f32),
        in_specs=[
            whole(),
            in_one((2, 8, channels)),
            pl.BlockSpec((2, 8, channels), lambda i: (0, points // 8 - 1, 0)),
            whole(),
            whole(),
        ],
        out_specs=whole(),
        compiler_params=pltpu.CompilerParams(vmem_limit_bytes=vmem_bytes),
    )(inner_state, outer_state, outer_state, surface_amp, group)
    got = lax.all_to_all(chunk, "chan", 0, 0)
    wide, mix, edges = pl.pallas_call(
        first_outer_kernel,
        out_shape=[
            jax.ShapeDtypeStruct((2, out_strips, folded_rows, lanes), f32),
            jax.ShapeDtypeStruct((2, channels, channels), bf16),
            jax.ShapeDtypeStruct((2, 3, 8, channels), f32),
        ],
        in_specs=[whole()] * 3,
        out_specs=[whole()] * 3,
        scratch_shapes=[
            pltpu.VMEM((2, out_strips, points + 2 * margin, lanes), f32),
            pltpu.VMEM((out_strips, points + 2 * margin, lanes), f32),
            pltpu.VMEM((2, folded_rows, channels), bf16),
            pltpu.VMEM((2, folded_rows, channels), bf16),
        ],
        compiler_params=pltpu.CompilerParams(vmem_limit_bytes=vmem_bytes),
    )(outer_state, potential, laser_mix)

    def block_product(got):
        size = 2 * rows
        parts = []
        for first, last in ((0, 4), (4, 8)):
            parts += run(
                lambda *refs, first=first: block_kernel(first, *refs),
                [(2, rows)],
                (got, pltpu.with_memory_space_constraint(inner_ham, pltpu.HBM)),
                [whole(), far()],
                [pltpu.VMEM((last - first, size, rows), f32), pltpu.SemaphoreType.DMA((last - first,))],
            )
        return parts

    def split_weights(after):
        return run(
            weights_kernel,
            [((2, 2) + inner_coupling.shape[2:], bf16), ((2, 2) + surface_amp.shape[2:], bf16)],
            (inner_coupling, surface_amp, after),
            [whole()] * 2 + [anywhere()],
        )

    gathered = [(24, rows), (16, rows), (2, 8, rows)]
    mine, kept, ends = run(gather_kernel, gathered, (got, wide), [whole(), anywhere()])
    block_parts = block_product(got)
    mine, other, kept = across_blocks(mine, kept, block_parts)
    coupling, amp = split_weights(mine)
    p_inner, chunk, patch = pl.pallas_call(
        between_kernel,
        out_shape=[
            jax.ShapeDtypeStruct((2, rows), f32),
            pltpu.HBM((strips, 24, rows), f32),
            pltpu.HBM((2, 8, channels), f32),
        ],
        in_specs=[scalars()] * 2 + [whole()] * 12,
        out_specs=[whole()] + [far()] * 2,
        scratch_shapes=[
            pltpu.VMEM((16, rows), f32),
            pltpu.SemaphoreType.DMA((strips,)),
            pltpu.VMEM((2, 8, rows), f32),
            pltpu.SemaphoreType.DMA((2,)),
        ]
        + [pltpu.VMEM((2, 8, channels), f32), pltpu.SemaphoreType.DMA, pltpu.VMEM((2, 2, 24, channels), f32)],
        compiler_params=pltpu.CompilerParams(vmem_limit_bytes=vmem_bytes),
    )(
        *by_coupling, *block_parts, inner_state, mine, other, coupling, amp, group,
        edges, mix, ends, kept,
    )
    got = lax.all_to_all(chunk, "chan", 0, 0)
    q_shape, notes_shape = (2, out_strips, points, lanes), (9 + 6 * out_strips, 8, lanes)
    wide, second, notes = pl.pallas_call(
        second_outer_kernel,
        grid=(1,),
        out_shape=[
            jax.ShapeDtypeStruct((2, out_strips, folded_rows, lanes), f32),
            pltpu.HBM(q_shape, f32),
            pltpu.HBM(notes_shape, f32),
        ],
        in_specs=[in_one((2, 8, channels))] + [whole()] * 4,
        out_specs=[whole(), far(), far()],
        scratch_shapes=[pltpu.VMEM((2, points, channels), bf16)] * 2
        + [
            pltpu.VMEM(q_shape, f32),
            pltpu.VMEM((out_strips, points, lanes), f32),
            pltpu.VMEM(q_shape, f32),
            pltpu.VMEM(notes_shape, f32),
            pltpu.SemaphoreType.DMA((2,)),
        ],
        input_output_aliases={1: 0},
        compiler_params=pltpu.CompilerParams(vmem_limit_bytes=vmem_bytes),
    )(pltpu.with_memory_space_constraint(patch, pltpu.HBM), wide, outer_state, potential, mix)
    mine, kept, ends = run(
        gather_kernel, gathered, (got, pltpu.with_memory_space_constraint(notes, pltpu.HBM)), [whole(), far()]
    )
    block_parts = block_product(got)
    mine, other, kept = across_blocks(mine, kept, block_parts)
    coupling, amp = split_weights(mine)
    q_inner, q_ends, parts = run(
        last_kernel,
        [(2, rows), (2, 2, 8, channels), (count, lanes)],
        (
            *by_coupling, *block_parts, p_inner, mine, other, coupling, amp, group,
            wide, mix, ends, kept, inner_state, second, notes,
        ),
        [scalars()] * 2 + [whole()] * 15,
        [pltpu.VMEM((2, 2, 24, channels), f32)],
    )
    parts = lax.all_to_all(parts.reshape(count, 1, lanes), both, 0, 0).reshape(count, lanes)
    last_inner, last_outer, columns, poor = pl.pallas_call(
        lambda *refs: finish_kernel(entries, *refs),
        out_shape=[
            jax.ShapeDtypeStruct((2, rows), f32),
            pltpu.HBM((2, points, channels), f32),
            jax.ShapeDtypeStruct((2, TERMS, TERMS + 1), f32),
            jax.ShapeDtypeStruct((1, lanes), f32),
        ],
        in_specs=[whole()] * 8,
        out_specs=[whole(), far(), whole(), whole()],
        scratch_shapes=[pltpu.VMEM((2, points, channels), f32), pltpu.SemaphoreType.DMA((8,))],
        compiler_params=pltpu.CompilerParams(vmem_limit_bytes=vmem_bytes),
    )(parts, inner_state, p_inner, q_inner, outer_state, wide, second, q_ends)

    def again(state):
        last_inner, last_outer, hessenberg = step_by_step(*inputs)
        columns = hessenberg.transpose(0, 2, 1)
        (columns,) = run(same_kernel, [columns.shape], (columns,), [whole()])
        return jnp.zeros((), f32), last_inner, last_outer, columns

    _, last_inner, last_outer, columns = lax.while_loop(
        lambda state: state[0] > 0.0, again, (poor[0, 0], last_inner, last_outer, columns)
    )
    return last_inner, last_outer, columns.transpose(0, 2, 1)


def solution(mesh):
    return jax.shard_map(
        body,
        mesh=mesh,
        in_specs=(
            P(None, ("rad", "chan")),
            P(None, ("rad", "chan"), None),
            P("rad", None, "chan"),
            P("rad", None, None, "chan"),
            P("rad", None, "chan", None),
            P(("rad", "chan"), None),
            P(),
            P(),
            P(),
            P(),
        ),
        out_specs=(P(None, ("rad", "chan")), P(None, ("rad", "chan"), None), P()),
        check_vma=False,
    )
```

```python
import jax
import jax.numpy as jnp
from jax import lax
from jax.experimental import pallas as pl
from jax.experimental.pallas import tpu as pltpu
from jax.sharding import PartitionSpec as P

STRIP = 256
TERMS = 2

highest = lax.Precision.HIGHEST
kinetic_coef = -0.5 * 0.05 / (12.0 * 0.25 * 0.25)
slope_coef = 1.0 / (12.0 * 0.25)
bloch_coef = 2.0
shift = 1.5
least_left = 0.1
both = ("rad", "chan")


def spread(block, axis, holder):
    block = jnp.where(lax.axis_index(axis) == holder, block, jnp.zeros_like(block))
    return lax.psum(block, axis)


def local_parts(left, right):
    real_part = jnp.sum(left[0] * right[0]) + jnp.sum(left[1] * right[1])
    imag_part = jnp.sum(left[0][0] * right[0][1] - left[0][1] * right[0][0]) + jnp.sum(
        left[1][0] * right[1][1] - left[1][1] * right[1][0]
    )
    return jnp.stack([real_part, imag_part])


def rotate(vector, real_coef, imag_coef):
    return jnp.stack(
        [
            real_coef * vector[0] - imag_coef * vector[1],
            real_coef * vector[1] + imag_coef * vector[0],
        ]
    )


def neighbours(last_rows, first_rows):
    count = lax.axis_size(both)
    forward = [(i, i + 1) for i in range(count - 1)]
    backward = [(target, source) for source, target in forward]
    return lax.ppermute(last_rows, both, forward), lax.ppermute(first_rows, both, backward)


def outer_apply(extended, potential, laser_mix, moved):
    points = extended.shape[1] - 4
    far_left = extended[:, 0:points]
    near_left = extended[:, 1 : points + 1]
    centre_row = extended[:, 2 : points + 2]
    near_right = extended[:, 3 : points + 3]
    far_right = extended[:, 4 : points + 4]
    laplace = -far_left + 16.0 * near_left - 30.0 * centre_row + 16.0 * near_right - far_right
    slope_rows = slope_coef * (far_left - 8.0 * near_left + 8.0 * near_right - far_right)
    mixed_slope = jnp.einsum("prc,cd->prd", slope_rows, laser_mix, precision=highest)
    return (
        kinetic_coef * laplace
        + (potential - moved) * centre_row
        + jnp.stack([mixed_slope[1], -mixed_slope[0]])
    )


def inner_windows(shards, own_partners, own_offsets):
    windows = []
    for couple_index in range(own_partners.shape[0]):
        source = lax.dynamic_index_in_dim(shards, own_partners[couple_index], 0, keepdims=False)
        source = source.transpose(1, 0, 2).reshape(2, -1)
        band_width = source.shape[1] // 2
        windows.append(
            lax.dynamic_slice_in_dim(source, own_offsets[couple_index] + band_width, band_width, 1)
        )
    return windows


def exchange(inner_vec, ghost_part, row):
    rows = inner_vec.shape[1]
    blocks, strips = lax.axis_size("rad"), lax.axis_size("chan")
    chunk = jnp.concatenate(
        [
            inner_vec,
            ghost_part.reshape(-1, rows),
            row.reshape(-1, rows),
            jnp.zeros((2, rows), jnp.float32),
        ],
        axis=0,
    )
    got = lax.all_to_all(jnp.broadcast_to(chunk, (strips,) + chunk.shape), "chan", 0, 0)
    own = got[:, 0:2]
    ghost_sum = jnp.sum(got[:, 2:10], axis=0)
    padded = jnp.pad(own, ((2, 1), (0, 0), (0, 0)))
    near = lax.dynamic_slice_in_dim(padded, lax.axis_index("chan"), 4, 0)
    chunk = jnp.concatenate(
        [near.reshape(8, rows), ghost_sum, got[0, 10:14], jnp.zeros((4, rows), jnp.float32)],
        axis=0,
    )
    got_blocks = lax.all_to_all(jnp.broadcast_to(chunk, (blocks,) + chunk.shape), "rad", 0, 0)
    shards = got_blocks[:, 0:8].reshape(blocks, 4, 2, rows)
    ghost = jnp.sum(got_blocks[:, 8:16], axis=0).reshape(2, 2, -1)
    first_row = got_blocks[0, 16:20].reshape(2, -1)
    return own.transpose(1, 0, 2).reshape(2, -1), shards, ghost, first_row


def step_by_step(
    inner_state,
    outer_state,
    inner_ham,
    inner_coupling,
    surface_amp,
    potential,
    laser_mix,
    partners,
    band_offsets,
    channel_group,
):
    block_order = inner_ham.shape[1]
    points, channels = outer_state.shape[1:]
    entries = float(
        lax.axis_size("rad") * block_order + lax.axis_size(both) * points * channels
    )
    block_index = lax.axis_index("rad")
    is_first = lax.axis_index(both) == 0
    member = (channel_group == block_index).astype(jnp.float32)
    masked_amp = surface_amp[0] * member[None, None, :]
    own_partners = lax.dynamic_index_in_dim(partners, block_index, 0, keepdims=False)
    own_offsets = lax.dynamic_index_in_dim(band_offsets, block_index, 0, keepdims=False)

    def total(value):
        return lax.psum(value, both) / entries

    def squares(vector):
        return jnp.sum(vector[0] * vector[0]) + jnp.sum(vector[1] * vector[1])

    start_len = jnp.sqrt(total(squares((inner_state, outer_state))))
    krylov = [(inner_state / start_len, outer_state / start_len)]
    hessenberg = jnp.zeros((2, TERMS + 1, TERMS), jnp.float32)
    for term_index in range(TERMS):
        inner_vec, outer_vec = krylov[term_index]
        ghost_part = jnp.einsum("pk,mki->pmi", inner_vec, masked_amp, precision=highest)
        row = jnp.where(is_first, outer_vec[:, 0], 0.0)
        own_vec, shards, ghost, first_row = exchange(inner_vec, ghost_part, row)
        result_in = jnp.dot(own_vec, inner_ham[0], precision=highest)
        for couple_index, window in enumerate(inner_windows(shards, own_partners, own_offsets)):
            result_in = result_in + jnp.dot(window, inner_coupling[0, couple_index], precision=highest)
        result_in = result_in + bloch_coef * jnp.einsum(
            "pi,ki->pk", first_row, masked_amp[0], precision=highest
        )
        low, high = neighbours(outer_vec[:, points - 2 :], outer_vec[:, :2])
        low = jnp.where(is_first, ghost[:, ::-1], low)
        extended = jnp.concatenate([low, outer_vec, high], axis=1)
        image = (result_in, outer_apply(extended, potential, laser_mix, 0.0))
        for prior_index in range(term_index + 1):
            prior = krylov[prior_index]
            coefs = total(local_parts(prior, image))
            image = tuple(
                part - rotate(prior_part, coefs[0], coefs[1])
                for part, prior_part in zip(image, prior)
            )
            hessenberg = hessenberg.at[:, prior_index, term_index].set(coefs)
        new_length = jnp.sqrt(total(squares(image)))
        hessenberg = hessenberg.at[0, term_index + 1, term_index].set(new_length)
        krylov.append((image[0] / new_length, image[1] / new_length))
    return (krylov[-1][0], krylov[-1][1], hessenberg)


lanes = 128
margin = 8
reach = 2
vmem_bytes = 16 * 2**20


def whole():
    return pl.BlockSpec(memory_space=pltpu.VMEM)


def anywhere():
    return pl.BlockSpec(memory_space=pl.ANY)


def far():
    return pl.BlockSpec(memory_space=pltpu.HBM)


def in_one(shape):
    return pl.BlockSpec(shape, lambda i: (0,) * len(shape))


def scalars():
    return pl.BlockSpec(memory_space=pltpu.SMEM)


def run(kernel, outs, args, in_specs, scratch=()):
    return pl.pallas_call(
        kernel,
        out_shape=[jax.ShapeDtypeStruct(*out) if isinstance(out[0], tuple) else jax.ShapeDtypeStruct(out, jnp.float32) for out in outs],
        in_specs=in_specs,
        out_specs=[whole()] * len(outs),
        scratch_shapes=list(scratch),
        compiler_params=pltpu.CompilerParams(vmem_limit_bytes=vmem_bytes),
    )(*args)


def two(x):
    high = x.astype(jnp.bfloat16)
    return high, (x - high.astype(jnp.float32)).astype(jnp.bfloat16)


def both_halves(x):
    high, low = two(x)
    rest = jnp.zeros((16 - 2 * x.shape[0], x.shape[1]), jnp.float32)
    return jnp.concatenate([high.astype(jnp.float32), low.astype(jnp.float32), rest], axis=0).astype(jnp.bfloat16)


def few_rows_dot(x, weights, flipped=False):
    rows = x.shape[0]
    lhs = both_halves(x)
    dims = (((1,), (1 if flipped else 0,)), ((), ()))
    total = sum(lax.dot_general(lhs, part, dims, preferred_element_type=jnp.float32) for part in weights)
    return total[:rows] + total[rows : 2 * rows]


def mixed_with(high, low, mix_ref):
    count = high.shape[0]
    first = jnp.dot(jnp.concatenate([high, low], axis=0), mix_ref[0], preferred_element_type=jnp.float32)
    return first[:count] + first[count:] + jnp.dot(high, mix_ref[1], preferred_element_type=jnp.float32)


def write_chunk(out_ref, inner_vec, ghosts, row, held_ref=None, written=None):
    half = inner_vec.shape[1]
    chunk = jnp.concatenate(
        [
            ghosts[:, :half],
            ghosts[:, half:],
            inner_vec,
            row[:, :half],
            row[:, half:],
            jnp.zeros((2, half), jnp.float32),
        ],
        axis=0,
    )
    if held_ref is None:
        for strip in range(out_ref.shape[0]):
            out_ref[strip, 0:16] = chunk
        return []
    few = held_ref.shape[0]
    for strip in range(few):
        held_ref[strip] = chunk
    copies = [
        pltpu.make_async_copy(held_ref, out_ref.at[pl.ds(k * few, few), pl.ds(0, 16)], written.at[k])
        for k in range(out_ref.shape[0] // few)
    ]
    for copy in copies:
        copy.start()
    return copies


def ghost_rows(inner_vec, amps, member):
    return jnp.concatenate([few_rows_dot(inner_vec, amp) * member for amp in amps], axis=0)


def member_of(group_ref):
    return jnp.where(group_ref[...] == lax.axis_index("rad"), 1.0, 0.0)


def at_first():
    return (lax.axis_index("rad") == 0) & (lax.axis_index("chan") == 0)


def at_last():
    last = [lax.axis_index(axis) == lax.axis_size(axis) - 1 for axis in both]
    return last[0] & last[1]


def send_ends(out_ref, first_rows, last_rows, held_ref=None, written=None):
    strips, _, half = out_ref.shape
    copies = []
    for end, (there, points) in enumerate(((1, last_rows), (strips - 1, first_rows))):
        both_parts = jnp.concatenate(points, axis=0)
        rows = jnp.concatenate([both_parts[:, :half], both_parts[:, half:]], axis=0)
        strip = lax.rem(lax.axis_index("chan") + there, strips)
        if held_ref is None:
            out_ref[strip, 16:24] = rows
        else:
            held_ref[end] = rows
            copies.append(pltpu.make_async_copy(held_ref.at[end], out_ref.at[strip, pl.ds(16, 8)], written.at[end]))
            copies[-1].start()
    return copies


def start_kernel(inner_ref, head_ref, tail_ref, amp_ref, group_ref, chunk_ref):
    send_ends(chunk_ref, [head_ref[part, 0:2] for part in range(2)], [tail_ref[part, 6:8] for part in range(2)])
    row = jnp.concatenate([head_ref[part, 0:1] for part in range(2)], axis=0)
    row = jnp.where(at_first(), row, 0.0)
    inner_vec = inner_ref[...]
    amps = [two(amp_ref[0, radius]) for radius in range(2)]
    ghosts = ghost_rows(inner_vec, amps, member_of(group_ref))
    write_chunk(chunk_ref, inner_vec, ghosts, row)


def stencils(window, pot):
    before_2, before_1, here, after_1, after_2 = window
    local = (pot - (30.0 * kinetic_coef + shift)) * here + (
        16.0 * kinetic_coef * (before_1 + after_1) - kinetic_coef * (before_2 + after_2)
    )
    return local, (before_2 - after_2) + 8.0 * (after_1 - before_1)


def first_outer_kernel(
    state_ref, pot_ref, mix_ref, out_ref, mix_out, edges_ref, wide_ref, pot_wide, slope_h, slope_l
):
    points, channels = state_ref.shape[1:]
    strips = channels // lanes
    length = points // 8
    for strip in range(strips):
        here = slice(strip * lanes, (strip + 1) * lanes)
        for part in range(3):
            source = pot_ref if part == 2 else state_ref.at[part]
            target = pot_wide.at[strip] if part == 2 else wide_ref.at[part, strip]
            target[margin : margin + points] = source[:, here]
            target[0:margin] = jnp.zeros((margin, lanes), jnp.float32)
            target[margin + points :] = jnp.zeros((margin, lanes), jnp.float32)
    for part in range(3):
        source = pot_ref if part == 2 else state_ref.at[part]
        edges_ref[0, part], edges_ref[1, part] = source[0:8], source[points - 8 : points]

    def strip_step(step, _):
        part, strip = lax.div(step, strips), lax.rem(step, strips)

        def load(place):
            return wide_ref[part, strip, pl.ds(margin + place, 8, stride=length)]

        window = [load(place) for place in range(-2 * reach, 0)]
        columns = pl.ds(pl.multiple_of(strip * lanes, lanes), lanes)
        for first in range(-reach, length + reach, 2):
            slopes = []
            for place in (first, first + 1):
                window.append(load(place + reach))
                local, slope = stencils(window, pot_wide[strip, pl.ds(margin + place, 8, stride=length)])
                out_ref[part, strip, (place + reach) * 8 : (place + reach + 1) * 8] = local
                slopes.append(slope)
                window.pop(0)
            rows = slice((first + reach) * 8, (first + reach + 2) * 8)
            slope_h[part, rows, columns], slope_l[part, rows, columns] = two(jnp.concatenate(slopes, axis=0))
        return 0

    lax.fori_loop(0, 2 * strips, strip_step, 0)
    mix_out[0], mix_out[1] = two(slope_coef * mix_ref[...])
    add_mixed(out_ref, slope_h, slope_l, mix_out)


def add_mixed(out_ref, slope_h, slope_l, mix_ref):
    for part in range(2):
        mixed = mixed_with(slope_h[1 - part], slope_l[1 - part], mix_ref)
        for strip in range(out_ref.shape[1]):
            own = mixed[:, strip * lanes : (strip + 1) * lanes]
            out_ref[part, strip] = out_ref[part, strip] + (own if part == 0 else -own)


def products(s, p, q):
    return [
        s[0] * s[0] + s[1] * s[1],
        s[0] * p[0] + s[1] * p[1],
        s[0] * p[1] - s[1] * p[0],
        s[0] * q[0] + s[1] * q[1],
        s[0] * q[1] - s[1] * q[0],
        p[0] * p[0] + p[1] * p[1],
        p[0] * q[0] + p[1] * q[1],
        p[0] * q[1] - p[1] * q[0],
        q[0] * q[0] + q[1] * q[1],
    ]


def second_outer_kernel(
    patch_ref, wide_in, state_in, pot_in, mix_ref,
    wide_ref, q_out, notes_out, slope_h, slope_l, state_ref, pot_ref, out_ref, notes_ref, written,
):
    strips, places = out_ref.shape[1:3]
    length = places // 8
    for part in range(2):
        for strip in range(strips):
            here = slice(strip * lanes, (strip + 1) * lanes)
            wide_ref[part, strip, pl.ds(reach * 8, 2, stride=8)] = patch_ref[part, 0:2, here]
            wide_ref[part, strip, pl.ds(length * 8 + 7, 2, stride=8)] = patch_ref[part, 2:4, here]
    for strip in range(strips):
        here = slice(strip * lanes, (strip + 1) * lanes)
        pot_ref[strip] = pot_in[:, here]
        for part in range(2):
            state_ref[part, strip] = state_in[part, :, here]

    def strip_step(step, _):
        part, strip = lax.div(step, strips), lax.rem(step, strips)

        def load(place):
            return wide_ref[part, strip, (place + reach) * 8 : (place + reach + 1) * 8]

        window = [load(place) for place in range(-reach, reach)]
        columns = pl.ds(pl.multiple_of(strip * lanes, lanes), lanes)
        for first in range(0, length, 2):
            slopes = []
            for place in (first, first + 1):
                window.append(load(place + reach))
                local, slope = stencils(window, pot_ref[strip, pl.ds(place, 8, stride=length)])
                out_ref[part, strip, place * 8 : (place + 1) * 8] = local
                slopes.append(slope)
                window.pop(0)
            rows = slice(first * 8, (first + 2) * 8)
            slope_h[part, rows, columns], slope_l[part, rows, columns] = two(jnp.concatenate(slopes, axis=0))
        return 0

    lax.fori_loop(0, 2 * strips, strip_step, 0)
    add_mixed(out_ref, slope_h, slope_l, mix_ref)
    copy = pltpu.make_async_copy(out_ref, q_out, written.at[0])
    copy.start()
    run_of = lax.broadcasted_iota(jnp.int32, (8, lanes), 0)

    def gram_step(strip, sums):
        for place in range(length):
            entries = products(
                [state_ref[part, strip, pl.ds(place, 8, stride=length)] for part in range(2)],
                [wide_ref[part, strip, (place + reach) * 8 : (place + reach + 1) * 8] for part in range(2)],
                [out_ref[part, strip, place * 8 : (place + 1) * 8] for part in range(2)],
            )
            if place < 4 or place >= length - 4:
                inside = run_of > 0 if place < 4 else run_of < 7
                entries = [jnp.where(inside, entry, 0.0) for entry in entries]
            sums = [total + entry for total, entry in zip(sums, entries)]
        return sums

    sums = lax.fori_loop(0, strips, gram_step, [jnp.zeros((8, lanes), jnp.float32)] * 9)
    for k in range(9):
        notes_ref[k] = sums[k]
    for strip in range(strips):
        here = slice(strip * lanes, (strip + 1) * lanes)
        for end, rows in enumerate((slice(0, 8), slice(places - 8, places))):
            notes_ref[9 + strips * 3 * end + strip] = pot_in[rows, here]
            for part in range(2):
                notes_ref[9 + strips * (3 * end + part + 1) + strip] = state_in[part, rows, here]
    notes_copy = pltpu.make_async_copy(notes_ref, notes_out, written.at[1])
    notes_copy.start()
    copy.wait()
    notes_copy.wait()


def block_kernel(first, got_ref, ham_ref, out_ref, held_ref, arrived):
    rows = ham_ref.shape[2]
    pieces, size = held_ref.shape[:2]
    copies = [
        pltpu.make_async_copy(ham_ref.at[0, pl.ds((first + k) * size, size)], held_ref.at[k], arrived.at[k])
        for k in range(pieces)
    ]
    for copy in copies:
        copy.start()
    total = jnp.zeros((16, rows), jnp.float32)
    for k, copy in enumerate(copies):
        copy.wait()
        for part in range(size // rows):
            lhs = both_halves(got_ref[(first + k) * (size // rows) + part, 8:10])
            for weights in two(held_ref[k, part * rows : (part + 1) * rows]):
                total = total + jnp.dot(lhs, weights, preferred_element_type=jnp.float32)
    out_ref[...] = total[0:2] + total[2:4]


def chip_index():
    return lax.div(lax.axis_index("rad"), 2)


def core_index():
    return lax.rem(lax.axis_index("rad"), 2)


def gather_kernel(got_ref, after_ref, out_ref, kept_ref, ends_ref):
    strips = got_ref.shape[0]
    own = lax.axis_index("chan")
    for k in range(4):
        strip = own + (k - 2)
        there = (strip >= 0) & (strip < strips)
        near = got_ref[jnp.clip(strip, 0, strips - 1), 8:10]
        out_ref[2 * k : 2 * k + 2] = jnp.where(there, near, 0.0)
    kept_ref[0:8] = sum(got_ref[strip, 0:8] for strip in range(strips))
    kept_ref[8:12] = got_ref[0, 10:14]
    kept_ref[12:16] = jnp.zeros((4, got_ref.shape[2]), jnp.float32)
    out_ref[8:16] = jnp.where(chip_index() == 0, kept_ref[8:16], kept_ref[0:8])
    before = got_ref[lax.rem(own + strips - 1, strips), 16:24]
    after = got_ref[lax.rem(own + 1, strips), 16:24]
    ends_ref[0], ends_ref[1] = before, after
    out_ref[16:24] = jnp.where(own == 0, before, after)


def joined(kept_ref, came, add_ghosts, take_row):
    ghosts = kept_ref[0:8] + jnp.where(add_ghosts, came, 0.0)
    return ghosts, jnp.where(take_row, came, kept_ref[8:16])


def join_kernel(mine_ref, other_ref, kept_ref, after_ref, out_ref, kept_out):
    chip = chip_index()
    out_ref[0:8], out_ref[8:16] = mine_ref[0:8], other_ref[0:8]
    ghosts, row = joined(kept_ref, other_ref[8:16], (chip == 0) | (chip == 3), chip == 1)
    kept_out[0:8], kept_out[8:16] = ghosts, row
    out_ref[16:24] = jnp.where(chip <= 1, row, ghosts)
    out_ref[24:32] = mine_ref[16:24]


def last_join_kernel(mine_ref, other_ref, kept_ref, near_ref, after_ref, out_ref, kept_out):
    chip, core = chip_index(), core_index()
    out_ref[0:16], out_ref[16:32] = mine_ref[0:16], other_ref[0:16]
    ghosts, row = joined(kept_ref, other_ref[16:24], chip == 0, chip >= 2)
    kept_out[0:8], kept_out[8:16] = ghosts, row
    out_ref[32:40] = jnp.where(core == 0, row, ghosts)
    is_low = lax.axis_index("chan") == 0
    from_own = (core == 0) == is_low
    from_near = (lax.rem(chip, 2) == 1) == is_low
    out_ref[40:48] = jnp.where(from_own, mine_ref[24:32], jnp.where(from_near, near_ref[16:24], other_ref[24:32]))


def join(kernel, count, *args):
    width = args[0].shape[1]
    return run(kernel, [(count, width), (16, width)], args, [whole()] * (len(args) - 1) + [anywhere()])


def inner_result(partners_ref, offsets_ref, block_a, block_b, inner_ref, mine_ref, other_ref, coupling_ref, amp_ref, member, row):
    result = block_a[...] + block_b[...] - shift * inner_ref[...]
    couplings, _, band_width = coupling_ref.shape[:3]
    block_index = lax.axis_index("rad")
    for couple_index in range(couplings):
        apart = partners_ref[couple_index, block_index] ^ block_index
        far_pair = lax.shift_right_logical(apart, 2)
        slot = 4 * (apart & 1) + lax.shift_right_logical(apart ^ (2 * far_pair), 1)
        rows = pl.ds(pl.multiple_of(lax.rem(slot, 4) * 8, 8), 8)
        near = jnp.where(slot < 4, mine_ref[rows], other_ref[rows])
        near = jnp.concatenate([near[2 * k : 2 * k + 2] for k in range(4)], axis=1)
        near = jnp.concatenate([near, jnp.zeros((6, near.shape[1]), jnp.float32)], axis=0)
        first = offsets_ref[couple_index, block_index] + band_width
        window = pltpu.roll(near, near.shape[1] - first, 1)[0:2, :band_width]
        result = result + few_rows_dot(window, [coupling_ref[couple_index, part] for part in range(2)])
    return result + bloch_coef * few_rows_dot(row * member, [amp_ref[0, part] for part in range(2)], flipped=True)


def unpacked(kept_ref, other_ref):
    ghosts, row = joined(kept_ref, other_ref[32:40], True, core_index() == 1)
    return jnp.concatenate([ghosts[0:4], ghosts[4:8]], axis=1), jnp.concatenate([row[0:2], row[2:4]], axis=1)


def points_of(ref, part, first, count, run_index=0):
    return jnp.concatenate(
        [ref[part, strip, pl.ds(first * 8 + run_index, count, stride=8)] for strip in range(ref.shape[1])], axis=1
    )


def mend(edge_ref, pots, mix_ref, more=None):
    local, slopes = [], []
    for part in range(2):
        for end in range(2):
            inner, slope = stencils([edge_ref[part, end, 8 + k : 16 + k] for k in range(-reach, reach + 1)], pots[end])
            local.append(inner)
            slopes.append(slope)
    mixed = mixed_with(*two(jnp.concatenate(slopes + ([] if more is None else [more]), axis=0)), mix_ref)
    image = [
        [
            local[2 * part + end] + (mixed[16 + 8 * end : 24 + 8 * end] if part == 0 else -mixed[8 * end : 8 * end + 8])
            for end in range(2)
        ]
        for part in range(2)
    ]
    return image, mixed[32:]


def pick_ends(ends_ref, other_ref):
    strip = lax.axis_index("chan")
    is_low, is_high = strip == 0, strip == lax.axis_size("chan") - 1
    came = other_ref[40:48]
    before = jnp.where(at_first(), 0.0, jnp.where(is_low, came, ends_ref[0]))
    after = jnp.where(at_last(), 0.0, jnp.where(is_high, came, ends_ref[1]))
    return [
        [jnp.concatenate([x[2 * part : 2 * part + 2], x[4 + 2 * part : 6 + 2 * part]], axis=1) for part in range(2)]
        for x in (before, after)
    ]


def between_kernel(
    partners_ref, offsets_ref, block_a, block_b, inner_ref, mine_ref, other_ref, coupling_ref, amp_ref, group_ref,
    edges_ref, mix_ref, ends_ref, kept_ref,
    image_ref, chunk_ref, patch_out, held_ref, written, ends_held, ends_written, patch_ref, patch_written, edge_ref,
):
    member = member_of(group_ref)
    ghosts, row = unpacked(kept_ref, other_ref)
    before, after = pick_ends(ends_ref, other_ref)
    edge_ref[...] = jnp.zeros_like(edge_ref)
    for part in range(2):
        edge_ref[part, 0, 6:8] = before[part]
        edge_ref[part, 1, 16:18] = after[part]
        for end in range(2):
            edge_ref[part, end, 8:16] = edges_ref[end, part]
    near, far_off = ghosts[0:2], ghosts[2:4]
    kinetic = [kinetic_coef * (16.0 * near - far_off), -kinetic_coef * near]
    slope = jnp.concatenate([far_off - 8.0 * near, near, jnp.zeros((12, near.shape[1]), jnp.float32)], axis=0)
    p, mixed = mend(edge_ref, [edges_ref[end, 2] for end in range(2)], mix_ref, slope)
    first_rows, last_rows = [], []
    for part in range(2):
        extra = jnp.concatenate(
            [
                kinetic[k][part : part + 1]
                + (mixed[2 * k + 1 : 2 * k + 2] if part == 0 else -mixed[2 * k : 2 * k + 1])
                for k in range(2)
            ],
            axis=0,
        )
        first_rows.append(p[part][0][0:2] + jnp.where(at_first(), extra, 0.0))
        last_rows.append(p[part][1][6:8])
        patch_ref[part] = jnp.concatenate(
            [first_rows[part], last_rows[part], jnp.zeros((4, near.shape[1]), jnp.float32)], axis=0
        )
    image = inner_result(
        partners_ref, offsets_ref, block_a, block_b, inner_ref, mine_ref, other_ref, coupling_ref, amp_ref, member, row
    )
    image_ref[...] = image
    row = jnp.where(at_first(), jnp.concatenate([rows[0:1] for rows in first_rows], axis=0), 0.0)
    amps = [[amp_ref[radius, part] for part in range(2)] for radius in range(2)]
    copies = write_chunk(chunk_ref, image, ghost_rows(image, amps, member), row, held_ref, written)
    copies += send_ends(chunk_ref, first_rows, last_rows, ends_held, ends_written)
    copies.append(pltpu.make_async_copy(patch_ref, patch_out, patch_written))
    copies[-1].start()
    for copy in copies:
        copy.wait()


def last_kernel(
    partners_ref, offsets_ref, block_a, block_b, inner_ref, mine_ref, other_ref, coupling_ref, amp_ref, group_ref,
    wide_ref, mix_ref, ends_ref, kept_ref, start_ref, second_ref, notes_ref,
    image_ref, out_ref, parts_ref, edge_ref,
):
    member = member_of(group_ref)
    ghosts, row = unpacked(kept_ref, other_ref)
    image = inner_result(
        partners_ref, offsets_ref, block_a, block_b, inner_ref, mine_ref, other_ref, coupling_ref, amp_ref, member, row
    )
    image_ref[...] = image
    strips = wide_ref.shape[1]
    length = second_ref.shape[2] // 8
    noted = [
        [
            jnp.concatenate([notes_ref[9 + strips * (3 * end + k) + strip] for strip in range(strips)], axis=1)
            for k in range(3)
        ]
        for end in range(2)
    ]
    before, after = pick_ends(ends_ref, other_ref)
    edge_ref[...] = jnp.zeros_like(edge_ref)
    for part in range(2):
        ghost = jnp.concatenate([ghosts[2 + part : 3 + part], ghosts[part : part + 1]], axis=0)
        edge_ref[part, 0, 6:8] = jnp.where(at_first(), ghost, before[part])
        edge_ref[part, 0, 8:24] = points_of(wide_ref, part, reach, 16)
        edge_ref[part, 1, 0:16] = points_of(wide_ref, part, length + reach - 16, 16, 7)
        edge_ref[part, 1, 16:18] = after[part]
    q, _ = mend(edge_ref, [noted[end][0] for end in range(2)], mix_ref)
    row_of = lax.broadcasted_iota(jnp.int32, q[0][0].shape, 0)
    mended = [row_of < 4, row_of >= 4]
    totals = [notes_ref[k] for k in range(9)]
    for end in range(2):
        for part in range(2):
            there = points_of(second_ref, part, 0 if end == 0 else length - 8, 8, 7 * end)
            q[part][end] = jnp.where(mended[end], q[part][end], there)
            out_ref[end, part] = q[part][end]
        entries = products(noted[end][1:], [edge_ref[part, end, 8:16] for part in range(2)], [q[part][end] for part in range(2)])
        for k, entry in enumerate(entries):
            entry = jnp.where(mended[end], entry, 0.0)
            totals[k] = totals[k] + sum(entry[:, strip * lanes : (strip + 1) * lanes] for strip in range(strips))
    start, inner = start_ref[...], inner_ref[...]
    inside = products([start[0:1], start[1:2]], [inner[0:1], inner[1:2]], [image[0:1], image[1:2]])
    lane = lax.broadcasted_iota(jnp.int32, (1, lanes), 1)
    sums = jnp.zeros((1, lanes), jnp.float32)
    for k in range(9):
        line = jnp.sum(totals[k], axis=0, keepdims=True) + inside[k][:, :lanes] + inside[k][:, lanes:]
        sums = jnp.where(lane == k, jnp.sum(line, axis=1, keepdims=True), sums)
    parts_ref[...] = jnp.broadcast_to(sums, parts_ref.shape)


def arnoldi_coefs(gram):
    ss, spr, spi, sqr, sqi, pp, pqr, pqi, qq = gram
    cr, ci = spr / ss, spi / ss
    left_1 = pp - (spr * cr + spi * ci)
    h10 = jnp.sqrt(left_1 / ss)
    sxr = sqr - (cr * spr - ci * spi)
    sxi = sqi - (cr * spi + ci * spr)
    h01r, h01i = sxr / (ss * h10), sxi / (ss * h10)
    pxr, pxi = pqr - cr * pp, pqi - ci * pp
    yxr = pxr - (cr * sxr + ci * sxi)
    yxi = pxi - (cr * sxi - ci * sxr)
    scale = 1.0 / left_1
    h11r, h11i = yxr * scale, yxi * scale
    xx = (qq - 2.0 * (cr * pqr + ci * pqi) + (cr * cr + ci * ci) * pp) * scale
    left_2 = xx - (h01r * h01r + h01i * h01i) - (h11r * h11r + h11i * h11i)
    h21 = jnp.sqrt(left_2)
    fine = (left_1 > least_left * pp) & (left_2 > least_left * xx)
    poor = jnp.where(fine, 0.0, 1.0)
    zero = jnp.zeros_like(ss)
    entries = [[[cr + shift, h10, zero], [h01r, h11r + shift, h21]], [[ci, zero, zero], [h01i, h11i, zero]]]
    a = jnp.sqrt(ss)
    coef_q = 1.0 / (a * h10 * h21)
    coef_p = (-(cr + h11r) * coef_q, -(ci + h11i) * coef_q)
    coef_s = (
        (h11r * cr - h11i * ci) * coef_q - h01r / (a * h21),
        (h11r * ci + h11i * cr) * coef_q - h01i / (a * h21),
    )
    return entries, (coef_q, coef_p, coef_s), poor


def combined(coefs, s, p, q):
    coef_q, coef_p, coef_s = coefs
    return (
        coef_q * q[0] + coef_p[0] * p[0] - coef_p[1] * p[1] + coef_s[0] * s[0] - coef_s[1] * s[1],
        coef_q * q[1] + coef_p[0] * p[1] + coef_p[1] * p[0] + coef_s[0] * s[1] + coef_s[1] * s[0],
    )


def finish_kernel(
    entries, parts_ref, start_ref, inner_ref, image_ref, state_ref, wide_ref, second_ref, edge_ref,
    inner_out, result_out, hess_out, poor_out, outer_out, written,
):
    strips, places = second_ref.shape[1:3]
    length = places // 8
    sums = jnp.sum(parts_ref[...], axis=0, keepdims=True) * (1.0 / entries)
    lane = lax.broadcasted_iota(jnp.int32, sums.shape, 1)
    gram = [jnp.sum(jnp.where(lane == k, sums, 0.0), axis=1, keepdims=True) for k in range(9)]
    values, (coef_q, coef_p, coef_s), poor = arnoldi_coefs(gram)
    tile = lambda coef: jnp.broadcast_to(coef, (8, lanes))
    coefs = tile(coef_q), [tile(coef) for coef in coef_p], [tile(coef) for coef in coef_s]

    def put(rows, p_first, q_first, run_index, edge=None):
        for strip in range(strips):
            here = slice(strip * lanes, (strip + 1) * lanes)
            result = combined(
                coefs,
                [state_ref[part, rows, here] for part in range(2)],
                [wide_ref[part, strip, pl.ds(p_first * 8 + run_index, 8, stride=8)] for part in range(2)],
                [
                    second_ref[part, strip, pl.ds(q_first * 8 + run_index, 8, stride=8)]
                    if edge is None
                    else edge_ref[edge, part, :, here]
                    for part in range(2)
                ],
            )
            for part in range(2):
                outer_out[part, rows, here] = result[part]

    copies = []
    for run_index in range(8):
        for first in range(0, length, 8):
            row = run_index * length + first
            edge = 0 if row == 0 else 1 if row == places - 8 else None
            put(slice(row, row + 8), first + reach, first, run_index, edge)
        rows = pl.ds(run_index * length, length)
        copies.append(
            pltpu.make_async_copy(outer_out.at[:, rows], result_out.at[:, rows], written.at[run_index])
        )
        copies[-1].start()
    for first in range(0, inner_out.shape[1], lanes):
        here = slice(first, first + lanes)
        result = combined(
            [coefs[0][0:1], [c[0:1] for c in coefs[1]], [c[0:1] for c in coefs[2]]],
            *[[ref[0:1, here], ref[1:2, here]] for ref in (start_ref, inner_ref, image_ref)],
        )
        for part in range(2):
            inner_out[part : part + 1, here] = result[part]
    lane = lax.broadcasted_iota(jnp.int32, (1, TERMS + 1), 1)
    for part in range(2):
        for column in range(TERMS):
            line = jnp.zeros((1, TERMS + 1), jnp.float32)
            for k, value in enumerate(values[part][column]):
                line = jnp.where(lane == k, value, line)
            hess_out[part, column : column + 1] = line
    poor_out[...] = jnp.broadcast_to(poor, poor_out.shape)
    for copy in copies:
        copy.wait()


def weights_kernel(coupling_ref, amp_ref, after_ref, coupling_out, amp_out):
    for k in range(2):
        coupling_out[k, 0], coupling_out[k, 1] = two(coupling_ref[0, k])
        amp_out[k, 0], amp_out[k, 1] = two(amp_ref[0, k])


def same_kernel(in_ref, out_ref):
    out_ref[...] = in_ref[...]


def across_blocks(mine, kept, after):
    blocks = lax.axis_size("rad")
    last = blocks // 2 - 1
    near = lax.ppermute(mine, "rad", [(i, i ^ 2) for i in range(blocks)])
    mine, kept = join(join_kernel, 32, mine, near, kept, after[0])
    other = lax.ppermute(mine, "rad", [(i, 2 * (last - i // 2) + i % 2) for i in range(blocks)])
    mine, kept = join(last_join_kernel, 48, mine, other, kept, near, after[1])
    return mine, lax.ppermute(mine, "rad", [(i, i ^ 1) for i in range(blocks)]), kept


def body(*inputs):
    (
        inner_state,
        outer_state,
        inner_ham,
        inner_coupling,
        surface_amp,
        potential,
        laser_mix,
        partners,
        band_offsets,
        channel_group,
    ) = inputs
    block_order, rows = inner_ham.shape[1:]
    points, channels = outer_state.shape[1:]
    count = lax.axis_size(both)
    blocks, strips = lax.axis_size("rad"), lax.axis_size("chan")
    entries = float(blocks * block_order + count * points * channels)
    group = channel_group.reshape(1, channels)
    by_coupling = partners.T, band_offsets.T
    f32, bf16 = jnp.float32, jnp.bfloat16
    out_strips = channels // lanes
    folded_rows = points + 2 * reach * 8

    chunk = pl.pallas_call(
        start_kernel,
        grid=(1,),
        out_shape=jax.ShapeDtypeStruct((strips, 24, rows), f32),
        in_specs=[
            whole(),
            in_one((2, 8, channels)),
            pl.BlockSpec((2, 8, channels), lambda i: (0, points // 8 - 1, 0)),
            whole(),
            whole(),
        ],
        out_specs=whole(),
        compiler_params=pltpu.CompilerParams(vmem_limit_bytes=vmem_bytes),
    )(inner_state, outer_state, outer_state, surface_amp, group)
    got = lax.all_to_all(chunk, "chan", 0, 0)
    wide, mix, edges = pl.pallas_call(
        first_outer_kernel,
        out_shape=[
            jax.ShapeDtypeStruct((2, out_strips, folded_rows, lanes), f32),
            jax.ShapeDtypeStruct((2, channels, channels), bf16),
            jax.ShapeDtypeStruct((2, 3, 8, channels), f32),
        ],
        in_specs=[whole()] * 3,
        out_specs=[whole()] * 3,
        scratch_shapes=[
            pltpu.VMEM((2, out_strips, points + 2 * margin, lanes), f32),
            pltpu.VMEM((out_strips, points + 2 * margin, lanes), f32),
            pltpu.VMEM((2, folded_rows, channels), bf16),
            pltpu.VMEM((2, folded_rows, channels), bf16),
        ],
        compiler_params=pltpu.CompilerParams(vmem_limit_bytes=vmem_bytes),
    )(outer_state, potential, laser_mix)

    def block_product(got):
        size = 2 * rows
        parts = []
        for first, last in ((0, 4), (4, 8)):
            parts += run(
                lambda *refs, first=first: block_kernel(first, *refs),
                [(2, rows)],
                (got, pltpu.with_memory_space_constraint(inner_ham, pltpu.HBM)),
                [whole(), far()],
                [pltpu.VMEM((last - first, size, rows), f32), pltpu.SemaphoreType.DMA((last - first,))],
            )
        return parts

    def split_weights(after):
        return run(
            weights_kernel,
            [((2, 2) + inner_coupling.shape[2:], bf16), ((2, 2) + surface_amp.shape[2:], bf16)],
            (inner_coupling, surface_amp, after),
            [whole()] * 2 + [anywhere()],
        )

    gathered = [(24, rows), (16, rows), (2, 8, rows)]
    mine, kept, ends = run(gather_kernel, gathered, (got, wide), [whole(), anywhere()])
    block_parts = block_product(got)
    mine, other, kept = across_blocks(mine, kept, block_parts)
    coupling, amp = split_weights(mine)
    p_inner, chunk, patch = pl.pallas_call(
        between_kernel,
        out_shape=[
            jax.ShapeDtypeStruct((2, rows), f32),
            pltpu.HBM((strips, 24, rows), f32),
            pltpu.HBM((2, 8, channels), f32),
        ],
        in_specs=[scalars()] * 2 + [whole()] * 12,
        out_specs=[whole()] + [far()] * 2,
        scratch_shapes=[
            pltpu.VMEM((4, 16, rows), f32),
            pltpu.SemaphoreType.DMA((strips // 4,)),
            pltpu.VMEM((2, 8, rows), f32),
            pltpu.SemaphoreType.DMA((2,)),
        ]
        + [pltpu.VMEM((2, 8, channels), f32), pltpu.SemaphoreType.DMA, pltpu.VMEM((2, 2, 24, channels), f32)],
        compiler_params=pltpu.CompilerParams(vmem_limit_bytes=vmem_bytes),
    )(
        *by_coupling, *block_parts, inner_state, mine, other, coupling, amp, group,
        edges, mix, ends, kept,
    )
    got = lax.all_to_all(chunk, "chan", 0, 0)
    q_shape, notes_shape = (2, out_strips, points, lanes), (9 + 6 * out_strips, 8, lanes)
    wide, second, notes = pl.pallas_call(
        second_outer_kernel,
        grid=(1,),
        out_shape=[
            jax.ShapeDtypeStruct((2, out_strips, folded_rows, lanes), f32),
            pltpu.HBM(q_shape, f32),
            pltpu.HBM(notes_shape, f32),
        ],
        in_specs=[in_one((2, 8, channels))] + [whole()] * 4,
        out_specs=[whole(), far(), far()],
        scratch_shapes=[pltpu.VMEM((2, points, channels), bf16)] * 2
        + [
            pltpu.VMEM(q_shape, f32),
            pltpu.VMEM((out_strips, points, lanes), f32),
            pltpu.VMEM(q_shape, f32),
            pltpu.VMEM(notes_shape, f32),
            pltpu.SemaphoreType.DMA((2,)),
        ],
        input_output_aliases={1: 0},
        compiler_params=pltpu.CompilerParams(vmem_limit_bytes=vmem_bytes),
    )(pltpu.with_memory_space_constraint(patch, pltpu.HBM), wide, outer_state, potential, mix)
    mine, kept, ends = run(
        gather_kernel, gathered, (got, pltpu.with_memory_space_constraint(notes, pltpu.HBM)), [whole(), far()]
    )
    block_parts = block_product(got)
    mine, other, kept = across_blocks(mine, kept, block_parts)
    coupling, amp = split_weights(mine)
    q_inner, q_ends, parts = run(
        last_kernel,
        [(2, rows), (2, 2, 8, channels), (count, lanes)],
        (
            *by_coupling, *block_parts, p_inner, mine, other, coupling, amp, group,
            wide, mix, ends, kept, inner_state, second, notes,
        ),
        [scalars()] * 2 + [whole()] * 15,
        [pltpu.VMEM((2, 2, 24, channels), f32)],
    )
    parts = lax.all_to_all(parts.reshape(count, 1, lanes), both, 0, 0).reshape(count, lanes)
    last_inner, last_outer, columns, poor = pl.pallas_call(
        lambda *refs: finish_kernel(entries, *refs),
        out_shape=[
            jax.ShapeDtypeStruct((2, rows), f32),
            pltpu.HBM((2, points, channels), f32),
            jax.ShapeDtypeStruct((2, TERMS, TERMS + 1), f32),
            jax.ShapeDtypeStruct((1, lanes), f32),
        ],
        in_specs=[whole()] * 8,
        out_specs=[whole(), far(), whole(), whole()],
        scratch_shapes=[pltpu.VMEM((2, points, channels), f32), pltpu.SemaphoreType.DMA((8,))],
        compiler_params=pltpu.CompilerParams(vmem_limit_bytes=vmem_bytes),
    )(parts, inner_state, p_inner, q_inner, outer_state, wide, second, q_ends)

    def again(state):
        last_inner, last_outer, hessenberg = step_by_step(*inputs)
        columns = hessenberg.transpose(0, 2, 1)
        (columns,) = run(same_kernel, [columns.shape], (columns,), [whole()])
        return jnp.zeros((), f32), last_inner, last_outer, columns

    _, last_inner, last_outer, columns = lax.while_loop(
        lambda state: state[0] > 0.0, again, (poor[0, 0], last_inner, last_outer, columns)
    )
    return last_inner, last_outer, columns.transpose(0, 2, 1)


def solution(mesh):
    return jax.shard_map(
        body,
        mesh=mesh,
        in_specs=(
            P(None, ("rad", "chan")),
            P(None, ("rad", "chan"), None),
            P("rad", None, "chan"),
            P("rad", None, None, "chan"),
            P("rad", None, "chan", None),
            P(("rad", "chan"), None),
            P(),
            P(),
            P(),
            P(),
        ),
        out_specs=(P(None, ("rad", "chan")), P(None, ("rad", "chan"), None), P()),
        check_vma=False,
    )
```
